32 devices in a mesh: dp: 2 (over y), seq: 4 (over x, core), tensor: 4 (over z).
Axes of the slice: x: 2, y: 2, z: 4, core: 2. Of those that a mesh axis runs over, the one named last changes fastest.
Arguments:
- inputs: bfloat16 [6, 2048, 768], P('dp', 'seq'), may hold values from -6 to 6
- lengths: int32 [6], P('dp'), may hold values from 512 to 2048, as said below
- gain_attn: bfloat16 [768], P('dp'), may hold values from 0.5 to 1.5
- w_query: bfloat16 [768, 768], P('dp', 'tensor'), may hold values from -0.109375 to 0.109375
- w_key: bfloat16 [768, 768], P('dp', 'tensor'), may hold values from -0.109375 to 0.109375
- w_value: bfloat16 [768, 768], P('dp', 'tensor'), may hold values from -0.21875 to 0.21875
- w_out: bfloat16 [768, 768], P('tensor', 'dp'), may hold values from -1.75 to 1.75
- bias_table: bfloat16 [32, 12], P('dp', 'tensor'), may hold values from -4 to 4
- gain_ffn: bfloat16 [768], P('dp'), may hold values from 0.5 to 1.5
- w_in: bfloat16 [768, 3072], P('dp', 'tensor'), may hold values from -0.21875 to 0.21875
- w_down: bfloat16 [3072, 768], P('tensor', 'dp'), may hold values from -0.15625 to 0.15625
- cotangent: bfloat16 [6, 2048, 768], P('dp', 'seq'), may hold values from -6 to 6
Outputs:
- outputs: bfloat16 [6, 2048, 768], P('dp', 'seq')
- grad_inputs: bfloat16 [6, 2048, 768], P('dp', 'seq')
- grad_gain_attn: float32 [768], P('dp')
- grad_query: float32 [768, 768], P('dp', 'tensor')
- grad_key: float32 [768, 768], P('dp', 'tensor')
- grad_value: float32 [768, 768], P('dp', 'tensor')
- grad_out: float32 [768, 768], P('tensor', 'dp')
- grad_table: float32 [32, 12], P('dp', 'tensor')
- grad_gain_ffn: float32 [768], P('dp')
- grad_in: float32 [768, 3072], P('dp', 'tensor')
- grad_down: float32 [3072, 768], P('tensor', 'dp')
The draws below stay inside these ranges and needn't reach their ends.
Inputs may be any that keep to these rules, and one draw needn't show every extreme that they name: `lengths`: real tokens of each sequence, counted from its first slot; in every draw some sequence fills all 2048 slots.
All inputs are finite; a program needn't handle non-finite values.
Results may differ from the reference program's by a relative error of at most 0.019.
Values may be sent and summed in bfloat16 or wider, within the bound.
No kernel may reach another device: no remote copies, remote signals or barrier semaphores. Data moves between devices by JAX's collectives and lax.ppermute only.
A program may use at most 256 MiB of HBM per device.

```python
import jax
import jax.numpy as jnp
from jax import lax

D = 768
HEADS = 12
HEAD = 64
FF = 3072
BUCKETS = 32
LEN = 2048
SLOTS = 6


def draw_lengths(key, part):
    first_key, second_key = jax.random.split(key)
    drawn = jax.random.randint(first_key, (SLOTS,), LEN // 4, LEN + 1)
    chosen = jax.random.randint(second_key, (), 0, SLOTS)
    return jnp.where(jnp.arange(SLOTS) == chosen, LEN, drawn).astype(jnp.int32)


def levels(stream_key, shape, shards, smallest, high):
    def one(position, parts):
        steps = jax.random.uniform(jax.random.fold_in(jax.random.fold_in(stream_key, 6), position), (parts,), jnp.float32, smallest / len(shards), high / len(shards))
        return jnp.repeat(jnp.exp(steps), shape[position] // parts).reshape((-1,) + (1,) * (len(shape) - position - 1))

    level = one(*shards[0])
    for cut in shards[1:]:
        level = level * one(*cut)
    return level


def noise(own_key, shape, scale, most, shards=(), kind=jnp.bfloat16):
    values = jax.random.normal(own_key, shape, jnp.float32) * scale
    if len(shards) > 0:
        values = levels(own_key, shape, shards, -0.22, 0.18) * values
    return jnp.clip(values, min=-most, max=most).astype(kind)


def setup_inputs(seed: int = 0) -> dict:
    splits = jax.random.split(jax.random.key(seed), 13)
    inputs = noise(splits[0], (SLOTS, LEN, D), 1.0, 6.0, ((0, 2), (1, 4)))
    lengths = draw_lengths(jax.random.fold_in(splits[12], 71), 0)
    gain_attn = jnp.clip(1.0 + 0.1 * jax.random.normal(splits[2], (D,), jnp.float32), 0.5, 1.5).astype(jnp.bfloat16)
    w_query = noise(splits[3], (D, HEADS * HEAD), (4 * D) ** -0.5, 0.109375, ((0, 2), (1, 4)))
    w_key = noise(splits[4], (D, HEADS * HEAD), (4 * D) ** -0.5, 0.109375, ((0, 2), (1, 4)))
    w_value = noise(splits[5], (D, HEADS * HEAD), D ** -0.5, 0.21875, ((0, 2), (1, 4)))
    w_out = noise(splits[6], (HEADS * HEAD, D), (HEADS * HEAD // 64) ** -0.5, 1.75, ((0, 4), (1, 2)))
    bias_table = noise(splits[7], (BUCKETS, HEADS), 1.0, 4.0, ((0, 2), (1, 4)))
    gain_ffn = jnp.clip(1.0 + 0.1 * jax.random.normal(splits[8], (D,), jnp.float32), 0.5, 1.5).astype(jnp.bfloat16)
    w_in = noise(splits[9], (D, FF), D ** -0.5, 0.21875, ((0, 2), (1, 4)))
    w_down = noise(splits[10], (FF, D), (FF // 2) ** -0.5, 0.15625, ((0, 4), (1, 2)))
    cotangent = noise(splits[11], (SLOTS, LEN, D), 1.0, 6.0, ((0, 2), (1, 4)))
    return dict(inputs=inputs, lengths=lengths, gain_attn=gain_attn, w_query=w_query, w_key=w_key, w_value=w_value, w_out=w_out, bias_table=bias_table, gain_ffn=gain_ffn, w_in=w_in, w_down=w_down, cotangent=cotangent)


EPSILON = 1e-06
LIMITS = (12, 16, 23, 32, 46, 64, 91)
HIGHEST = lax.Precision.HIGHEST

@jax.custom_vjp
def low(v):
    return lax.optimization_barrier(v.astype(jnp.bfloat16)).astype(jnp.float32)

@jax.custom_vjp
def low_back(v):
    return v

def low_keep(v):
    return (low(v), None)

def low_pass(kept, grad):
    return (grad,)

def back_keep(v):
    return (v, None)

def back_low(kept, grad):
    return (low(grad),)
low.defvjp(low_keep, low_pass)
low_back.defvjp(back_keep, back_low)

def bucket_of(relative):
    relative = relative.astype(jnp.int32)
    sign_part = jnp.where(relative > 0, 16, 0).astype(jnp.int32)
    distance = jnp.abs(relative).astype(jnp.int32)
    far_part = jnp.full(distance.shape, 8, jnp.int32)
    for limit in LIMITS:
        far_part = far_part + (distance >= limit).astype(jnp.int32)
    return sign_part + jnp.where(distance < 8, distance, far_part)

def matmul(left, right):
    return jnp.dot(left, right, precision=HIGHEST)

def rms_norm(values, gain):
    return values * lax.rsqrt(lax.optimization_barrier(jnp.mean(values * values, axis=-1, keepdims=True)) + EPSILON) * gain

def layer(resid_in, length, params):
    gain_attn, w_query, w_key, w_value, w_out, bias_table, gain_ffn, w_in, w_down = params
    normed_one = low(rms_norm(resid_in, gain_attn))
    query = low_back(low(matmul(normed_one, w_query))).reshape(LEN, HEADS, HEAD)
    keys = low_back(low(matmul(normed_one, w_key))).reshape(LEN, HEADS, HEAD)
    values = low_back(low(matmul(normed_one, w_value))).reshape(LEN, HEADS, HEAD)
    block = min(512, LEN)
    key_pos = jnp.arange(LEN).astype(jnp.int32)
    key_live = key_pos < length

    def attend(start):
        query_pos = (start + jnp.arange(block)).astype(jnp.int32)
        rows_now = lax.dynamic_slice_in_dim(query, start, block, 0)
        buckets = bucket_of(key_pos[None, :] - query_pos[:, None])
        bias = jnp.transpose(jnp.take(bias_table, buckets, axis=0), (2, 0, 1))
        scores = jnp.einsum('qhe,khe->hqk', rows_now, keys, precision=HIGHEST) + bias
        scores = low_back(scores)
        scores = jnp.where(key_live[None, None, :], scores, -1e+30)
        top_score = lax.optimization_barrier(jnp.max(scores, axis=-1, keepdims=True))
        lse = top_score + jnp.log(lax.optimization_barrier(jnp.sum(jnp.exp(scores - top_score), axis=-1, keepdims=True)))
        probs = jnp.exp(scores - lse)
        return jnp.einsum('hqk,khe->qhe', low(probs), values, precision=HIGHEST)
    starts = (jnp.arange(LEN // block) * block).astype(jnp.int32)
    mixed = lax.map(jax.checkpoint(attend), starts).reshape(LEN, HEADS * HEAD)
    mixed = low_back(low(mixed))
    resid_mid = resid_in + low_back(matmul(mixed, w_out))
    normed_two = low(rms_norm(resid_mid, gain_ffn))
    hidden = low_back(matmul(normed_two, w_in))
    active = low(jax.nn.gelu(hidden, approximate=True))
    return resid_mid + low_back(matmul(active, w_down))

def reference(inputs, lengths, gain_attn, w_query, w_key, w_value, w_out, bias_table, gain_ffn, w_in, w_down, cotangent):
    params = tuple((p.astype(jnp.float32) for p in (gain_attn, w_query, w_key, w_value, w_out, bias_table, gain_ffn, w_in, w_down)))
    zeros = jax.tree.map(jnp.zeros_like, params)

    def one_slot(totals, item):
        resid_in, length, grad_seen = item
        resid_in = resid_in.astype(jnp.float32)
        live_rows = (jnp.arange(LEN).astype(jnp.int32) < length).astype(jnp.float32)
        result, pull = jax.vjp(lambda xs, ps: layer(xs, length, ps), resid_in, params)
        grad_x, grad_params = pull(grad_seen.astype(jnp.float32) * live_rows[:, None])
        totals = jax.tree.map(jnp.add, totals, grad_params)
        return (totals, (result.astype(jnp.bfloat16), grad_x.astype(jnp.bfloat16)))
    totals, (outputs, grad_inputs) = lax.scan(one_slot, zeros, (inputs, lengths, cotangent))
    return (outputs, grad_inputs, totals[0], totals[1], totals[2], totals[3], totals[4], totals[5], totals[6], totals[7], totals[8])
```

```python
import functools

import jax
import jax.numpy as jnp
from jax import lax
from jax.experimental import pallas as pl
from jax.experimental.pallas import tpu as pltpu
from jax.sharding import PartitionSpec as P

HEAD = 64
BUCKETS = 32
EPSILON = 1e-06
LIMITS = (12, 16, 23, 32, 46, 64, 91)
LOW = jnp.bfloat16
FULL = jnp.float32
TILE = 128
RANKS = 4
MIX = (0, 2, 1, 3)
IDLE = 1
SPLIT = 1
GELU_A = 0.7978845608028654
GELU_B = 0.044715
KERNEL_MEMORY = 60 * 1024 * 1024


def bucket_of(relative):
    sign_part = jnp.where(relative > 0, 16, 0).astype(jnp.int32)
    distance = jnp.abs(relative)
    far_part = jnp.full(distance.shape, 8, jnp.int32)
    for limit in LIMITS:
        far_part = far_part + (distance >= limit).astype(jnp.int32)
    return sign_part + jnp.where(distance < 8, distance, far_part)


def dot_nn(left, right):
    return lax.dot_general(left, right, (((1,), (0,)), ((), ())), preferred_element_type=FULL)


def dot_nt(left, right):
    return lax.dot_general(left, right, (((1,), (1,)), ((), ())), preferred_element_type=FULL)


def dot_tn(left, right):
    return lax.dot_general(left, right, (((0,), (0,)), ((), ())), preferred_element_type=FULL)


def tile_place(tile, per):
    sub = per // SPLIT
    return ((tile % per) // sub) * (RANKS * sub) + (tile // per) * sub + tile % sub


def tile_at(place, per):
    sub = per // SPLIT
    return ((place // sub) % RANKS) * per + (place // (RANKS * sub)) * sub + place % sub


def params(name_cost=None):
    return pltpu.CompilerParams(vmem_limit_bytes=KERNEL_MEMORY)


def whole_spec(shape):
    return pl.BlockSpec(shape, lambda i, c: tuple(0 for _ in shape))


def project_kernel(heads, per, info, x_ref, gain_ref, w_ref, far_ref, normed, qa, ka, va, kt, vt):
    step = pl.program_id(0)
    rows = x_ref.shape[2]
    x = x_ref[0, 0].astype(FULL)
    scale = lax.rsqrt(jnp.mean(x * x, axis=-1, keepdims=True) + EPSILON)
    xn = (x * scale * gain_ref[...]).astype(LOW)
    normed[...] = xn
    y = dot_nn(xn, w_ref[...])
    row = lax.broadcasted_iota(jnp.int32, (rows, HEAD), 0)
    lane = lax.broadcasted_iota(jnp.int32, (rows, HEAD), 1)
    place = step * (rows // TILE) + row // TILE
    here = tile_at(place, per)
    there = tile_at(lane, per)
    count = RANKS * per
    position = here * TILE + row % TILE
    q_extra = jnp.where(jnp.logical_or(lane == place, lane == count), 1.0, 0.0)
    v_extra = jnp.where(lane == 0, 1.0, 0.0)
    dead = jnp.where(jnp.logical_and(lane == count, position >= info[RANKS]), -1e30, 0.0)
    is_tile = lane < count
    left = jnp.logical_and(is_tile, here < there - 1)
    right = jnp.logical_and(is_tile, here > there + 1)
    width = heads * HEAD
    for h in range(heads):
        k_extra = jnp.where(left, far_ref[0, h], jnp.where(right, far_ref[1, h], dead))
        at = slice(TILE * h, TILE * h + TILE)
        qh = jnp.concatenate([y[:, HEAD * h : HEAD * h + HEAD], q_extra], axis=1)
        kh = jnp.concatenate([y[:, width + HEAD * h : width + HEAD * h + HEAD], k_extra], axis=1)
        vh = jnp.concatenate(
            [y[:, 2 * width + HEAD * h : 2 * width + HEAD * h + HEAD], v_extra], axis=1
        )
        qa[:, at] = qh.astype(LOW)
        ka[:, at] = kh.astype(LOW)
        va[:, at] = vh.astype(LOW)
        kt[at, :] = kh.T.astype(LOW)
        vt[at, :] = vh.T.astype(LOW)


def project(info, x_rel, gain, w_qkv, far, heads, per):
    rows = x_rel.shape[2]
    total = RANKS * SPLIT * rows
    width = x_rel.shape[3]
    row_block = lambda w: pl.BlockSpec((rows, w), lambda i, c: (i, 0))
    col_block = lambda w: pl.BlockSpec((w, rows), lambda i, c: (0, i))
    wide = heads * TILE
    return pl.pallas_call(
        functools.partial(project_kernel, heads, per),
        grid_spec=pltpu.PrefetchScalarGridSpec(
            num_scalar_prefetch=1,
            grid=(RANKS * SPLIT,),
            in_specs=[
                pl.BlockSpec(
                    (1, 1, rows, width), lambda i, c: (c[i % RANKS], i // RANKS, 0, 0)
                ),
                whole_spec(gain.shape),
                whole_spec(w_qkv.shape),
                pl.BlockSpec(memory_space=pltpu.SMEM),
            ],
            out_specs=[
                row_block(width),
                row_block(wide),
                row_block(wide),
                row_block(wide),
                col_block(wide),
                col_block(wide),
            ],
        ),
        out_shape=[
            jax.ShapeDtypeStruct((total, width), LOW),
            jax.ShapeDtypeStruct((total, wide), LOW),
            jax.ShapeDtypeStruct((total, wide), LOW),
            jax.ShapeDtypeStruct((total, wide), LOW),
            jax.ShapeDtypeStruct((wide, total), LOW),
            jax.ShapeDtypeStruct((wide, total), LOW),
        ],
        compiler_params=params(),
        name="project",
    )(info, x_rel, gain, w_qkv, far)


def near_tiles(first_place, tiles, per, visit):
    count = RANKS * per
    for u in range(tiles):
        here = tile_at(first_place + u, per)
        for d in (-1, 0, 1):
            there = here + d
            valid = jnp.logical_and(there >= 0, there < count)
            place = tile_place(jnp.clip(there, 0, count - 1), per)
            rows = pl.ds(pl.multiple_of(place * TILE, TILE), TILE)
            visit(d + 1, rows, slice(u * TILE, u * TILE + TILE), jnp.where(valid, 1.0, 0.0))


def score_block(h, first_place, per, qa, ka, near, s_ref):
    bq = qa.shape[0]
    at = slice(TILE * h, TILE * h + TILE)
    s_ref[h] = dot_nt(ka[:, at], qa[:, at])

    def add(d, rows, cols, valid):
        s_ref[h, rows, cols] = s_ref[h, rows, cols] + near[h, d] * valid

    near_tiles(first_place, bq // TILE, per, add)


def forward_kernel(heads, per, offset, qa, ka, vt, near, mixed, ot, lse, s_ref):
    bq = qa.shape[0]
    first = (pl.program_id(0) + offset) * (bq // TILE)
    for h in range(heads):
        score_block(h, first, per, qa, ka, near, s_ref)
    parts = []
    for h in range(heads):
        s = s_ref[h]
        top = jnp.max(s, axis=0, keepdims=True)
        p = jnp.exp(s - top).astype(LOW)
        o = dot_nn(vt[TILE * h : TILE * h + TILE, :], p)
        total = o[HEAD : HEAD + 1]
        o = o[:HEAD] * (1.0 / total)
        ot[HEAD * h : HEAD * h + HEAD, :] = o
        lse[h : h + 1, :] = top + jnp.log(total)
        parts.append(o.T)
    mixed[...] = jnp.concatenate(parts, axis=1).astype(LOW)


def attend(qa, ka, vt, near, part, bq, per):
    total, wide = ka.shape
    heads = wide // TILE
    span = total // SPLIT
    steps = span // bq
    offset = part * steps
    full = lambda shape: pl.BlockSpec(shape, lambda i: tuple(0 for _ in shape))
    width = heads * HEAD
    return pl.pallas_call(
        functools.partial(forward_kernel, heads, per, offset),
        grid=(steps,),
        in_specs=[
            pl.BlockSpec((bq, wide), lambda i: (i + offset, 0)),
            full(ka.shape),
            full(vt.shape),
            full(near.shape),
        ],
        out_specs=[
            pl.BlockSpec((bq, width), lambda i: (i, 0)),
            pl.BlockSpec((width, bq), lambda i: (0, i)),
            pl.BlockSpec((8, bq), lambda i: (0, i)),
        ],
        out_shape=[
            jax.ShapeDtypeStruct((span, width), LOW),
            jax.ShapeDtypeStruct((width, span), FULL),
            jax.ShapeDtypeStruct((8, span), FULL),
        ],
        scratch_shapes=[pltpu.VMEM((heads, total, bq), FULL)],
        compiler_params=params(),
        name="attend",
    )(qa, ka, vt, near)


def middle_kernel(
    info, x_ref, m0, m1, m2, m3, w_out, gain, w_in, w_down, c_ref,
    ffn, dn, own_resid, g_in, g_down,
):
    step = pl.program_id(0)

    @pl.when(step == 0)
    def _():
        g_in[...] = jnp.zeros_like(g_in)
        g_down[...] = jnp.zeros_like(g_down)

    mixed = jnp.concatenate([m0[...], m1[...], m2[...], m3[...]], axis=1)
    resid = x_ref[0, 0].astype(FULL) + dot_nn(mixed, w_out[...])

    @pl.when(info[step] == 0)
    def _():
        own_resid[...] = resid

    scale = lax.rsqrt(jnp.mean(resid * resid, axis=-1, keepdims=True) + EPSILON)
    normed = (resid * scale * gain[...]).astype(LOW)
    hidden = dot_nn(normed, w_in[...])
    grad = c_ref[0, 0]
    d_active = dot_nt(grad, w_down[...])
    square = hidden * hidden
    th = jnp.tanh(GELU_A * hidden * (1.0 + GELU_B * square))
    half = 0.5 * (1.0 + th)
    active = (hidden * half).astype(LOW)
    slope = half + 0.5 * hidden * (1.0 - th * th) * (GELU_A * (1.0 + (3.0 * GELU_B) * square))
    d_hidden = (d_active * slope).astype(LOW)
    dn[0] = dot_nt(d_hidden, w_in[...]).astype(LOW)
    ffn[0] = dot_nn(active, w_down[...]).astype(LOW)
    g_in[...] += dot_tn(normed, d_hidden)
    g_down[...] += dot_tn(active, grad)


def middle(info, x_rel, pieces, w_out, gain, w_in, w_down, c_rel, part):
    rows, width = x_rel.shape[2:]
    narrow = pieces[0].shape[1]
    hidden = w_in.shape[1]
    rel_block = pl.BlockSpec((1, 1, rows, width), lambda i, c: (c[i], part, 0, 0))
    piece_block = pl.BlockSpec((rows, narrow), lambda i, c: (i, 0))
    out_block = pl.BlockSpec((1, rows, width), lambda i, c: (c[i], 0, 0))
    return pl.pallas_call(
        middle_kernel,
        grid_spec=pltpu.PrefetchScalarGridSpec(
            num_scalar_prefetch=1,
            grid=(RANKS,),
            in_specs=[rel_block]
            + [piece_block] * 4
            + [
                whole_spec(w_out.shape),
                whole_spec(gain.shape),
                whole_spec(w_in.shape),
                whole_spec(w_down.shape),
                rel_block,
            ],
            out_specs=[
                out_block,
                out_block,
                whole_spec((rows, width)),
                whole_spec((width, hidden)),
                whole_spec((hidden, width)),
            ],
        ),
        out_shape=[
            jax.ShapeDtypeStruct((RANKS, rows, width), LOW),
            jax.ShapeDtypeStruct((RANKS, rows, width), LOW),
            jax.ShapeDtypeStruct((rows, width), FULL),
            jax.ShapeDtypeStruct((width, hidden), FULL),
            jax.ShapeDtypeStruct((hidden, width), FULL),
        ],
        compiler_params=params(),
        name="middle",
    )(info, x_rel, *pieces, w_out, gain, w_in, w_down, c_rel)


def backward_kernel(
    heads, per, offset, kc, info, qa, ka, kt, va, d_ref, wo, ot, lse, near,
    dq, dk, dv, d_near, far, g_out, s_ref, ds_ref, dk_acc, dv_acc,
):
    step = pl.program_id(0)
    bq = qa.shape[0]
    total = ka.shape[0]
    count = RANKS * per
    first = (step + offset) * (bq // TILE)

    @pl.when(step == 0)
    def _():
        dk_acc[...] = jnp.zeros_like(dk_acc)
        dv_acc[...] = jnp.zeros_like(dv_acc)
        d_near[...] = jnp.zeros_like(d_near)
        g_out[...] = jnp.zeros_like(g_out)

    d_rows = d_ref[0]
    do = dot_nt(d_rows, wo[...]).astype(LOW)
    do_t = dot_nt(wo[...], d_rows).astype(LOW).astype(FULL)
    g_out[...] += dot_nn(ot[...].astype(LOW), d_rows)
    for h in range(heads):
        score_block(h, first, per, qa, ka, near, s_ref)
    parts = []
    for h in range(heads):
        at = slice(TILE * h, TILE * h + TILE)
        delta = jnp.sum(
            do_t[TILE * h : TILE * h + HEAD] * ot[HEAD * h : HEAD * h + HEAD, :],
            axis=0,
            keepdims=True,
        )
        do_h = do[:, at]
        lse_h = lse[h : h + 1, :]
        dq_t = jnp.zeros((TILE, bq), FULL)
        for c in range(total // kc):
            rows = slice(kc * c, kc * c + kc)
            p = jnp.exp(s_ref[h, rows, :] - lse_h)
            d_p = dot_nt(va[rows, at], do_h)
            d_s = (p * (d_p - delta)).astype(LOW)
            ds_ref[h, rows, :] = d_s
            dv_acc[h, rows, :] += dot_nn(p.astype(LOW), do_h)
            dk_acc[h, rows, :] += dot_nn(d_s, qa[:, at])
            dq_t += dot_nn(kt[at, rows], d_s)
        parts.append(dq_t[:HEAD].T)

        def collect(d, rows, cols, valid):
            d_near[h, d] += ds_ref[h, rows, cols].astype(FULL) * valid

        near_tiles(first, bq // TILE, per, collect)
    dq[...] = jnp.concatenate(parts, axis=1).astype(LOW)

    @pl.when(step == pl.num_programs(0) - 1)
    def _():
        dk[...] = jnp.concatenate([dk_acc[h][:, :HEAD] for h in range(heads)], axis=1).astype(LOW)
        dv[...] = jnp.concatenate([dv_acc[h][:, :HEAD] for h in range(heads)], axis=1).astype(LOW)
        row = lax.broadcasted_iota(jnp.int32, (total, TILE), 0)
        lane = lax.broadcasted_iota(jnp.int32, (total, TILE), 1)
        key_tile = tile_at(row // TILE, per)
        place = lane - HEAD
        is_tile = jnp.logical_and(place >= 0, place < count)
        query_tile = tile_at(jnp.where(is_tile, place, 0), per)
        left = jnp.logical_and(is_tile, key_tile < query_tile - 1)
        right = jnp.logical_and(is_tile, key_tile > query_tile + 1)
        sums = []
        for h in range(heads):
            x = dk_acc[h]
            sums.append(jnp.sum(jnp.where(left, x, 0.0), axis=0, keepdims=True))
            sums.append(jnp.sum(jnp.where(right, x, 0.0), axis=0, keepdims=True))
        sums.append(jnp.zeros((8 - 2 * heads, TILE), FULL))
        far[...] = jnp.concatenate(sums, axis=0)


def attend_back(info, qa, ka, kt, va, d_rel, wo, ot, lse, near, part, kc, per):
    total, wide = ka.shape
    heads = wide // TILE
    rows, model = d_rel.shape[1:]
    bq = rows
    span = total // SPLIT
    steps = span // bq
    offset = part * steps
    width = heads * HEAD
    row_block = lambda w: pl.BlockSpec((bq, w), lambda i, c: (i, 0))
    col_block = lambda w: pl.BlockSpec((w, bq), lambda i, c: (0, i))
    return pl.pallas_call(
        functools.partial(backward_kernel, heads, per, offset, kc),
        grid_spec=pltpu.PrefetchScalarGridSpec(
            num_scalar_prefetch=1,
            grid=(steps,),
            in_specs=[
                pl.BlockSpec((bq, wide), lambda i, c: (i + offset, 0)),
                whole_spec(ka.shape),
                whole_spec(kt.shape),
                whole_spec(va.shape),
                pl.BlockSpec((1, rows, model), lambda i, c: (c[i], 0, 0)),
                whole_spec(wo.shape),
                col_block(width),
                col_block(8),
                whole_spec(near.shape),
            ],
            out_specs=[
                row_block(width),
                whole_spec((total, width)),
                whole_spec((total, width)),
                whole_spec((heads, 3, TILE, TILE)),
                whole_spec((8, TILE)),
                whole_spec((width, model)),
            ],
            scratch_shapes=[
                pltpu.VMEM((heads, total, bq), FULL),
                pltpu.VMEM((heads, total, bq), LOW),
                pltpu.VMEM((heads, total, TILE), FULL),
                pltpu.VMEM((heads, total, TILE), FULL),
            ],
        ),
        out_shape=[
            jax.ShapeDtypeStruct((span, width), LOW),
            jax.ShapeDtypeStruct((total, width), LOW),
            jax.ShapeDtypeStruct((total, width), LOW),
            jax.ShapeDtypeStruct((heads, 3, TILE, TILE), FULL),
            jax.ShapeDtypeStruct((8, TILE), FULL),
            jax.ShapeDtypeStruct((width, model), FULL),
        ],
        compiler_params=params(),
        name="attend_back",
    )(info, qa, ka, kt, va, d_rel, wo, ot, lse, near)


def swap_seq(value, bit):
    return lax.ppermute(value, "seq", [(i, i ^ bit) for i in range(RANKS)])


def gather_seq(value):
    near_one = swap_seq(value, 1)
    far_one = swap_seq(value, 2)
    return (value, near_one, far_one, swap_seq(far_one, 1))


def scatter_seq(parts):
    moved = swap_seq(parts[1::2], 1)
    mine = parts[0].astype(FULL) + moved[0].astype(FULL)
    other = (parts[2].astype(FULL) + moved[1].astype(FULL)).astype(LOW)
    return mine + swap_seq(other, 2).astype(FULL)


def regroup(value, skip):
    pairs = []
    for s in range(RANKS):
        for t in range(RANKS):
            if t != skip:
                pairs.append((s * RANKS + t, s * RANKS + (t ^ MIX[s])))
    return lax.ppermute(value, ("seq", "tensor"), pairs)


def along_tensor(value, pairs):
    return lax.ppermute(value, "tensor", pairs)


def spread(own, rank):
    r1 = along_tensor(own, [(0, 1), (2, 3)])
    l1 = along_tensor(own, [(3, 2), (2, 1)])
    r2 = along_tensor(r1, [(1, 2)])
    l2 = along_tensor(l1, [(2, 1), (1, 0)])
    r3 = along_tensor(r2, [(2, 3)])
    l3 = along_tensor(l2, [(1, 0)])

    def pick(options):
        out = options[0]
        for index in range(1, RANKS):
            out = jnp.where(rank == index, options[index], out)
        return out

    return jnp.stack(
        [pick((own, r1, r2, r3)), pick((l2, l1, own, r1)), pick((l3, l2, l1, own))]
    )


def reduce_weight(partial, axis):
    count = lax.axis_size("dp")
    if count == 2:
        size = partial.shape[axis] // 2
        mine = lax.axis_index("dp")
        keep = lax.dynamic_slice_in_dim(partial, mine * size, size, axis)
        give = lax.dynamic_slice_in_dim(partial, (1 - mine) * size, size, axis)
        keep = keep + lax.ppermute(give.astype(LOW), "dp", [(0, 1), (1, 0)]).astype(FULL)
    else:
        keep = lax.psum_scatter(partial, "dp", scatter_dimension=axis, tiled=True)
    moved = regroup(keep.astype(LOW), IDLE)
    half = moved.shape[0] // 2
    core = lax.axis_index("seq") % 2
    keep = lax.dynamic_slice_in_dim(moved, core * half, half, 0).astype(FULL)
    give = lax.dynamic_slice_in_dim(moved, (1 - core) * half, half, 0)
    keep = (keep + swap_seq(give, 1).astype(FULL)).astype(LOW)
    keep = keep.astype(FULL) + swap_seq(keep, 2).astype(FULL)
    other = swap_seq(keep, 1)
    first = jnp.where(core == 0, keep, other)
    second = jnp.where(core == 0, other, keep)
    return jnp.concatenate([first, second], axis=0)


def gather_dp(value, axis):
    return lax.all_gather(value, "dp", axis=axis, tiled=True)


def body(
    inputs, lengths, gain_attn, w_query, w_key, w_value, w_out, bias_table,
    gain_ffn, w_in, w_down, cotangent,
):
    slots, rows_here, model = inputs.shape
    assert lax.axis_size("seq") == RANKS and lax.axis_size("tensor") == RANKS and slots == 3
    total = RANKS * rows_here
    per = rows_here // TILE
    narrow = w_query.shape[1]
    heads = narrow // HEAD
    rank = lax.axis_index("tensor")
    chunk = lax.axis_index("seq")
    slot = jnp.where(rank == 0, 0, rank - 1)
    length = lax.dynamic_index_in_dim(lengths, slot, 0, keepdims=False)
    order = jnp.bitwise_xor(chunk, jnp.arange(RANKS, dtype=jnp.int32)).astype(jnp.int32)
    info = jnp.concatenate([order, length[None], jnp.zeros((3,), jnp.int32)])
    rows_part = rows_here // SPLIT

    x_own = lax.dynamic_index_in_dim(inputs, slot, 0, keepdims=False)
    c_own = lax.dynamic_index_in_dim(cotangent, slot, 0, keepdims=False)
    position = chunk * rows_here + jnp.arange(rows_here, dtype=jnp.int32)
    live = jnp.logical_and(position < length, rank != IDLE)
    c_own = jnp.where(live[:, None], c_own, jnp.zeros((), LOW))

    w_qkv = gather_dp(regroup(jnp.concatenate([w_query, w_key, w_value], axis=1), None), 0)
    table = gather_dp(regroup(bias_table, None), 0).astype(FULL)
    gain_one = gather_dp(gain_attn, 0).astype(FULL)[None, :]
    gain_two = gather_dp(gain_ffn, 0).astype(FULL)[None, :]
    shape4 = (RANKS, SPLIT, rows_part, model)
    x_rel = jnp.stack(gather_seq(x_own)).reshape(shape4)
    out_mine = gather_dp(regroup(w_out, None), 1)
    in_mine = gather_dp(regroup(w_in, None), 0)
    down_mine = gather_dp(regroup(w_down, None), 1)
    out_rel = jnp.concatenate(gather_seq(out_mine), axis=0)
    c_rel = jnp.stack(gather_seq(c_own)).reshape(shape4)
    out_wide = jnp.pad(
        out_mine.reshape(heads, HEAD, model), ((0, 0), (0, TILE - HEAD), (0, 0))
    ).reshape(heads * TILE, model)

    offset = jnp.arange(TILE, dtype=jnp.int32)
    near_bucket = jnp.stack(
        [bucket_of(TILE * d + offset[:, None] - offset[None, :]) for d in (-1, 0, 1)]
    )
    near = jnp.zeros((heads, 3, TILE, TILE), FULL)
    for b in range(BUCKETS):
        near = near + jnp.where(near_bucket == b, 1.0, 0.0)[None] * table[b][:, None, None, None]
    far_bias = jnp.stack([table[BUCKETS // 2 - 1], table[BUCKETS - 1]])

    normed, qa, ka, va, kt, vt = project(info, x_rel, gain_one, w_qkv, far_bias, heads, per)

    bq = min(512, total // SPLIT)
    attended = [attend(qa, ka, vt, near, part, bq, per) for part in range(SPLIT)]
    mids = [
        middle(
            info, x_rel, gather_seq(attended[part][0]), out_rel, gain_two, in_mine, down_mine,
            c_rel, part,
        )
        for part in range(SPLIT)
    ]
    d_sums = [scatter_seq(mid[1]) for mid in mids]
    ffn_sums = [scatter_seq(mid[0]) for mid in mids]
    g_in = sum(mid[3] for mid in mids)
    g_down = sum(mid[4] for mid in mids)
    c_parts = c_own.reshape(SPLIT, rows_part, model).astype(FULL)
    x_parts = x_own.reshape(SPLIT, rows_part, model).astype(FULL)
    out_parts, d_resids, gain_ffn_part = [], [], 0.0
    for part in range(SPLIT):
        resid = mids[part][2]
        out_parts.append((resid + ffn_sums[part]).astype(LOW))
        scale = lax.rsqrt(jnp.mean(resid * resid, axis=-1, keepdims=True) + EPSILON)
        unit = resid * scale
        along = d_sums[part] * gain_two
        d_resids.append(
            c_parts[part]
            + scale * (along - unit * jnp.mean(along * unit, axis=-1, keepdims=True))
        )
        gain_ffn_part = gain_ffn_part + jnp.sum(d_sums[part] * unit, axis=0)
    d_rels = [jnp.stack(gather_seq(d.astype(LOW))) for d in d_resids]
    outputs = spread(jnp.concatenate(out_parts, axis=0), rank)

    dq, dk, dv, d_near, far, g_out = attend_back(
        info, qa, ka, kt, va, d_rels[0], out_wide, attended[0][1], attended[0][2], near, 0,
        512, per,
    )
    d_qkv = jnp.concatenate([dq, dk, dv], axis=1)
    dn_part = dot_nt(d_qkv, w_qkv).astype(LOW).reshape(SPLIT, RANKS, rows_part, model)
    g_qkv = dot_tn(normed, d_qkv)
    dn_rel = jnp.stack(
        [lax.dynamic_index_in_dim(dn_part, order[r], 1, keepdims=False) for r in range(RANKS)]
    )
    dn_sum = scatter_seq(dn_rel)
    unit = x_parts * lax.rsqrt(jnp.mean(x_parts * x_parts, axis=-1, keepdims=True) + EPSILON)
    scale = lax.rsqrt(jnp.mean(x_parts * x_parts, axis=-1, keepdims=True) + EPSILON)
    along = dn_sum * gain_one
    d_in = jnp.stack(d_resids) + scale * (
        along - unit * jnp.mean(along * unit, axis=-1, keepdims=True)
    )
    gain_attn_part = jnp.sum(dn_sum * unit, axis=(0, 1))
    grad_inputs = spread(d_in.astype(LOW).reshape(rows_here, model), rank)

    d_table = jnp.stack(
        [
            jnp.sum(jnp.where(near_bucket == b, d_near, 0.0), axis=(1, 2, 3))
            for b in range(BUCKETS)
        ]
    )
    far_sum = jnp.sum(far, axis=1)[: 2 * heads].reshape(heads, 2)
    d_table = d_table.at[BUCKETS // 2 - 1].add(far_sum[:, 0]).at[BUCKETS - 1].add(far_sum[:, 1])
    mix = jnp.asarray(MIX, jnp.int32)
    group = jnp.bitwise_xor(rank, lax.dynamic_index_in_dim(mix, chunk, 0, keepdims=False))
    placed = jnp.where(jnp.arange(RANKS)[None, :, None] == group, d_table[:, None, :], 0.0)
    small = jnp.concatenate([gain_attn_part, gain_ffn_part, placed.reshape(-1)])
    small = lax.psum(small, ("dp", "seq", "tensor"))
    mine = lax.axis_index("dp")
    size = gain_attn.shape[0]
    grad_gain_attn = lax.dynamic_slice_in_dim(small, mine * size, size, 0)
    grad_gain_ffn = lax.dynamic_slice_in_dim(small, model + mine * size, size, 0)
    table_all = small[2 * model :].reshape(BUCKETS, RANKS, heads)
    grad_table = lax.dynamic_index_in_dim(table_all, rank, 1, keepdims=False)
    grad_table = lax.dynamic_slice_in_dim(
        grad_table, mine * bias_table.shape[0], bias_table.shape[0], 0
    )

    grad_in = reduce_weight(g_in, 0)
    grad_down = reduce_weight(g_down, 1)
    grad_out = reduce_weight(g_out, 1)
    grad_qkv = reduce_weight(g_qkv, 0)
    return (
        outputs,
        grad_inputs,
        grad_gain_attn,
        grad_qkv[:, :narrow],
        grad_qkv[:, narrow : 2 * narrow],
        grad_qkv[:, 2 * narrow :],
        grad_out,
        grad_table,
        grad_gain_ffn,
        grad_in,
        grad_down,
    )


def solution(mesh):
    in_specs = (
        P("dp", "seq", None),
        P("dp"),
        P("dp"),
        P("dp", "tensor"),
        P("dp", "tensor"),
        P("dp", "tensor"),
        P("tensor", "dp"),
        P("dp", "tensor"),
        P("dp"),
        P("dp", "tensor"),
        P("tensor", "dp"),
        P("dp", "seq", None),
    )
    out_specs = (
        P("dp", "seq", None),
        P("dp", "seq", None),
        P("dp"),
        P("dp", "tensor"),
        P("dp", "tensor"),
        P("dp", "tensor"),
        P("tensor", "dp"),
        P("dp", "tensor"),
        P("dp"),
        P("dp", "tensor"),
        P("tensor", "dp"),
    )
    return jax.shard_map(body, mesh=mesh, in_specs=in_specs, out_specs=out_specs, check_vma=False)
```

```python
import functools

import jax
import jax.numpy as jnp
from jax import lax
from jax.experimental import pallas as pl
from jax.experimental.pallas import tpu as pltpu
from jax.sharding import PartitionSpec as P

HEAD = 64
BUCKETS = 32
EPSILON = 1e-06
LIMITS = (12, 16, 23, 32, 46, 64, 91)
LOW = jnp.bfloat16
FULL = jnp.float32
TILE = 128
RANKS = 4
MIX = (0, 2, 1, 3)
IDLE = 1
SPLIT = 2
EXTRA = 32
GELU_A = 0.7978845608028654
GELU_B = 0.044715
KERNEL_MEMORY = 60 * 1024 * 1024


def bucket_of(relative):
    sign_part = jnp.where(relative > 0, 16, 0).astype(jnp.int32)
    distance = jnp.abs(relative)
    far_part = jnp.full(distance.shape, 8, jnp.int32)
    for limit in LIMITS:
        far_part = far_part + (distance >= limit).astype(jnp.int32)
    return sign_part + jnp.where(distance < 8, distance, far_part)


def dot_nn(left, right):
    return lax.dot_general(left, right, (((1,), (0,)), ((), ())), preferred_element_type=FULL)


def dot_nt(left, right):
    return lax.dot_general(left, right, (((1,), (1,)), ((), ())), preferred_element_type=FULL)


def dot_tn(left, right):
    return lax.dot_general(left, right, (((0,), (0,)), ((), ())), preferred_element_type=FULL)


def tile_place(tile, per):
    sub = per // SPLIT
    return ((tile % per) // sub) * (RANKS * sub) + (tile // per) * sub + tile % sub


def tile_at(place, per):
    sub = per // SPLIT
    return ((place // sub) % RANKS) * per + (place // (RANKS * sub)) * sub + place % sub


def cost(flops):
    return pl.CostEstimate(flops=flops, bytes_accessed=flops // 512, transcendentals=0)


def params():
    return pltpu.CompilerParams(vmem_limit_bytes=KERNEL_MEMORY)


def whole_spec(shape):
    return pl.BlockSpec(shape, lambda i, c: tuple(0 for _ in shape))


def near_bucket(d):
    key = lax.broadcasted_iota(jnp.int32, (TILE, TILE), 0)
    query = lax.broadcasted_iota(jnp.int32, (TILE, TILE), 1)
    return bucket_of(TILE * d + key - query)


def buckets_near(d):
    half = BUCKETS // 2
    if d < 0:
        return range(half)
    return range(half, BUCKETS) if d > 0 else range(BUCKETS)


def pick_block(index, refs):
    value = refs[0][...]
    for k in range(1, len(refs)):
        value = jnp.where(index == k, refs[k][...], value)
    return value


def project_kernel(
    heads, per, info, x0, x1, x2, x3, gain_ref, w_ref, table, normed, qa, ka, va, kt, vt, near
):
    step = pl.program_id(0)

    @pl.when(step == 0)
    def _():
        for d in (-1, 0, 1):
            buckets = near_bucket(d)
            for h in range(heads):
                tile = jnp.zeros((TILE, TILE), FULL)
                for b in buckets_near(d):
                    tile = jnp.where(buckets == b, table[b, h], tile)
                near[h, d + 1] = tile

    rows = x0.shape[0]
    x = pick_block(info[step % RANKS], (x0, x1, x2, x3)).astype(FULL)
    scale = lax.rsqrt(jnp.mean(x * x, axis=-1, keepdims=True) + EPSILON)
    xn = (x * scale * gain_ref[...]).astype(LOW)
    normed[...] = xn
    y = dot_nt(xn, w_ref[...])
    row = lax.broadcasted_iota(jnp.int32, (rows, TILE), 0)
    lane = lax.broadcasted_iota(jnp.int32, (rows, TILE), 1) - HEAD
    place = step * (rows // TILE) + row // TILE
    count = RANKS * per
    is_tile = jnp.logical_and(lane >= 0, lane < count)
    here = tile_at(place, per)
    there = tile_at(jnp.where(is_tile, lane, 0), per)
    position = here * TILE + row % TILE
    q_extra = jnp.where(jnp.logical_or(lane == place, lane == count), 1.0, 0.0)
    v_extra = jnp.where(lane == 0, 1.0, 0.0)
    dead = jnp.where(jnp.logical_and(lane == count, position >= info[RANKS]), -1e30, 0.0)
    left = jnp.logical_and(is_tile, here < there - 1)
    right = jnp.logical_and(is_tile, here > there + 1)
    wide = heads * TILE
    for h in range(heads):
        before, behind = table[BUCKETS // 2 - 1, h], table[BUCKETS - 1, h]
        k_extra = jnp.where(left, before, jnp.where(right, behind, dead))
        at = slice(TILE * h, TILE * h + TILE)
        qa[:, at] = (y[:, at] + q_extra).astype(LOW)
        kh = y[:, wide + TILE * h : wide + TILE * h + TILE] + k_extra
        vh = y[:, 2 * wide + TILE * h : 2 * wide + TILE * h + TILE] + v_extra
        ka[:, at] = kh.astype(LOW)
        va[:, at] = vh.astype(LOW)
        kt[at, :] = kh.T.astype(LOW)
        vt[at, :] = vh.T.astype(LOW)


def project(info, xs, gain, w_qkv, table, heads, per):
    total = RANKS * xs[0].shape[0]
    rows = xs[0].shape[0] // SPLIT
    width = xs[0].shape[1]
    row_block = lambda w: pl.BlockSpec((rows, w), lambda i, c: (i, 0))
    col_block = lambda w: pl.BlockSpec((w, rows), lambda i, c: (0, i))
    wide = heads * TILE
    return pl.pallas_call(
        functools.partial(project_kernel, heads, per),
        grid_spec=pltpu.PrefetchScalarGridSpec(
            num_scalar_prefetch=1,
            grid=(RANKS * SPLIT,),
            in_specs=[pl.BlockSpec((rows, width), lambda i, c: (i // RANKS, 0))] * RANKS
            + [
                whole_spec(gain.shape),
                whole_spec(w_qkv.shape),
                pl.BlockSpec(memory_space=pltpu.SMEM),
            ],
            out_specs=[
                row_block(width),
                row_block(wide),
                row_block(wide),
                row_block(wide),
                col_block(wide),
                col_block(wide),
                whole_spec((heads, 3, TILE, TILE)),
            ],
        ),
        out_shape=[
            jax.ShapeDtypeStruct((total, width), LOW),
            jax.ShapeDtypeStruct((total, wide), LOW),
            jax.ShapeDtypeStruct((total, wide), LOW),
            jax.ShapeDtypeStruct((total, wide), LOW),
            jax.ShapeDtypeStruct((wide, total), LOW),
            jax.ShapeDtypeStruct((wide, total), LOW),
            jax.ShapeDtypeStruct((heads, 3, TILE, TILE), FULL),
        ],
        compiler_params=params(),
        name="project",
        cost_estimate=cost(8 * total * width * heads * HEAD),
    )(info, *xs, gain, w_qkv, table)


def near_tiles(first_place, tiles, per, visit):
    count = RANKS * per
    for u in range(tiles):
        here = tile_at(first_place + u, per)
        for d in (-1, 0, 1):
            there = here + d
            valid = jnp.logical_and(there >= 0, there < count)
            place = tile_place(jnp.clip(there, 0, count - 1), per)
            rows = pl.ds(pl.multiple_of(place * TILE, TILE), TILE)
            visit(d + 1, rows, slice(u * TILE, u * TILE + TILE), jnp.where(valid, 1.0, 0.0))


def score_block(h, first_place, per, qa, ka, near, s_ref):
    bq = qa.shape[0]
    at = slice(TILE * h, TILE * h + TILE)
    s_ref[h] = dot_nt(ka[:, at], qa[:, at])

    def add(d, rows, cols, valid):
        s_ref[h, rows, cols] = s_ref[h, rows, cols] + near[h, d] * valid

    near_tiles(first_place, bq // TILE, per, add)


def forward_kernel(heads, per, offset, qa, ka, vt, near, mixed, ot, lse, s_ref):
    bq = qa.shape[0]
    first = (pl.program_id(0) + offset) * (bq // TILE)
    for h in range(heads):
        score_block(h, first, per, qa, ka, near, s_ref)
    parts = []
    for h in range(heads):
        s = s_ref[h]
        top = jnp.max(s, axis=0, keepdims=True)
        p = jnp.exp(s - top).astype(LOW)
        o = dot_nn(vt[TILE * h : TILE * h + TILE, :], p)
        total = o[HEAD : HEAD + 1]
        o = o[:HEAD] * (1.0 / total)
        ot[HEAD * h : HEAD * h + HEAD, :] = o
        lse[h : h + 1, :] = top + jnp.log(total)
        parts.append(o.T)
    mixed[...] = jnp.concatenate(parts, axis=1).astype(LOW)


def attend(qa, ka, vt, near, part, bq, per):
    total, wide = ka.shape
    heads = wide // TILE
    span = total // SPLIT
    steps = span // bq
    offset = part * steps
    full = lambda shape: pl.BlockSpec(shape, lambda i: tuple(0 for _ in shape))
    width = heads * HEAD
    return pl.pallas_call(
        functools.partial(forward_kernel, heads, per, offset),
        grid=(steps,),
        in_specs=[
            pl.BlockSpec((bq, wide), lambda i: (i + offset, 0)),
            full(ka.shape),
            full(vt.shape),
            full(near.shape),
        ],
        out_specs=[
            pl.BlockSpec((bq, width), lambda i: (i, 0)),
            pl.BlockSpec((width, bq), lambda i: (0, i)),
            pl.BlockSpec((8, bq), lambda i: (0, i)),
        ],
        out_shape=[
            jax.ShapeDtypeStruct((span, width), LOW),
            jax.ShapeDtypeStruct((width, span), FULL),
            jax.ShapeDtypeStruct((8, span), FULL),
        ],
        scratch_shapes=[pltpu.VMEM((heads, total, bq), FULL)],
        compiler_params=params(),
        name="attend",
        cost_estimate=cost(20 * heads * span * total * HEAD),
    )(qa, ka, vt, near)


def middle_kernel(
    first, info, x0, x1, x2, x3, c0, c1, c2, c3, m0, m1, m2, m3, w0, w1, w2, w3,
    gain, w_ffn, *refs
):
    given, (f_keep, f_give, d_keep, d_give, resid_out, grads_out, grads) = refs[:-7], refs[-7:]
    step = pl.program_id(0)
    hid = w_ffn.shape[1] // 2

    @pl.when(step == 0)
    def _():
        grads[...] = jnp.zeros_like(grads) if first else given[0][...].astype(FULL)

    attn = dot_nn(m0[...], w0[...]) + dot_nn(m1[...], w1[...])
    attn = attn + dot_nn(m2[...], w2[...]) + dot_nn(m3[...], w3[...])
    resid = pick_block(info[step], (x0, x1, x2, x3)).astype(FULL) + attn
    resid_out[...] = resid
    scale = lax.rsqrt(jnp.mean(resid * resid, axis=-1, keepdims=True) + EPSILON)
    normed = (resid * scale * gain[...]).astype(LOW)
    hidden = dot_nn(normed, w_ffn[:, :hid])
    grad = pick_block(info[step], (c0, c1, c2, c3))
    d_active = dot_nn(grad, w_ffn[:, hid:])
    square = hidden * hidden
    th = jnp.tanh(GELU_A * hidden * (1.0 + GELU_B * square))
    half = 0.5 * (1.0 + th)
    active = (hidden * half).astype(LOW)
    slope = half + 0.5 * hidden * (1.0 - th * th) * (GELU_A * (1.0 + (3.0 * GELU_B) * square))
    d_hidden = (d_active * slope).astype(LOW)
    dn = dot_nt(d_hidden, w_ffn[:, :hid]).astype(LOW)
    ffn = dot_nt(active, w_ffn[:, hid:]).astype(LOW)

    @pl.when(info[step] % 2 == 0)
    def _():
        d_keep[0] = dn
        f_keep[0] = ffn

    @pl.when(info[step] % 2 == 1)
    def _():
        d_give[0] = dn
        f_give[0] = ffn

    grads[:, :hid] += dot_tn(normed, d_hidden)
    grads[:, hid:] += dot_tn(grad, active)

    @pl.when(step == RANKS - 1)
    def _():
        grads_out[...] = grads[...].astype(LOW)


def middle(info, xs, cs, pieces, outs, gain, w_ffn, part, given):
    rows, width = xs[0].shape[0] // SPLIT, xs[0].shape[1]
    narrow = pieces[0].shape[1]
    own_block = pl.BlockSpec((rows, width), lambda i, c: (part, 0))
    piece_block = pl.BlockSpec((rows, narrow), lambda i, c: (i, 0))
    rel_block = pl.BlockSpec((1, rows, width), lambda i, c: (c[i] // 2, 0, 0))
    pair_block = pl.BlockSpec((1, rows, width), lambda i, c: (i // 2, 0, 0))
    extra = () if given is None else (given,)
    two = jax.ShapeDtypeStruct((2, rows, width), LOW)
    return pl.pallas_call(
        functools.partial(middle_kernel, given is None),
        grid_spec=pltpu.PrefetchScalarGridSpec(
            num_scalar_prefetch=1,
            grid=(RANKS,),
            in_specs=[own_block] * (2 * RANKS)
            + [piece_block] * RANKS
            + [whole_spec(outs[0].shape)] * RANKS
            + [whole_spec(v.shape) for v in (gain, w_ffn) + extra],
            out_specs=[
                rel_block,
                rel_block,
                pair_block,
                pair_block,
                pl.BlockSpec((rows, width), lambda i, c: (i, 0)),
                whole_spec(w_ffn.shape),
            ],
            scratch_shapes=[pltpu.VMEM(w_ffn.shape, FULL)],
        ),
        out_shape=[two, two, two, two]
        + [
            jax.ShapeDtypeStruct((RANKS * rows, width), FULL),
            jax.ShapeDtypeStruct(w_ffn.shape, LOW),
        ],
        compiler_params=params(),
        name="middle",
        cost_estimate=cost(20 * RANKS * rows * width * w_ffn.shape[1] // 2),
    )(info, *xs, *cs, *pieces, *outs, gain, w_ffn, *extra)


def backward_kernel(
    per, offset, kc, info, qa, ka, kt, va, sum_mine, sum_other, resid_ref,
    c0, c1, c2, c3, gain, wo, ot, lse, near, *refs
):
    given = refs[:-11]
    dq, dk, dv, d_near, g_out, tiles, s_ref, ds_ref, dk_acc, dv_acc, d_rows = refs[-11:]
    head, step = pl.program_id(0), pl.program_id(1)
    bq = qa.shape[0]
    total = ka.shape[0]
    count = RANKS * per
    first = (step + offset) * (bq // TILE)
    here = pl.ds(pl.multiple_of(step * bq, bq), bq)

    @pl.when(step == 0)
    def _():
        if len(given) > 0:
            dk_acc[...] = given[0][...]
            dv_acc[...] = given[1][...]
            d_near[...] = given[2][...]
            g_out[...] = given[3][...]
        else:
            dk_acc[...] = jnp.zeros_like(dk_acc)
            dv_acc[...] = jnp.zeros_like(dv_acc)
            d_near[...] = jnp.zeros_like(d_near)
            g_out[...] = jnp.zeros_like(g_out)

    @pl.when(head == 0)
    def _():
        even = info[2 * step] % 2 == 0
        mine, other = sum_mine[0], sum_other[0]
        d_norm = jnp.concatenate(
            [jnp.where(even, mine, other), jnp.where(even, other, mine)], axis=0
        ).astype(FULL)
        cot = jnp.concatenate(
            [pick_block(info[2 * step + k], (c0, c1, c2, c3)) for k in range(2)], axis=0
        ).astype(FULL)
        resid = resid_ref[...]
        scale = lax.rsqrt(jnp.mean(resid * resid, axis=-1, keepdims=True) + EPSILON)
        unit = resid * scale
        along = d_norm * gain[...]
        rows = cot + scale * (along - unit * jnp.mean(along * unit, axis=-1, keepdims=True))
        d_rows[here, :] = rows.astype(LOW)

    s_ref[...] = dot_nt(ka[...], qa[...])

    def add(d, rows, cols, valid):
        s_ref[rows, cols] = s_ref[rows, cols] + near[0, d] * valid

    near_tiles(first, bq // TILE, per, add)
    grad = d_rows[here, :]
    do = dot_nt(grad, wo[...]).astype(LOW)
    do_t = dot_nt(wo[...], grad).astype(LOW).astype(FULL)
    o_t = ot[...]
    g_out[...] += dot_nn(o_t.astype(LOW), grad)
    delta = jnp.sum(do_t[:HEAD] * o_t, axis=0, keepdims=True)
    lse_row = lse[pl.ds(head, 1), :]
    dq_t = jnp.zeros((TILE, bq), FULL)
    for c in range(total // kc):
        rows = slice(kc * c, kc * c + kc)
        p = jnp.exp(s_ref[rows, :] - lse_row)
        d_p = dot_nt(va[rows, :], do)
        d_s = (p * (d_p - delta)).astype(LOW)
        ds_ref[rows, :] = d_s
        dv_acc[rows, :] += dot_nn(p.astype(LOW), do)
        dk_acc[rows, :] += dot_nn(d_s, qa[...])
        dq_t += dot_nn(kt[:, rows], d_s)
    lane = lax.broadcasted_iota(jnp.int32, (bq, TILE), 1)
    dq[...] = jnp.where(lane < HEAD, dq_t.T, 0.0).astype(LOW)

    def collect(d, rows, cols, valid):
        d_near[0, d] += ds_ref[rows, cols].astype(FULL) * valid

    near_tiles(first, bq // TILE, per, collect)

    @pl.when(step == pl.num_programs(1) - 1)
    def _():
        if dk.dtype == FULL:
            dk[...] = dk_acc[...]
            dv[...] = dv_acc[...]
        else:
            side = lax.broadcasted_iota(jnp.int32, (total, TILE), 1)
            dk[...] = jnp.where(side < HEAD, dk_acc[...], 0.0).astype(LOW)
            dv[...] = jnp.where(side < HEAD, dv_acc[...], 0.0).astype(LOW)
        sums = [
            jnp.sum(dk_acc[k * TILE : k * TILE + TILE, :], axis=0, keepdims=True)
            for k in range(count)
        ]
        tiles[0] = jnp.concatenate(sums, axis=0)


def attend_back(
    info, qa, ka, kt, va, sums, resid, cs, gain, wo, ot, lse, near, part, kc, per, given
):
    total, wide = ka.shape
    heads = wide // TILE
    model = resid.shape[1]
    rows = total // SPLIT // RANKS
    bq = 2 * rows
    span = total // SPLIT
    steps = span // bq
    offset = part * steps
    last = part == SPLIT - 1
    once = lambda h, i: jnp.where(h == 0, i, steps - 1)
    head_cols = pl.BlockSpec((total, TILE), lambda h, i, c: (0, h))
    near_block = pl.BlockSpec((1, 3, TILE, TILE), lambda h, i, c: (h, 0, 0, 0))
    out_block = pl.BlockSpec((HEAD, model), lambda h, i, c: (h, 0))
    kind = LOW if last else FULL
    full = lambda shape: pl.BlockSpec(shape, lambda h, i, c: tuple(0 for _ in shape))
    return pl.pallas_call(
        functools.partial(backward_kernel, per, offset, kc),
        grid_spec=pltpu.PrefetchScalarGridSpec(
            num_scalar_prefetch=1,
            grid=(heads, steps),
            in_specs=[
                pl.BlockSpec((bq, TILE), lambda h, i, c: (i + offset, h)),
                head_cols,
                pl.BlockSpec((TILE, total), lambda h, i, c: (h, 0)),
                head_cols,
            ]
            + [pl.BlockSpec((1, rows, model), lambda h, i, c: (once(h, i), 0, 0))] * 2
            + [pl.BlockSpec((bq, model), lambda h, i, c: (once(h, i), 0))]
            + [pl.BlockSpec((rows, model), lambda h, i, c: (part, 0))] * RANKS
            + [
                full(gain.shape),
                pl.BlockSpec((TILE, model), lambda h, i, c: (h, 0)),
                pl.BlockSpec((HEAD, bq), lambda h, i, c: (h, i)),
                pl.BlockSpec((8, bq), lambda h, i, c: (0, i)),
                near_block,
            ]
            + ([] if len(given) == 0 else [head_cols, head_cols, near_block, out_block]),
            out_specs=[
                pl.BlockSpec((bq, TILE), lambda h, i, c: (i, h)),
                head_cols,
                head_cols,
                near_block,
                out_block,
                pl.BlockSpec((1, RANKS * per, TILE), lambda h, i, c: (h, 0, 0)),
            ],
            scratch_shapes=[
                pltpu.VMEM((total, bq), FULL),
                pltpu.VMEM((total, bq), LOW),
                pltpu.VMEM((total, TILE), FULL),
                pltpu.VMEM((total, TILE), FULL),
                pltpu.VMEM((span, model), LOW),
            ],
        ),
        out_shape=[
            jax.ShapeDtypeStruct((span, wide), LOW),
            jax.ShapeDtypeStruct((total, wide), kind),
            jax.ShapeDtypeStruct((total, wide), kind),
            jax.ShapeDtypeStruct((heads, 3, TILE, TILE), FULL),
            jax.ShapeDtypeStruct((heads * HEAD, model), FULL),
            jax.ShapeDtypeStruct((heads, RANKS * per, TILE), FULL),
        ],
        compiler_params=params(),
        name="attend_back",
        cost_estimate=cost(40 * heads * span * total * HEAD),
    )(info, qa, ka, kt, va, *sums, resid, *cs, gain, wo, ot, lse, near, *given)


def bucket_kernel(d_near, out):
    heads = d_near.shape[0]
    found = [[jnp.zeros((1, TILE), FULL)] * BUCKETS for _ in range(heads)]
    for d in (-1, 0, 1):
        buckets = near_bucket(d)
        for b in buckets_near(d):
            here = buckets == b
            for h in range(heads):
                found[h][b] = found[h][b] + jnp.sum(
                    jnp.where(here, d_near[h, d + 1], 0.0), axis=0, keepdims=True
                )
    for h in range(heads):
        out[h] = jnp.concatenate(found[h], axis=0)


def bucket_sums(d_near):
    heads = d_near.shape[0]
    return pl.pallas_call(
        bucket_kernel,
        out_shape=jax.ShapeDtypeStruct((heads, BUCKETS, TILE), FULL),
        compiler_params=params(),
        name="bucket_sums",
    )(d_near)


def tail_kernel(info, dq0, dq1, dk, dv, w_ref, keep, give):
    step = pl.program_id(0)
    wide = dk.shape[1]
    dq = pick_block(step // RANKS, (dq0, dq1))
    out = dot_nn(dq, w_ref[:wide, :]) + dot_nn(dk[...], w_ref[wide : 2 * wide, :])
    out = (out + dot_nn(dv[...], w_ref[2 * wide :, :])).astype(LOW)
    even = info[step % RANKS] % 2 == 0

    @pl.when(even)
    def _():
        keep[0] = out

    @pl.when(jnp.logical_not(even))
    def _():
        give[0] = out


def tail(info, dqs, dk, dv, w_wide):
    total, wide = dk.shape
    model = w_wide.shape[1]
    rows = total // RANKS // SPLIT
    rel_block = pl.BlockSpec(
        (1, rows, model), lambda i, c: (2 * (i // RANKS) + c[i % RANKS] // 2, 0, 0)
    )
    return pl.pallas_call(
        tail_kernel,
        grid_spec=pltpu.PrefetchScalarGridSpec(
            num_scalar_prefetch=1,
            grid=(RANKS * SPLIT,),
            in_specs=[
                pl.BlockSpec((rows, wide), lambda i, c: (jnp.minimum(i, RANKS - 1), 0)),
                pl.BlockSpec((rows, wide), lambda i, c: (jnp.maximum(i - RANKS, 0), 0)),
                pl.BlockSpec((rows, wide), lambda i, c: (i, 0)),
                pl.BlockSpec((rows, wide), lambda i, c: (i, 0)),
                whole_spec(w_wide.shape),
            ],
            out_specs=[rel_block, rel_block],
        ),
        out_shape=[jax.ShapeDtypeStruct((2 * SPLIT, rows, model), LOW)] * 2,
        compiler_params=params(),
        name="tail",
        cost_estimate=cost(6 * total * wide * model),
    )(info, *dqs, dk, dv, w_wide)


def weights_kernel(steps, dq0, dq1, dk, dv, normed, g_out, extra, out, acc):
    step = pl.program_id(0)

    @pl.when(step == 0)
    def _():
        acc[...] = jnp.zeros_like(acc)

    dq = pick_block(step // (steps // 2), (dq0, dq1))
    acc[...] += dot_tn(jnp.concatenate([dq, dk[...], dv[...]], axis=1), normed[...])

    @pl.when(step == steps - 1)
    def _():
        count = acc.shape[0] // TILE
        for j in range(count):
            out[j * HEAD : j * HEAD + HEAD, :] = acc[j * TILE : j * TILE + HEAD, :].astype(LOW)
        base = count * HEAD
        out[base : base + g_out.shape[0], :] = g_out[...].astype(LOW)
        out[base + g_out.shape[0] :, :] = extra[...]


def weights(dqs, dk, dv, normed, g_out, extra):
    total, wide = dk.shape
    model = normed.shape[1]
    steps = 4
    rows = total // steps
    half = steps // 2
    full = lambda shape: pl.BlockSpec(shape, lambda i: tuple(0 for _ in shape))
    block = lambda w: pl.BlockSpec((rows, w), lambda i: (i, 0))
    out_rows = 3 * wide * HEAD // TILE + g_out.shape[0] + extra.shape[0]
    return pl.pallas_call(
        functools.partial(weights_kernel, steps),
        grid=(steps,),
        in_specs=[
            pl.BlockSpec((rows, wide), lambda i: (jnp.minimum(i, half - 1), 0)),
            pl.BlockSpec((rows, wide), lambda i: (jnp.maximum(i - half, 0), 0)),
            block(wide),
            block(wide),
            block(model),
            full(g_out.shape),
            full(extra.shape),
        ],
        out_specs=full((out_rows, model)),
        out_shape=jax.ShapeDtypeStruct((out_rows, model), LOW),
        scratch_shapes=[pltpu.VMEM((3 * wide, model), FULL)],
        compiler_params=params(),
        name="weights",
        cost_estimate=cost(6 * total * wide * model),
    )(*dqs, dk, dv, normed, g_out, extra)


def together(*values):
    return lax.optimization_barrier(values)


def after(value, *given):
    return lax.optimization_barrier((value,) + given)[0]


def swap_seq(value, bit):
    return lax.ppermute(value, "seq", [(i, i ^ bit) for i in range(RANKS)])


def regroup(value, skip):
    pairs = []
    for s in range(RANKS):
        for t in range(RANKS):
            if t != skip and MIX[s] != 0:
                pairs.append((s * RANKS + t, s * RANKS + (t ^ MIX[s])))
    moved = lax.ppermute(value, ("seq", "tensor"), pairs)
    return jnp.where(lax.axis_index("seq") == MIX.index(0), value, moved)


def along_tensor(value, pairs):
    return lax.ppermute(value, "tensor", pairs)


def swap_dp(value):
    return lax.ppermute(value, "dp", [(0, 1), (1, 0)])


def gather_dp(value, axis):
    if lax.axis_size("dp") != 2:
        return lax.all_gather(value, "dp", axis=axis, tiled=True)
    other = swap_dp(value)
    swap = lax.axis_index("dp") == 1
    return jnp.concatenate(
        [jnp.where(swap, other, value), jnp.where(swap, value, other)], axis=axis
    )


def scatter_dp(value, axis):
    if lax.axis_size("dp") != 2:
        return lax.psum_scatter(value, "dp", scatter_dimension=axis, tiled=True).astype(LOW)
    size = value.shape[axis] // 2
    mine = lax.axis_index("dp")
    keep = lax.dynamic_slice_in_dim(value, mine * size, size, axis)
    give = lax.dynamic_slice_in_dim(value, (1 - mine) * size, size, axis)
    return (keep.astype(FULL) + swap_dp(give.astype(LOW)).astype(FULL)).astype(LOW)


def sum_core(value):
    half = value.shape[0] // 2
    core = lax.axis_index("seq") % 2
    keep = lax.dynamic_slice_in_dim(value, core * half, half, 0).astype(FULL)
    give = lax.dynamic_slice_in_dim(value, (1 - core) * half, half, 0)
    return (keep + swap_seq(give, 1).astype(FULL)).astype(LOW)


def sum_chip(value):
    return value.astype(FULL) + swap_seq(value, 2).astype(FULL)


def join_core(value):
    other = swap_seq(value, 1)
    core = lax.axis_index("seq") % 2
    return jnp.concatenate(
        [jnp.where(core == 0, value, other), jnp.where(core == 0, other, value)], axis=0
    )


def normalize(values):
    scale = lax.rsqrt(jnp.mean(values * values, axis=-1, keepdims=True) + EPSILON)
    return values * scale, scale


def norm_back(grad, unit, scale, gain):
    along = grad * gain
    return scale * (along - unit * jnp.mean(along * unit, axis=-1, keepdims=True))


def body(
    inputs, lengths, gain_attn, w_query, w_key, w_value, w_out, bias_table,
    gain_ffn, w_in, w_down, cotangent,
):
    slots, rows_here, model = inputs.shape
    assert lax.axis_size("seq") == RANKS and lax.axis_size("tensor") == RANKS and slots == 3
    total = RANKS * rows_here
    per = rows_here // TILE
    narrow = w_query.shape[1]
    heads = narrow // HEAD
    hid = w_in.shape[1]
    rank = lax.axis_index("tensor")
    chunk = lax.axis_index("seq")
    mine = lax.axis_index("dp")
    slot = jnp.where(rank == 0, 0, rank - 1)
    length = lax.dynamic_index_in_dim(lengths, slot, 0, keepdims=False)
    order = jnp.bitwise_xor(chunk, jnp.arange(RANKS, dtype=jnp.int32)).astype(jnp.int32)
    info = jnp.concatenate([order, length[None], jnp.zeros((3,), jnp.int32)])
    rows_part = rows_here // SPLIT
    size = gain_attn.shape[0]
    cut = lambda v: v.reshape(SPLIT, rows_part, model)

    x_own = lax.dynamic_index_in_dim(inputs, slot, 0, keepdims=False)
    x_far = swap_seq(x_own, 2)
    x_near = swap_seq(x_own, 1)

    flat = bias_table.reshape(-1)
    small = jnp.stack(
        [gain_attn, gain_ffn, jnp.pad(flat, (0, size - flat.shape[0]))]
        + [jnp.zeros((size,), LOW)] * (EXTRA - 3)
    )
    w_first = after(w_query, x_own)
    pack = jnp.concatenate([w_first.T, w_key.T, w_value.T, w_out, small], axis=0)
    pack = regroup(pack, None)
    pack_ready = pack
    w_all = gather_dp(pack, 1)
    main = 4 * narrow
    w_wide = jnp.pad(
        w_all[: 3 * narrow].reshape(3 * heads, HEAD, model), ((0, 0), (0, TILE - HEAD), (0, 0))
    ).reshape(3 * heads * TILE, model)
    gain_one = w_all[main : main + 1].astype(FULL)
    gain_two = w_all[main + 1 : main + 2].astype(FULL)
    table = w_all[main + 2].reshape(-1, size)[:, : flat.shape[0]]
    table = table.reshape(BUCKETS, heads).astype(FULL)
    xs = [x_own, x_near, x_far, swap_seq(x_far, 1)]

    position = chunk * rows_here + jnp.arange(rows_here, dtype=jnp.int32)
    live = jnp.logical_and(position < length, rank != IDLE)
    c_own = lax.dynamic_index_in_dim(cotangent, slot, 0, keepdims=False)
    c_own = jnp.where(live[:, None], c_own, jnp.zeros((), LOW))
    c_first = after(c_own, x_far)
    c_far = swap_seq(c_first, 2)

    ffn_pack = after(jnp.concatenate([w_in, w_down.T], axis=1), pack_ready)
    ffn_pack = regroup(ffn_pack, None)

    normed, qa, ka, va, kt, vt, near = project(info, xs, gain_one, w_wide, table, heads, per)

    out_mine = w_all[3 * narrow : main]
    outs = [out_mine] + [swap_seq(out_mine, bit) for bit in (1, 2, 3)]

    bq = min(512, total // SPLIT)
    attended = [attend(qa, ka, vt, near, 0, bq, per)]
    attended[0], outs, c_far, ffn_pack = together(attended[0], outs, c_far, ffn_pack)
    w_ffn = gather_dp(ffn_pack, 0)
    cs = [c_own, swap_seq(c_first, 1), c_far, swap_seq(c_far, 1)]
    mixed = attended[0][0]
    pieces = [[mixed] + [swap_seq(mixed, bit) for bit in (1, 2, 3)]]
    out_wide = jnp.pad(
        out_mine.reshape(heads, HEAD, model), ((0, 0), (0, TILE - HEAD), (0, 0))
    ).reshape(heads * TILE, model)
    attended.append(attend(qa, ka, vt, near, 1, bq, per))
    attended[1], pieces[0], cs, w_ffn = together(attended[1], pieces[0], cs, w_ffn)
    mixed = attended[1][0]
    pieces.append([mixed] + [swap_seq(mixed, bit) for bit in (1, 2, 3)])

    mids = [middle(info, xs, cs, pieces[0], outs, gain_two, w_ffn, 0, None)]
    mids[0], pieces[1] = together(mids[0], pieces[1])

    def chip_sum(mid):
        return (mid[2].astype(FULL) + swap_seq(mid[3], 1).astype(FULL)).astype(LOW)

    chip = [chip_sum(mids[0])]
    chip_far = [swap_seq(chip[0], 2)]
    mids.append(
        middle(info, xs, cs, pieces[1], outs, gain_two, w_ffn, 1, mids[0][5])
    )
    mids[1], chip_far[0] = together(mids[1], chip_far[0])
    chip.append(chip_sum(mids[1]))
    chip_far.append(swap_seq(chip[1], 2))

    def whole_sum(part):
        both = chip[part].astype(FULL) + chip_far[part].astype(FULL)
        both = both.astype(LOW)
        return both, swap_seq(both, 1)

    ffn = [after(mid[:2], chip[1]) for mid in mids]
    ffn = [f[0].astype(FULL) + swap_seq(f[1], 1).astype(FULL) for f in ffn]
    ffn_far = jnp.stack([f[1].astype(LOW) for f in ffn])
    sums = [whole_sum(0)]
    ffn_far = swap_seq(after(ffn_far, sums[0][0]), 2)
    g_ffn = after(mids[1][5], chip[1])
    g_ffn = lax.psum_scatter(g_ffn, "dp", scatter_dimension=0, tiled=True)

    args = (gain_two, out_wide)
    back = [
        attend_back(
            info, qa, ka, kt, va, sums[0], mids[0][4], cs, *args, *attended[0][1:], near, 0,
            512, per, (),
        )
    ]
    back[0], chip_far[1], ffn_far, g_ffn = together(back[0], chip_far[1], ffn_far, g_ffn)
    sums.append(whole_sum(1))
    resids = [
        lax.dynamic_index_in_dim(
            mid[4].reshape(RANKS, rows_part, model), chunk, 0, keepdims=False
        )
        for mid in mids
    ]
    out_own = jnp.concatenate(
        [
            (resids[part] + (ffn[part][0] + ffn_far[part].astype(FULL))).astype(LOW)
            for part in range(SPLIT)
        ],
        axis=0,
    )
    outputs = lax.all_gather(out_own, "tensor")
    outputs = jnp.stack([outputs[0], outputs[2], outputs[3]])
    g_ffn = regroup(g_ffn, IDLE)
    given = back[0][1:5]
    sums[1] = after(sums[1], out_own)
    back.append(
        attend_back(
            info, qa, ka, kt, va, sums[1], mids[1][4], cs, *args, *attended[1][1:], near, 1,
            512, per, given,
        )
    )
    back[1], g_ffn = together(back[1], g_ffn)
    dk, dv, d_near = back[1][1:4]
    dqs = [b[0] for b in back]
    keep, give = tail(info, dqs, dk, dv, w_wide)
    both = keep.astype(FULL) + swap_seq(give, 1).astype(FULL)
    kept = both[0::2]
    far_low = both[1::2].astype(LOW)
    fars = [swap_seq(far_low[part], 2) for part in range(SPLIT)]
    dqs, dk, dv, d_near, g_ffn = after((dqs, dk, dv, d_near, g_ffn), far_low)
    near_sum = jnp.sum(bucket_sums(d_near), axis=2).T
    tile_sum = back[1][5][:, :, HEAD : HEAD + RANKS * per]
    tiles = tile_at(jnp.arange(RANKS * per), per)
    left = tiles[:, None] < tiles[None, :] - 1
    right = tiles[:, None] > tiles[None, :] + 1
    left_sum = jnp.sum(jnp.where(left, tile_sum, 0.0), axis=(1, 2))
    right_sum = jnp.sum(jnp.where(right, tile_sum, 0.0), axis=(1, 2))
    spot = jnp.arange(BUCKETS)[:, None]
    d_table = near_sum + jnp.where(spot == BUCKETS // 2 - 1, left_sum[None], 0.0)
    d_table = d_table + jnp.where(spot == BUCKETS - 1, right_sum[None], 0.0)
    d_table = d_table.reshape(model // size, flat.shape[0])
    d_table = jnp.pad(d_table, ((0, 0), (0, size - flat.shape[0]))).reshape(1, model)
    extra = jnp.concatenate([d_table, jnp.zeros((EXTRA - 1, model), FULL)], axis=0)
    g_all = weights(dqs, dk, dv, normed, back[1][4], extra.astype(LOW))
    g_all, fars = together(g_all, fars)
    g_all = regroup(scatter_dp(g_all, 1), IDLE)
    g_all = join_core(sum_chip(sum_core(g_all)))
    g_ffn = join_core(sum_chip(sum_core(g_ffn)))

    x_parts, c_parts = cut(x_own).astype(FULL), cut(c_own).astype(FULL)
    spread = []
    for part in range(SPLIT):
        total_two = lax.dynamic_index_in_dim(sums[part][0], chunk // 2, 0, keepdims=False)
        total_two = total_two.astype(FULL)
        unit_two, scale_two = normalize(resids[part])
        gain_ffn_part = jnp.sum(total_two * unit_two, axis=0)
        d_resid = c_parts[part] + norm_back(total_two, unit_two, scale_two, gain_two)
        unit, scale = normalize(x_parts[part])
        grad = kept[part] + fars[part].astype(FULL)
        gain_attn_part = jnp.sum(grad * unit, axis=0)
        own = d_resid + norm_back(grad, unit, scale, gain_one)
        own = jnp.concatenate(
            [own, gain_attn_part[None], gain_ffn_part[None], jnp.zeros((14, model), FULL)], axis=0
        ).astype(LOW)
        r1 = along_tensor(own, [(0, 1), (2, 3)])
        l1 = along_tensor(own, [(3, 2), (2, 1)])
        r2 = along_tensor(r1, [(1, 2)])
        l2 = along_tensor(l1, [(2, 1), (1, 0)])
        r3 = along_tensor(r2, [(2, 3)])
        l3 = along_tensor(l2, [(1, 0)])

        def pick(options):
            out = options[0]
            for index in range(1, RANKS):
                out = jnp.where(rank == index, options[index], out)
            return out

        spread.append(
            [pick((own, r1, r2, r3)), pick((l2, l1, own, r1)), pick((l3, l2, l1, own))]
        )
    grad_inputs = jnp.stack(
        [jnp.concatenate([part[k][:rows_part] for part in spread], axis=0) for k in range(slots)]
    )
    gains = sum(
        part[k][rows_part : rows_part + 2].astype(FULL) for k in range(slots) for part in spread
    )
    gains = gains + swap_seq(gains, 1)
    gains = gains + swap_seq(gains, 2)
    if lax.axis_size("dp") == 2:
        gains = gains + swap_dp(gains)
    else:
        gains = lax.psum(gains, "dp")
    gains = lax.dynamic_slice_in_dim(gains, mine * size, size, 1)
    grad_gain_attn, grad_gain_ffn = gains[0], gains[1]
    grad_table = g_all[main, : flat.shape[0]].reshape(bias_table.shape)
    return (
        outputs,
        grad_inputs,
        grad_gain_attn,
        g_all[:narrow].T,
        g_all[narrow : 2 * narrow].T,
        g_all[2 * narrow : 3 * narrow].T,
        g_all[3 * narrow : main],
        grad_table,
        grad_gain_ffn,
        g_ffn[:, :hid],
        g_ffn[:, hid:].T,
    )


def solution(mesh):
    in_specs = (
        P("dp", "seq", None),
        P("dp"),
        P("dp"),
        P("dp", "tensor"),
        P("dp", "tensor"),
        P("dp", "tensor"),
        P("tensor", "dp"),
        P("dp", "tensor"),
        P("dp"),
        P("dp", "tensor"),
        P("tensor", "dp"),
        P("dp", "seq", None),
    )
    out_specs = (
        P("dp", "seq", None),
        P("dp", "seq", None),
        P("dp"),
        P("dp", "tensor"),
        P("dp", "tensor"),
        P("dp", "tensor"),
        P("tensor", "dp"),
        P("dp", "tensor"),
        P("dp"),
        P("dp", "tensor"),
        P("tensor", "dp"),
    )
    return jax.shard_map(body, mesh=mesh, in_specs=in_specs, out_specs=out_specs, check_vma=False)
```

```python
import functools

import jax
import jax.numpy as jnp
from jax import lax
from jax.experimental import pallas as pl
from jax.experimental.pallas import tpu as pltpu
from jax.sharding import PartitionSpec as P

HEAD = 64
BUCKETS = 32
EPSILON = 1e-06
LIMITS = (12, 16, 23, 32, 46, 64, 91)
LOW = jnp.bfloat16
FULL = jnp.float32
TILE = 128
RANKS = 4
MIX = (0, 2, 1, 3)
IDLE = 1
SPLIT = 2
EXTRA = 32
SHORTEN = 64
GELU_A = 0.7978845608028654
GELU_B = 0.044715
KERNEL_MEMORY = 60 * 1024 * 1024


def bucket_of(relative):
    sign_part = jnp.where(relative > 0, 16, 0).astype(jnp.int32)
    distance = jnp.abs(relative)
    far_part = jnp.full(distance.shape, 8, jnp.int32)
    for limit in LIMITS:
        far_part = far_part + (distance >= limit).astype(jnp.int32)
    return sign_part + jnp.where(distance < 8, distance, far_part)


def dot_nn(left, right):
    return lax.dot_general(left, right, (((1,), (0,)), ((), ())), preferred_element_type=FULL)


def dot_nt(left, right):
    return lax.dot_general(left, right, (((1,), (1,)), ((), ())), preferred_element_type=FULL)


def dot_tn(left, right):
    return lax.dot_general(left, right, (((0,), (0,)), ((), ())), preferred_element_type=FULL)


def tile_place(tile, per):
    sub = per // SPLIT
    return ((tile % per) // sub) * (RANKS * sub) + (tile // per) * sub + tile % sub


def tile_at(place, per):
    sub = per // SPLIT
    return ((place // sub) % RANKS) * per + (place // (RANKS * sub)) * sub + place % sub


def cost(flops):
    return pl.CostEstimate(flops=flops // SHORTEN, bytes_accessed=0, transcendentals=0)


def params():
    return pltpu.CompilerParams(vmem_limit_bytes=KERNEL_MEMORY)


def whole_spec(shape):
    return pl.BlockSpec(shape, lambda i, c: tuple(0 for _ in shape))


def near_bucket(d):
    key = lax.broadcasted_iota(jnp.int32, (TILE, TILE), 0)
    query = lax.broadcasted_iota(jnp.int32, (TILE, TILE), 1)
    return bucket_of(TILE * d + key - query)


def buckets_near(d):
    half = BUCKETS // 2
    if d < 0:
        return range(half)
    return range(half, BUCKETS) if d > 0 else range(BUCKETS)


def pick_block(index, refs):
    value = refs[0][...]
    for k in range(1, len(refs)):
        value = jnp.where(index == k, refs[k][...], value)
    return value


def pick_pair(info, chunk, refs):
    return jnp.concatenate([pick_block(info[chunk + k], refs) for k in range(2)], axis=0)


def project_kernel(
    heads, per, info, x0, x1, x2, x3, gain_ref, w_ref, table, normed, qa, ka, va, kt, vt, near
):
    step = pl.program_id(0)

    @pl.when(step == 0)
    def _():
        for d in (-1, 0, 1):
            buckets = near_bucket(d)
            for h in range(heads):
                tile = jnp.zeros((TILE, TILE), FULL)
                for b in buckets_near(d):
                    tile = jnp.where(buckets == b, table[b, h], tile)
                near[h, d + 1] = tile

    rows = 2 * x0.shape[0]
    x = pick_pair(info, (2 * step) % RANKS, (x0, x1, x2, x3)).astype(FULL)
    scale = lax.rsqrt(jnp.mean(x * x, axis=-1, keepdims=True) + EPSILON)
    xn = (x * scale * gain_ref[...]).astype(LOW)
    normed[...] = xn
    y = dot_nt(xn, w_ref[...])
    row = lax.broadcasted_iota(jnp.int32, (rows, TILE), 0)
    lane = lax.broadcasted_iota(jnp.int32, (rows, TILE), 1) - HEAD
    place = step * (rows // TILE) + row // TILE
    count = RANKS * per
    is_tile = jnp.logical_and(lane >= 0, lane < count)
    here = tile_at(place, per)
    there = tile_at(jnp.where(is_tile, lane, 0), per)
    position = here * TILE + row % TILE
    q_extra = jnp.where(jnp.logical_or(lane == place, lane == count), 1.0, 0.0)
    v_extra = jnp.where(lane == 0, 1.0, 0.0)
    dead = jnp.where(jnp.logical_and(lane == count, position >= info[RANKS]), -1e30, 0.0)
    left = jnp.logical_and(is_tile, here < there - 1)
    right = jnp.logical_and(is_tile, here > there + 1)
    wide = heads * TILE
    for h in range(heads):
        before, behind = table[BUCKETS // 2 - 1, h], table[BUCKETS - 1, h]
        k_extra = jnp.where(left, before, jnp.where(right, behind, dead))
        at = slice(TILE * h, TILE * h + TILE)
        qa[:, at] = (y[:, at] + q_extra).astype(LOW)
        kh = y[:, wide + TILE * h : wide + TILE * h + TILE] + k_extra
        vh = y[:, 2 * wide + TILE * h : 2 * wide + TILE * h + TILE] + v_extra
        ka[:, at] = kh.astype(LOW)
        va[:, at] = vh.astype(LOW)
        kt[at, :] = kh.T.astype(LOW)
        vt[at, :] = vh.T.astype(LOW)


def project(info, xs, gain, w_qkv, table, heads, per):
    total = RANKS * xs[0].shape[0]
    rows = xs[0].shape[0] // SPLIT
    width = xs[0].shape[1]
    row_block = lambda w: pl.BlockSpec((2 * rows, w), lambda i, c: (i, 0))
    col_block = lambda w: pl.BlockSpec((w, 2 * rows), lambda i, c: (0, i))
    wide = heads * TILE
    return pl.pallas_call(
        functools.partial(project_kernel, heads, per),
        grid_spec=pltpu.PrefetchScalarGridSpec(
            num_scalar_prefetch=1,
            grid=(RANKS * SPLIT // 2,),
            in_specs=[pl.BlockSpec((rows, width), lambda i, c: (2 * i // RANKS, 0))] * RANKS
            + [
                whole_spec(gain.shape),
                whole_spec(w_qkv.shape),
                pl.BlockSpec(memory_space=pltpu.SMEM),
            ],
            out_specs=[
                row_block(width),
                row_block(wide),
                row_block(wide),
                row_block(wide),
                col_block(wide),
                col_block(wide),
                whole_spec((heads, 3, TILE, TILE)),
            ],
        ),
        out_shape=[
            jax.ShapeDtypeStruct((total, width), LOW),
            jax.ShapeDtypeStruct((total, wide), LOW),
            jax.ShapeDtypeStruct((total, wide), LOW),
            jax.ShapeDtypeStruct((total, wide), LOW),
            jax.ShapeDtypeStruct((wide, total), LOW),
            jax.ShapeDtypeStruct((wide, total), LOW),
            jax.ShapeDtypeStruct((heads, 3, TILE, TILE), FULL),
        ],
        compiler_params=params(),
        name="project",
        cost_estimate=cost(8 * total * width * heads * HEAD),
    )(info, *xs, gain, w_qkv, table)


def near_tiles(first_place, tiles, per, visit):
    count = RANKS * per
    for u in range(tiles):
        here = tile_at(first_place + u, per)
        for d in (-1, 0, 1):
            there = here + d
            valid = jnp.logical_and(there >= 0, there < count)
            place = tile_place(jnp.clip(there, 0, count - 1), per)
            rows = pl.ds(pl.multiple_of(place * TILE, TILE), TILE)
            visit(d + 1, rows, slice(u * TILE, u * TILE + TILE), jnp.where(valid, 1.0, 0.0))


def score_block(h, first_place, per, qa, ka, near, s_ref):
    bq = qa.shape[0]
    at = slice(TILE * h, TILE * h + TILE)
    s_ref[h] = dot_nt(ka[:, at], qa[:, at])

    def add(d, rows, cols, valid):
        s_ref[h, rows, cols] = s_ref[h, rows, cols] + near[h, d] * valid

    near_tiles(first_place, bq // TILE, per, add)


def forward_kernel(heads, per, offset, qa, ka, vt, near, mixed, ot, lse, s_ref):
    bq = qa.shape[0]
    first = (pl.program_id(0) + offset) * (bq // TILE)
    for h in range(heads):
        score_block(h, first, per, qa, ka, near, s_ref)
    parts = []
    for h in range(heads):
        s = s_ref[h]
        top = jnp.max(s, axis=0, keepdims=True)
        p = jnp.exp(s - top).astype(LOW)
        o = dot_nn(vt[TILE * h : TILE * h + TILE, :], p)
        total = o[HEAD : HEAD + 1]
        o = o[:HEAD] * (1.0 / total)
        ot[HEAD * h : HEAD * h + HEAD, :] = o
        lse[h : h + 1, :] = top + jnp.log(total)
        parts.append(o.T)
    mixed[...] = jnp.concatenate(parts, axis=1).astype(LOW)


def attend(qa, ka, vt, near, part, bq, per):
    total, wide = ka.shape
    heads = wide // TILE
    span = total // SPLIT
    steps = span // bq
    offset = part * steps
    full = lambda shape: pl.BlockSpec(shape, lambda i: tuple(0 for _ in shape))
    width = heads * HEAD
    return pl.pallas_call(
        functools.partial(forward_kernel, heads, per, offset),
        grid=(steps,),
        in_specs=[
            pl.BlockSpec((bq, wide), lambda i: (i + offset, 0)),
            full(ka.shape),
            full(vt.shape),
            full(near.shape),
        ],
        out_specs=[
            pl.BlockSpec((bq, width), lambda i: (i, 0)),
            pl.BlockSpec((width, bq), lambda i: (0, i)),
            pl.BlockSpec((8, bq), lambda i: (0, i)),
        ],
        out_shape=[
            jax.ShapeDtypeStruct((span, width), LOW),
            jax.ShapeDtypeStruct((width, span), FULL),
            jax.ShapeDtypeStruct((8, span), FULL),
        ],
        scratch_shapes=[pltpu.VMEM((heads, total, bq), FULL)],
        compiler_params=params(),
        name="attend",
        cost_estimate=cost(20 * heads * span * total * HEAD),
    )(qa, ka, vt, near)


def middle_kernel(
    first, info, x0, x1, x2, x3, c0, c1, c2, c3, m0, m1, m2, m3, w0, w1, w2, w3,
    gain, w_ffn, *refs
):
    given, (f_keep, f_give, d_keep, d_give, resid_out, grads_out, grads) = refs[:-7], refs[-7:]
    step = pl.program_id(0)
    hid = w_ffn.shape[1] // 2

    @pl.when(step == 0)
    def _():
        grads[...] = jnp.zeros_like(grads) if first else given[0][...].astype(FULL)

    attn = dot_nn(m0[...], w0[...]) + dot_nn(m1[...], w1[...])
    attn = attn + dot_nn(m2[...], w2[...]) + dot_nn(m3[...], w3[...])
    resid = pick_block(info[step], (x0, x1, x2, x3)).astype(FULL) + attn
    resid_out[...] = resid
    scale = lax.rsqrt(jnp.mean(resid * resid, axis=-1, keepdims=True) + EPSILON)
    normed = (resid * scale * gain[...]).astype(LOW)
    hidden = dot_nn(normed, w_ffn[:, :hid])
    grad = pick_block(info[step], (c0, c1, c2, c3))
    d_active = dot_nn(grad, w_ffn[:, hid:])
    square = hidden * hidden
    th = jnp.tanh(GELU_A * hidden * (1.0 + GELU_B * square))
    half = 0.5 * (1.0 + th)
    active = (hidden * half).astype(LOW)
    slope = half + 0.5 * hidden * (1.0 - th * th) * (GELU_A * (1.0 + (3.0 * GELU_B) * square))
    d_hidden = (d_active * slope).astype(LOW)
    dn = dot_nt(d_hidden, w_ffn[:, :hid]).astype(LOW)
    ffn = dot_nt(active, w_ffn[:, hid:]).astype(LOW)

    @pl.when(info[step] % 2 == 0)
    def _():
        d_keep[0] = dn
        f_keep[0] = ffn

    @pl.when(info[step] % 2 == 1)
    def _():
        d_give[0] = dn
        f_give[0] = ffn

    grads[:, :hid] += dot_tn(normed, d_hidden)
    grads[:, hid:] += dot_tn(grad, active)

    @pl.when(step == RANKS - 1)
    def _():
        grads_out[...] = grads[...].astype(LOW)


def middle(info, xs, cs, pieces, outs, gain, w_ffn, part, given):
    rows, width = xs[0].shape[0] // SPLIT, xs[0].shape[1]
    narrow = pieces[0].shape[1]
    own_block = pl.BlockSpec((rows, width), lambda i, c: (part, 0))
    piece_block = pl.BlockSpec((rows, narrow), lambda i, c: (i, 0))
    rel_block = pl.BlockSpec((1, rows, width), lambda i, c: (c[i] // 2, 0, 0))
    pair_block = pl.BlockSpec((1, rows, width), lambda i, c: (i // 2, 0, 0))
    extra = () if given is None else (given,)
    two = jax.ShapeDtypeStruct((2, rows, width), LOW)
    return pl.pallas_call(
        functools.partial(middle_kernel, given is None),
        grid_spec=pltpu.PrefetchScalarGridSpec(
            num_scalar_prefetch=1,
            grid=(RANKS,),
            in_specs=[own_block] * (2 * RANKS)
            + [piece_block] * RANKS
            + [whole_spec(outs[0].shape)] * RANKS
            + [whole_spec(v.shape) for v in (gain, w_ffn) + extra],
            out_specs=[
                rel_block,
                rel_block,
                pair_block,
                pair_block,
                pl.BlockSpec((rows, width), lambda i, c: (i, 0)),
                whole_spec(w_ffn.shape),
            ],
            scratch_shapes=[pltpu.VMEM(w_ffn.shape, FULL)],
        ),
        out_shape=[two, two, two, two]
        + [
            jax.ShapeDtypeStruct((RANKS * rows, width), FULL),
            jax.ShapeDtypeStruct(w_ffn.shape, LOW),
        ],
        compiler_params=params(),
        name="middle",
        cost_estimate=cost(20 * RANKS * rows * width * w_ffn.shape[1] // 2),
    )(info, *xs, *cs, *pieces, *outs, gain, w_ffn, *extra)


def backward_kernel(
    per, offset, kc, info, qa, ka, kt, va, sum_mine, sum_other, resid_ref,
    c0, c1, c2, c3, gain, wo, ot, lse, near, *refs
):
    given = refs[:-11]
    dq, dk, dv, d_near, g_out, tiles, s_ref, ds_ref, dk_acc, dv_acc, d_rows = refs[-11:]
    head, step = pl.program_id(0), pl.program_id(1)
    bq = qa.shape[0]
    total = ka.shape[0]
    count = RANKS * per
    first = (step + offset) * (bq // TILE)
    here = pl.ds(pl.multiple_of(step * bq, bq), bq)

    @pl.when(step == 0)
    def _():
        if len(given) > 0:
            dk_acc[...] = given[0][...]
            dv_acc[...] = given[1][...]
            d_near[...] = given[2][...]
            g_out[...] = given[3][...]
        else:
            dk_acc[...] = jnp.zeros_like(dk_acc)
            dv_acc[...] = jnp.zeros_like(dv_acc)
            d_near[...] = jnp.zeros_like(d_near)
            g_out[...] = jnp.zeros_like(g_out)

    @pl.when(head == 0)
    def _():
        even = info[2 * step] % 2 == 0
        mine, other = sum_mine[0], sum_other[0]
        d_norm = jnp.concatenate(
            [jnp.where(even, mine, other), jnp.where(even, other, mine)], axis=0
        ).astype(FULL)
        cot = jnp.concatenate(
            [pick_block(info[2 * step + k], (c0, c1, c2, c3)) for k in range(2)], axis=0
        ).astype(FULL)
        resid = resid_ref[...]
        scale = lax.rsqrt(jnp.mean(resid * resid, axis=-1, keepdims=True) + EPSILON)
        unit = resid * scale
        along = d_norm * gain[...]
        rows = cot + scale * (along - unit * jnp.mean(along * unit, axis=-1, keepdims=True))
        d_rows[here, :] = rows.astype(LOW)

    s_ref[...] = dot_nt(ka[...], qa[...])

    def add(d, rows, cols, valid):
        s_ref[rows, cols] = s_ref[rows, cols] + near[0, d] * valid

    near_tiles(first, bq // TILE, per, add)
    grad = d_rows[here, :]
    do = dot_nt(grad, wo[...]).astype(LOW)
    do_t = dot_nt(wo[...], grad).astype(LOW).astype(FULL)
    o_t = ot[...]
    g_out[...] += dot_nn(o_t.astype(LOW), grad)
    delta = jnp.sum(do_t[:HEAD] * o_t, axis=0, keepdims=True)
    lse_row = lse[pl.ds(head, 1), :]
    dq_t = jnp.zeros((TILE, bq), FULL)
    for c in range(total // kc):
        rows = slice(kc * c, kc * c + kc)
        p = jnp.exp(s_ref[rows, :] - lse_row)
        d_p = dot_nt(va[rows, :], do)
        d_s = (p * (d_p - delta)).astype(LOW)
        ds_ref[rows, :] = d_s
        dv_acc[rows, :] += dot_nn(p.astype(LOW), do)
        dk_acc[rows, :] += dot_nn(d_s, qa[...])
        dq_t += dot_nn(kt[:, rows], d_s)
    lane = lax.broadcasted_iota(jnp.int32, (bq, TILE), 1)
    dq[...] = jnp.where(lane < HEAD, dq_t.T, 0.0).astype(LOW)

    def collect(d, rows, cols, valid):
        d_near[0, d] += ds_ref[rows, cols].astype(FULL) * valid

    near_tiles(first, bq // TILE, per, collect)

    @pl.when(step == pl.num_programs(1) - 1)
    def _():
        if dk.dtype == FULL:
            dk[...] = dk_acc[...]
            dv[...] = dv_acc[...]
        else:
            side = lax.broadcasted_iota(jnp.int32, (total, TILE), 1)
            dk[...] = jnp.where(side < HEAD, dk_acc[...], 0.0).astype(LOW)
            dv[...] = jnp.where(side < HEAD, dv_acc[...], 0.0).astype(LOW)
        sums = [
            jnp.sum(dk_acc[k * TILE : k * TILE + TILE, :], axis=0, keepdims=True)
            for k in range(count)
        ]
        tiles[0] = jnp.concatenate(sums, axis=0)


def attend_back(
    info, qa, ka, kt, va, sums, resid, cs, gain, wo, ot, lse, near, part, kc, per, given
):
    total, wide = ka.shape
    heads = wide // TILE
    model = resid.shape[1]
    rows = total // SPLIT // RANKS
    bq = 2 * rows
    span = total // SPLIT
    steps = span // bq
    offset = part * steps
    last = part == SPLIT - 1
    once = lambda h, i: jnp.where(h == 0, i, steps - 1)
    head_cols = pl.BlockSpec((total, TILE), lambda h, i, c: (0, h))
    near_block = pl.BlockSpec((1, 3, TILE, TILE), lambda h, i, c: (h, 0, 0, 0))
    out_block = pl.BlockSpec((HEAD, model), lambda h, i, c: (h, 0))
    kind = LOW if last else FULL
    full = lambda shape: pl.BlockSpec(shape, lambda h, i, c: tuple(0 for _ in shape))
    return pl.pallas_call(
        functools.partial(backward_kernel, per, offset, kc),
        grid_spec=pltpu.PrefetchScalarGridSpec(
            num_scalar_prefetch=1,
            grid=(heads, steps),
            in_specs=[
                pl.BlockSpec((bq, TILE), lambda h, i, c: (i + offset, h)),
                head_cols,
                pl.BlockSpec((TILE, total), lambda h, i, c: (h, 0)),
                head_cols,
            ]
            + [pl.BlockSpec((1, rows, model), lambda h, i, c: (once(h, i), 0, 0))] * 2
            + [pl.BlockSpec((bq, model), lambda h, i, c: (once(h, i), 0))]
            + [pl.BlockSpec((rows, model), lambda h, i, c: (part, 0))] * RANKS
            + [
                full(gain.shape),
                pl.BlockSpec((TILE, model), lambda h, i, c: (h, 0)),
                pl.BlockSpec((HEAD, bq), lambda h, i, c: (h, i)),
                pl.BlockSpec((8, bq), lambda h, i, c: (0, i)),
                near_block,
            ]
            + ([] if len(given) == 0 else [head_cols, head_cols, near_block, out_block]),
            out_specs=[
                pl.BlockSpec((bq, TILE), lambda h, i, c: (i, h)),
                head_cols,
                head_cols,
                near_block,
                out_block,
                pl.BlockSpec((1, RANKS * per, TILE), lambda h, i, c: (h, 0, 0)),
            ],
            scratch_shapes=[
                pltpu.VMEM((total, bq), FULL),
                pltpu.VMEM((total, bq), LOW),
                pltpu.VMEM((total, TILE), FULL),
                pltpu.VMEM((total, TILE), FULL),
                pltpu.VMEM((span, model), LOW),
            ],
        ),
        out_shape=[
            jax.ShapeDtypeStruct((span, wide), LOW),
            jax.ShapeDtypeStruct((total, wide), kind),
            jax.ShapeDtypeStruct((total, wide), kind),
            jax.ShapeDtypeStruct((heads, 3, TILE, TILE), FULL),
            jax.ShapeDtypeStruct((heads * HEAD, model), FULL),
            jax.ShapeDtypeStruct((heads, RANKS * per, TILE), FULL),
        ],
        compiler_params=params(),
        name="attend_back",
        cost_estimate=cost(40 * heads * span * total * HEAD),
    )(info, qa, ka, kt, va, *sums, resid, *cs, gain, wo, ot, lse, near, *given)


def bucket_kernel(d_near, out):
    heads = d_near.shape[0]
    found = [[jnp.zeros((1, TILE), FULL)] * BUCKETS for _ in range(heads)]
    for d in (-1, 0, 1):
        buckets = near_bucket(d)
        for b in buckets_near(d):
            here = buckets == b
            for h in range(heads):
                found[h][b] = found[h][b] + jnp.sum(
                    jnp.where(here, d_near[h, d + 1], 0.0), axis=0, keepdims=True
                )
    for h in range(heads):
        out[h] = jnp.concatenate(found[h], axis=0)


def bucket_sums(d_near):
    heads = d_near.shape[0]
    return pl.pallas_call(
        bucket_kernel,
        out_shape=jax.ShapeDtypeStruct((heads, BUCKETS, TILE), FULL),
        compiler_params=params(),
        name="bucket_sums",
    )(d_near)


def tail_kernel(info, dq0, dq1, dk, dv, w_ref, keep, give):
    wide = dk.shape[1]
    dq = pick_block(pl.program_id(0), (dq0, dq1))
    out = dot_nn(dq, w_ref[:wide, :]) + dot_nn(dk[...], w_ref[wide : 2 * wide, :])
    out = (out + dot_nn(dv[...], w_ref[2 * wide :, :])).astype(LOW)
    rows = out.shape[0] // RANKS
    even = info[0] % 2 == 0
    low = info[0] // 2 == 0
    parts = [out[k * rows : k * rows + rows] for k in range(RANKS)]
    kept = [jnp.where(even, parts[k], parts[k + 1]) for k in (0, 2)]
    given = [jnp.where(even, parts[k + 1], parts[k]) for k in (0, 2)]
    keep[0], keep[1] = jnp.where(low, kept[0], kept[1]), jnp.where(low, kept[1], kept[0])
    give[0], give[1] = jnp.where(low, given[0], given[1]), jnp.where(low, given[1], given[0])


def tail(info, dqs, dk, dv, w_wide):
    total, wide = dk.shape
    model = w_wide.shape[1]
    span = total // SPLIT
    rows = span // RANKS
    rel_block = pl.BlockSpec((2, rows, model), lambda i, c: (i, 0, 0))
    return pl.pallas_call(
        tail_kernel,
        grid_spec=pltpu.PrefetchScalarGridSpec(
            num_scalar_prefetch=1,
            grid=(SPLIT,),
            in_specs=[
                whole_spec((span, wide)),
                whole_spec((span, wide)),
                pl.BlockSpec((span, wide), lambda i, c: (i, 0)),
                pl.BlockSpec((span, wide), lambda i, c: (i, 0)),
                whole_spec(w_wide.shape),
            ],
            out_specs=[rel_block, rel_block],
        ),
        out_shape=[jax.ShapeDtypeStruct((2 * SPLIT, rows, model), LOW)] * 2,
        compiler_params=params(),
        name="tail",
        cost_estimate=cost(6 * total * wide * model),
    )(info, *dqs, dk, dv, w_wide)


def weights_kernel(steps, dq0, dq1, dk, dv, normed, g_out, extra, out, acc):
    step = pl.program_id(0)

    @pl.when(step == 0)
    def _():
        acc[...] = jnp.zeros_like(acc)

    dq = pick_block(step // (steps // 2), (dq0, dq1))
    acc[...] += dot_tn(jnp.concatenate([dq, dk[...], dv[...]], axis=1), normed[...])

    @pl.when(step == steps - 1)
    def _():
        count = acc.shape[0] // TILE
        for j in range(count):
            out[j * HEAD : j * HEAD + HEAD, :] = acc[j * TILE : j * TILE + HEAD, :].astype(LOW)
        base = count * HEAD
        out[base : base + g_out.shape[0], :] = g_out[...].astype(LOW)
        out[base + g_out.shape[0] :, :] = extra[...]


def weights(dqs, dk, dv, normed, g_out, extra):
    total, wide = dk.shape
    model = normed.shape[1]
    steps = 4
    rows = total // steps
    half = steps // 2
    full = lambda shape: pl.BlockSpec(shape, lambda i: tuple(0 for _ in shape))
    block = lambda w: pl.BlockSpec((rows, w), lambda i: (i, 0))
    out_rows = 3 * wide * HEAD // TILE + g_out.shape[0] + extra.shape[0]
    return pl.pallas_call(
        functools.partial(weights_kernel, steps),
        grid=(steps,),
        in_specs=[
            pl.BlockSpec((rows, wide), lambda i: (jnp.minimum(i, half - 1), 0)),
            pl.BlockSpec((rows, wide), lambda i: (jnp.maximum(i - half, 0), 0)),
            block(wide),
            block(wide),
            block(model),
            full(g_out.shape),
            full(extra.shape),
        ],
        out_specs=full((out_rows, model)),
        out_shape=jax.ShapeDtypeStruct((out_rows, model), LOW),
        scratch_shapes=[pltpu.VMEM((3 * wide, model), FULL)],
        compiler_params=params(),
        name="weights",
        cost_estimate=cost(6 * total * wide * model),
    )(*dqs, dk, dv, normed, g_out, extra)


def together(*values):
    return lax.optimization_barrier(values)


def after(value, *given):
    return lax.optimization_barrier((value,) + given)[0]


def swap_seq(value, bit):
    return lax.ppermute(value, "seq", [(i, i ^ bit) for i in range(RANKS)])


def regroup(value, skip):
    pairs = []
    for s in range(RANKS):
        for t in range(RANKS):
            if t != skip and MIX[s] != 0:
                pairs.append((s * RANKS + t, s * RANKS + (t ^ MIX[s])))
    moved = lax.ppermute(value, ("seq", "tensor"), pairs)
    return jnp.where(lax.axis_index("seq") == MIX.index(0), value, moved)


def along_tensor(value, pairs):
    return lax.ppermute(value, "tensor", pairs)


def step_one(own):
    return along_tensor(own, [(0, 1), (2, 3)]), along_tensor(own, [(3, 2), (2, 1)])


def step_two(moved):
    return along_tensor(moved[0], [(1, 2)]), along_tensor(moved[1], [(2, 1), (1, 0)])


def step_three(moved):
    return along_tensor(moved[0], [(2, 3)]), along_tensor(moved[1], [(1, 0)])


HOME = (0, 0, 1, 2)
PLACES = (
    ((None, 0, None, 1), (None, 1, 2, None)),
    ((None, None, 0, None), (1, 2, None, None)),
    ((None, None, None, 0), (2, None, None, None)),
)


def by_rank(values, rank):
    out = values[0]
    for index in range(1, len(values)):
        out = jnp.where(rank == index, values[index], out)
    return out


def keep_step(held, own, moved, places, rank):
    for value, place in zip(moved, places):
        got = by_rank([p is not None for p in place], rank)
        at = by_rank([HOME[k] if p is None else p for k, p in enumerate(place)], rank)
        value = jnp.where(got, value, own)
        held = lax.dynamic_update_slice(held, value[None], (at, 0, 0))
    return held


def swap_dp(value):
    return lax.ppermute(value, "dp", [(0, 1), (1, 0)])


def join_dp(halves, axis):
    if len(halves) == 1:
        return lax.all_gather(halves[0], "dp", axis=axis, tiled=True)
    value, other = halves
    swap = lax.axis_index("dp") == 1
    return jnp.concatenate(
        [jnp.where(swap, other, value), jnp.where(swap, value, other)], axis=axis
    )


def gather_dp(value, axis):
    if lax.axis_size("dp") != 2:
        return join_dp((value,), axis)
    return join_dp((value, swap_dp(value)), axis)


def scatter_dp(value, axis):
    if lax.axis_size("dp") != 2:
        return lax.psum_scatter(value, "dp", scatter_dimension=axis, tiled=True).astype(LOW)
    size = value.shape[axis] // 2
    mine = lax.axis_index("dp")
    keep = lax.dynamic_slice_in_dim(value, mine * size, size, axis)
    give = lax.dynamic_slice_in_dim(value, (1 - mine) * size, size, axis)
    return (keep.astype(FULL) + swap_dp(give.astype(LOW)).astype(FULL)).astype(LOW)


def sum_pair(value, bit):
    return value.astype(FULL) + swap_seq(value, bit).astype(FULL)


def normalize(values):
    scale = lax.rsqrt(jnp.mean(values * values, axis=-1, keepdims=True) + EPSILON)
    return values * scale, scale


def norm_back(grad, unit, scale, gain):
    along = grad * gain
    return scale * (along - unit * jnp.mean(along * unit, axis=-1, keepdims=True))


def body(
    inputs, lengths, gain_attn, w_query, w_key, w_value, w_out, bias_table,
    gain_ffn, w_in, w_down, cotangent,
):
    slots, rows_here, model = inputs.shape
    assert lax.axis_size("seq") == RANKS and lax.axis_size("tensor") == RANKS and slots == 3
    total = RANKS * rows_here
    per = rows_here // TILE
    narrow = w_query.shape[1]
    heads = narrow // HEAD
    hid = w_in.shape[1]
    rank = lax.axis_index("tensor")
    chunk = lax.axis_index("seq")
    mine = lax.axis_index("dp")
    slot = jnp.where(rank == 0, 0, rank - 1)
    length = lax.dynamic_index_in_dim(lengths, slot, 0, keepdims=False)
    order = jnp.bitwise_xor(chunk, jnp.arange(RANKS, dtype=jnp.int32)).astype(jnp.int32)
    info = jnp.concatenate([order, length[None], jnp.zeros((3,), jnp.int32)])
    rows_part = rows_here // SPLIT
    size = gain_attn.shape[0]
    cut = lambda v: v.reshape(SPLIT, rows_part, model)

    x_own = lax.dynamic_index_in_dim(inputs, slot, 0, keepdims=False)
    x_far = swap_seq(x_own, 2)
    x_near = swap_seq(x_own, 1)

    flat = bias_table.reshape(-1)
    small = jnp.stack(
        [gain_attn, gain_ffn, jnp.pad(flat, (0, size - flat.shape[0]))]
        + [jnp.zeros((size,), LOW)] * (EXTRA - 3)
    )
    w_first = after(w_query, x_own)
    pack = jnp.concatenate([w_first.T, w_key.T, w_value.T, w_out, small], axis=0)
    pack = regroup(pack, None)
    w_all = gather_dp(pack, 1)
    main = 4 * narrow
    w_wide = jnp.pad(
        w_all[: 3 * narrow].reshape(3 * heads, HEAD, model), ((0, 0), (0, TILE - HEAD), (0, 0))
    ).reshape(3 * heads * TILE, model)
    gain_one = w_all[main : main + 1].astype(FULL)
    gain_two = w_all[main + 1 : main + 2].astype(FULL)
    table = w_all[main + 2].reshape(-1, size)[:, : flat.shape[0]]
    table = table.reshape(BUCKETS, heads).astype(FULL)
    xs = [x_own, x_near, x_far, swap_seq(x_far, 1)]

    position = chunk * rows_here + jnp.arange(rows_here, dtype=jnp.int32)
    live = jnp.logical_and(position < length, rank != IDLE)
    c_own = lax.dynamic_index_in_dim(cotangent, slot, 0, keepdims=False)
    c_own = jnp.where(live[:, None], c_own, jnp.zeros((), LOW))
    ffn_pack = regroup(after(jnp.concatenate([w_in, w_down.T], axis=1), pack), None)
    c_first = after(c_own, x_far)
    c_far = swap_seq(c_first, 2)

    normed, qa, ka, va, kt, vt, near = project(info, xs, gain_one, w_wide, table, heads, per)

    normed, c_far, ffn_pack = together(normed, c_far, ffn_pack)
    qa, ka, vt, _ = together(qa, ka, vt, normed)
    out_mine = w_all[3 * narrow : main]
    out_near, out_far = swap_seq(out_mine, 1), swap_seq(out_mine, 2)
    ffn_halves = (ffn_pack, swap_dp(ffn_pack)) if lax.axis_size("dp") == 2 else (ffn_pack,)
    cs = [c_own, swap_seq(c_first, 1), c_far, swap_seq(c_far, 1)]
    out_wide = jnp.pad(
        out_mine.reshape(heads, HEAD, model), ((0, 0), (0, TILE - HEAD), (0, 0))
    ).reshape(heads * TILE, model)

    bq = min(512, total // SPLIT)
    attended = [attend(qa, ka, vt, near, 0, bq, per)]
    attended[0], cs, out_far = together(attended[0], cs, out_far)
    outs = [out_mine, out_near, out_far, swap_seq(out_far, 1)]
    mixed = attended[0][0]
    pieces = [[mixed] + [swap_seq(mixed, bit) for bit in (1, 2, 3)]]

    attended.append(attend(after(qa, mixed), ka, vt, near, 1, bq, per))
    attended[1], pieces[0], outs, ffn_halves = together(
        attended[1], pieces[0], outs, ffn_halves
    )
    w_ffn = join_dp(ffn_halves, 0)
    mixed = attended[1][0]
    pieces.append([mixed] + [swap_seq(mixed, bit) for bit in (1, 2, 3)])

    def chip_sum(mid, core):
        return (mid[2].astype(FULL) + core.astype(FULL)).astype(LOW)

    def whole_sum(part):
        both = chip[part].astype(FULL) + chip_far[part].astype(FULL)
        both = both.astype(LOW)
        return both, swap_seq(both, 1)

    def out_rows(part):
        resid = lax.dynamic_index_in_dim(
            mids[part][4].reshape(RANKS, rows_part, model), chunk, 0, keepdims=False
        )
        return (resid + (ffn[part][0] + ffn_far[part].astype(FULL))).astype(LOW)

    mids, chip, chip_far = [], [], []
    for part in range(SPLIT):
        mid = middle(
            info, xs, cs, pieces[part], outs, gain_two, w_ffn, part,
            None if part == 0 else mids[0][5],
        )
        if part == 0:
            mid, pieces[1] = together(mid, pieces[1])
        else:
            mid, chip_far[0] = together(mid, chip_far[0])
        mids.append(mid)
        chip.append(chip_sum(mid, swap_seq(mid[3], 1)))
        chip_far.append(swap_seq(chip[part], 2))
        if part == 0:
            pieces[1] = after(pieces[1], chip[0])

    sums = [whole_sum(0)]
    ffn = [after(mid[:2], chip[1]) for mid in mids]
    ffn = [f[0].astype(FULL) + swap_seq(f[1], 1).astype(FULL) for f in ffn]
    ffn_far = jnp.stack([f[1].astype(LOW) for f in ffn])
    g_ffn = after(mids[1][5], chip[1])
    g_ffn = lax.psum_scatter(g_ffn, "dp", scatter_dimension=0, tiled=True)
    sums[0] = after(sums[0], ffn_far)
    ffn_far = swap_seq(ffn_far, 2)

    args = (gain_two, out_wide)
    back = [
        attend_back(
            info, qa, ka, kt, va, sums[0], mids[0][4], cs, *args, *attended[0][1:], near, 0,
            512, per, (),
        )
    ]
    back[0], chip_far[1], ffn_far, g_ffn = together(back[0], chip_far[1], ffn_far, g_ffn)
    sums.append(whole_sum(1))
    out_own = jnp.concatenate([out_rows(part) for part in range(SPLIT)], axis=0)
    out_own = after(out_own, sums[1][0])
    g_ffn = regroup(g_ffn, IDLE)
    given = back[0][1:5]
    sums[1] = after(sums[1], out_own)
    back.append(
        attend_back(
            info, qa, ka, kt, va, sums[1], mids[1][4], cs, *args, *attended[1][1:], near, 1,
            512, per, given,
        )
    )
    back[1], g_ffn = together(back[1], g_ffn)
    outputs = lax.all_gather(after(out_own, g_ffn), "tensor")
    g_core = swap_seq(g_ffn, 1)
    dk, dv, d_near = back[1][1:4]
    resids = [
        lax.dynamic_index_in_dim(
            mid[4].reshape(RANKS, rows_part, model), chunk, 0, keepdims=False
        )
        for mid in mids
    ]

    dqs = [b[0] for b in back]
    keep, give = tail(info, dqs, dk, dv, w_wide)
    core = swap_seq(give, 1)
    found = bucket_sums(after(d_near, give))
    found, core, g_core = together(found, core, g_core)
    far_low = (keep[1::2].astype(FULL) + core[1::2].astype(FULL)).astype(LOW)
    far = swap_seq(far_low, 2)
    dqs, dk, dv, found, g_core = after((dqs, dk, dv, found, g_core), far_low)
    near_sum = jnp.sum(found, axis=2).T
    tile_sum = back[1][5][:, :, HEAD : HEAD + RANKS * per]
    tiles = tile_at(jnp.arange(RANKS * per), per)
    left = tiles[:, None] < tiles[None, :] - 1
    right = tiles[:, None] > tiles[None, :] + 1
    left_sum = jnp.sum(jnp.where(left, tile_sum, 0.0), axis=(1, 2))
    right_sum = jnp.sum(jnp.where(right, tile_sum, 0.0), axis=(1, 2))
    spot = jnp.arange(BUCKETS)[:, None]
    d_table = near_sum + jnp.where(spot == BUCKETS // 2 - 1, left_sum[None], 0.0)
    d_table = d_table + jnp.where(spot == BUCKETS - 1, right_sum[None], 0.0)
    d_table = d_table.reshape(model // size, flat.shape[0])
    d_table = jnp.pad(d_table, ((0, 0), (0, size - flat.shape[0]))).reshape(1, model)
    extra = jnp.concatenate([d_table, jnp.zeros((EXTRA - 1, model), FULL)], axis=0)
    g_all = weights(dqs, dk, dv, normed, back[1][4], extra.astype(LOW))
    g_all, far = together(g_all, far)
    x_parts, c_parts = cut(x_own).astype(FULL), cut(c_own).astype(FULL)
    own, gain_attn_part, gain_ffn_part = [], 0.0, 0.0
    for part in range(SPLIT):
        total_two = lax.dynamic_index_in_dim(sums[part][0], chunk // 2, 0, keepdims=False)
        total_two = total_two.astype(FULL)
        unit_two, scale_two = normalize(resids[part])
        gain_ffn_part = gain_ffn_part + jnp.sum(total_two * unit_two, axis=0)
        d_resid = c_parts[part] + norm_back(total_two, unit_two, scale_two, gain_two)
        unit, scale = normalize(x_parts[part])
        grad = keep[2 * part].astype(FULL) + core[2 * part].astype(FULL)
        grad = grad + far[part].astype(FULL)
        gain_attn_part = gain_attn_part + jnp.sum(grad * unit, axis=0)
        own.append((d_resid + norm_back(grad, unit, scale, gain_one)).astype(LOW))
    own = jnp.concatenate(own, axis=0)
    gains = jnp.stack([gain_attn_part, gain_ffn_part])
    g_ffn = (g_ffn.astype(FULL) + g_core.astype(FULL)).astype(LOW)
    g_all, g_ffn, gains = after((g_all, g_ffn, gains), own)

    held = jnp.zeros((slots, rows_here, model), LOW)
    home = by_rank(HOME, rank)
    held = lax.dynamic_update_slice(held, own[None], (home, 0, 0))
    one = step_one(own)
    gains = sum_pair(sum_pair(gains, 1), 2)
    g_all = scatter_dp(g_all, 1)
    g_far = swap_seq(after(g_ffn, gains), 2)
    one, g_all, gains = together(one, g_all, gains)

    two = step_two(one)
    held = keep_step(held, own, one, PLACES[0], rank)
    own = jnp.where(rank == IDLE, one[0], own)
    g_all = regroup(g_all, IDLE)
    gains = gains + swap_dp(gains) if lax.axis_size("dp") == 2 else lax.psum(gains, "dp")
    gains = gains + along_tensor(gains, [(t, t ^ 1) for t in range(RANKS)])
    g_ffn = g_ffn.astype(FULL) + g_far.astype(FULL)
    g_all = sum_pair(g_all, 1).astype(LOW)
    two, g_all, gains, held, g_ffn, outputs = together(two, g_all, gains, held, g_ffn, outputs)

    three = step_three(two)
    held = keep_step(held, own, two, PLACES[1], rank)
    g_all = sum_pair(g_all, 2)
    gains = gains + along_tensor(gains, [(t, t ^ 2) for t in range(RANKS)])
    grad_in, grad_down = g_ffn[:, :hid], g_ffn[:, hid:].T
    outputs = jnp.stack([outputs[0], outputs[2], outputs[3]])
    three, g_all, gains, held, grad_in, grad_down, outputs = together(
        three, g_all, gains, held, grad_in, grad_down, outputs
    )
    grad_inputs = keep_step(held, own, three, PLACES[2], rank)
    gains = lax.dynamic_slice_in_dim(gains, mine * size, size, 1)
    grad_gain_attn, grad_gain_ffn = gains[0], gains[1]
    grad_table = g_all[main, : flat.shape[0]].reshape(bias_table.shape)
    return (
        outputs,
        grad_inputs,
        grad_gain_attn,
        g_all[:narrow].T,
        g_all[narrow : 2 * narrow].T,
        g_all[2 * narrow : 3 * narrow].T,
        g_all[3 * narrow : main],
        grad_table,
        grad_gain_ffn,
        grad_in,
        grad_down,
    )


def solution(mesh):
    in_specs = (
        P("dp", "seq", None),
        P("dp"),
        P("dp"),
        P("dp", "tensor"),
        P("dp", "tensor"),
        P("dp", "tensor"),
        P("tensor", "dp"),
        P("dp", "tensor"),
        P("dp"),
        P("dp", "tensor"),
        P("tensor", "dp"),
        P("dp", "seq", None),
    )
    out_specs = (
        P("dp", "seq", None),
        P("dp", "seq", None),
        P("dp"),
        P("dp", "tensor"),
        P("dp", "tensor"),
        P("dp", "tensor"),
        P("tensor", "dp"),
        P("dp", "tensor"),
        P("dp"),
        P("dp", "tensor"),
        P("tensor", "dp"),
    )
    return jax.shard_map(body, mesh=mesh, in_specs=in_specs, out_specs=out_specs, check_vma=False)
```

```python
import functools

import jax
import jax.numpy as jnp
from jax import lax
from jax.experimental import pallas as pl
from jax.experimental.pallas import tpu as pltpu
from jax.sharding import PartitionSpec as P

HEAD = 64
BUCKETS = 32
EPSILON = 1e-06
LIMITS = (12, 16, 23, 32, 46, 64, 91)
LOW = jnp.bfloat16
FULL = jnp.float32
TILE = 128
RANKS = 4
MIX = (0, 2, 1, 3)
IDLE = 1
SPLIT = 2
EXTRA = 32
SHORTEN = 64
GELU_A = 0.7978845608028654
GELU_B = 0.044715
KERNEL_MEMORY = 60 * 1024 * 1024


def bucket_of(relative):
    sign_part = jnp.where(relative > 0, 16, 0).astype(jnp.int32)
    distance = jnp.abs(relative)
    far_part = jnp.full(distance.shape, 8, jnp.int32)
    for limit in LIMITS:
        far_part = far_part + (distance >= limit).astype(jnp.int32)
    return sign_part + jnp.where(distance < 8, distance, far_part)


def dot_nn(left, right):
    return lax.dot_general(left, right, (((1,), (0,)), ((), ())), preferred_element_type=FULL)


def dot_nt(left, right):
    return lax.dot_general(left, right, (((1,), (1,)), ((), ())), preferred_element_type=FULL)


def dot_tn(left, right):
    return lax.dot_general(left, right, (((0,), (0,)), ((), ())), preferred_element_type=FULL)


def tile_place(tile, per):
    sub = per // SPLIT
    return ((tile % per) // sub) * (RANKS * sub) + (tile // per) * sub + tile % sub


def tile_at(place, per):
    sub = per // SPLIT
    return ((place // sub) % RANKS) * per + (place // (RANKS * sub)) * sub + place % sub


def cost(flops):
    return pl.CostEstimate(flops=flops // SHORTEN, bytes_accessed=0, transcendentals=0)


def params():
    return pltpu.CompilerParams(vmem_limit_bytes=KERNEL_MEMORY)


def whole_spec(shape):
    return pl.BlockSpec(shape, lambda i, c: tuple(0 for _ in shape))


def near_bucket(d):
    key = lax.broadcasted_iota(jnp.int32, (TILE, TILE), 0)
    query = lax.broadcasted_iota(jnp.int32, (TILE, TILE), 1)
    return bucket_of(TILE * d + key - query)


def buckets_near(d):
    half = BUCKETS // 2
    if d < 0:
        return range(half)
    return range(half, BUCKETS) if d > 0 else range(BUCKETS)


def pick_block(index, refs):
    value = refs[0][...]
    for k in range(1, len(refs)):
        value = jnp.where(index == k, refs[k][...], value)
    return value


def pick_pair(info, chunk, refs):
    return jnp.concatenate([pick_block(info[chunk + k], refs) for k in range(2)], axis=0)


def project_kernel(
    heads, per, info, x0, x1, x2, x3, gain_ref, w_ref, table, normed, qa, ka, va, kt, vt, near
):
    step = pl.program_id(0)

    @pl.when(step == 0)
    def _():
        for d in (-1, 0, 1):
            buckets = near_bucket(d)
            for h in range(heads):
                tile = jnp.zeros((TILE, TILE), FULL)
                for b in buckets_near(d):
                    tile = jnp.where(buckets == b, table[b, h], tile)
                near[h, d + 1] = tile

    rows = 2 * x0.shape[0]
    x = pick_pair(info, (2 * step) % RANKS, (x0, x1, x2, x3)).astype(FULL)
    scale = lax.rsqrt(jnp.mean(x * x, axis=-1, keepdims=True) + EPSILON)
    xn = (x * scale * gain_ref[...]).astype(LOW)
    normed[...] = xn
    y = dot_nt(xn, w_ref[...])
    row = lax.broadcasted_iota(jnp.int32, (rows, TILE), 0)
    lane = lax.broadcasted_iota(jnp.int32, (rows, TILE), 1) - HEAD
    place = step * (rows // TILE) + row // TILE
    count = RANKS * per
    is_tile = jnp.logical_and(lane >= 0, lane < count)
    here = tile_at(place, per)
    there = tile_at(jnp.where(is_tile, lane, 0), per)
    position = here * TILE + row % TILE
    q_extra = jnp.where(jnp.logical_or(lane == place, lane == count), 1.0, 0.0)
    v_extra = jnp.where(lane == 0, 1.0, 0.0)
    dead = jnp.where(jnp.logical_and(lane == count, position >= info[RANKS]), -1e30, 0.0)
    left = jnp.logical_and(is_tile, here < there - 1)
    right = jnp.logical_and(is_tile, here > there + 1)
    wide = heads * TILE
    for h in range(heads):
        before, behind = table[BUCKETS // 2 - 1, h], table[BUCKETS - 1, h]
        k_extra = jnp.where(left, before, jnp.where(right, behind, dead))
        at = slice(TILE * h, TILE * h + TILE)
        qa[:, at] = (y[:, at] + q_extra).astype(LOW)
        kh = y[:, wide + TILE * h : wide + TILE * h + TILE] + k_extra
        vh = y[:, 2 * wide + TILE * h : 2 * wide + TILE * h + TILE] + v_extra
        ka[:, at] = kh.astype(LOW)
        va[:, at] = vh.astype(LOW)
        kt[at, :] = kh.T.astype(LOW)
        vt[at, :] = vh.T.astype(LOW)


def project(info, xs, gain, w_qkv, table, heads, per):
    total = RANKS * xs[0].shape[0]
    rows = xs[0].shape[0] // SPLIT
    width = xs[0].shape[1]
    row_block = lambda w: pl.BlockSpec((2 * rows, w), lambda i, c: (i, 0))
    col_block = lambda w: pl.BlockSpec((w, 2 * rows), lambda i, c: (0, i))
    wide = heads * TILE
    return pl.pallas_call(
        functools.partial(project_kernel, heads, per),
        grid_spec=pltpu.PrefetchScalarGridSpec(
            num_scalar_prefetch=1,
            grid=(RANKS * SPLIT // 2,),
            in_specs=[pl.BlockSpec((rows, width), lambda i, c: (2 * i // RANKS, 0))] * RANKS
            + [
                whole_spec(gain.shape),
                whole_spec(w_qkv.shape),
                pl.BlockSpec(memory_space=pltpu.SMEM),
            ],
            out_specs=[
                row_block(width),
                row_block(wide),
                row_block(wide),
                row_block(wide),
                col_block(wide),
                col_block(wide),
                whole_spec((heads, 3, TILE, TILE)),
            ],
        ),
        out_shape=[
            jax.ShapeDtypeStruct((total, width), LOW),
            jax.ShapeDtypeStruct((total, wide), LOW),
            jax.ShapeDtypeStruct((total, wide), LOW),
            jax.ShapeDtypeStruct((total, wide), LOW),
            jax.ShapeDtypeStruct((wide, total), LOW),
            jax.ShapeDtypeStruct((wide, total), LOW),
            jax.ShapeDtypeStruct((heads, 3, TILE, TILE), FULL),
        ],
        compiler_params=params(),
        name="project",
        cost_estimate=cost(8 * total * width * heads * HEAD),
    )(info, *xs, gain, w_qkv, table)


def near_tiles(first_place, tiles, per, visit):
    count = RANKS * per
    for u in range(tiles):
        here = tile_at(first_place + u, per)
        for d in (-1, 0, 1):
            there = here + d
            valid = jnp.logical_and(there >= 0, there < count)
            place = tile_place(jnp.clip(there, 0, count - 1), per)
            rows = pl.ds(pl.multiple_of(place * TILE, TILE), TILE)
            visit(d + 1, rows, slice(u * TILE, u * TILE + TILE), jnp.where(valid, 1.0, 0.0))


def score_block(h, first_place, per, qa, ka, near, s_ref):
    bq = qa.shape[0]
    at = slice(TILE * h, TILE * h + TILE)
    s_ref[h] = dot_nt(ka[:, at], qa[:, at])

    def add(d, rows, cols, valid):
        s_ref[h, rows, cols] = s_ref[h, rows, cols] + near[h, d] * valid

    near_tiles(first_place, bq // TILE, per, add)


def forward_kernel(heads, per, offset, qa, ka, vt, near, mixed, ot, lse, s_ref):
    bq = qa.shape[0]
    first = (pl.program_id(0) + offset) * (bq // TILE)
    for h in range(heads):
        score_block(h, first, per, qa, ka, near, s_ref)
    parts = []
    for h in range(heads):
        s = s_ref[h]
        top = jnp.max(s, axis=0, keepdims=True)
        p = jnp.exp(s - top).astype(LOW)
        o = dot_nn(vt[TILE * h : TILE * h + TILE, :], p)
        total = o[HEAD : HEAD + 1]
        o = o[:HEAD] * (1.0 / total)
        ot[HEAD * h : HEAD * h + HEAD, :] = o
        lse[h : h + 1, :] = top + jnp.log(total)
        parts.append(o.T)
    mixed[...] = jnp.concatenate(parts, axis=1).astype(LOW)


def attend(qa, ka, vt, near, part, bq, per):
    total, wide = ka.shape
    heads = wide // TILE
    span = total // SPLIT
    steps = span // bq
    offset = part * steps
    full = lambda shape: pl.BlockSpec(shape, lambda i: tuple(0 for _ in shape))
    width = heads * HEAD
    return pl.pallas_call(
        functools.partial(forward_kernel, heads, per, offset),
        grid=(steps,),
        in_specs=[
            pl.BlockSpec((bq, wide), lambda i: (i + offset, 0)),
            full(ka.shape),
            full(vt.shape),
            full(near.shape),
        ],
        out_specs=[
            pl.BlockSpec((bq, width), lambda i: (i, 0)),
            pl.BlockSpec((width, bq), lambda i: (0, i)),
            pl.BlockSpec((8, bq), lambda i: (0, i)),
        ],
        out_shape=[
            jax.ShapeDtypeStruct((span, width), LOW),
            jax.ShapeDtypeStruct((width, span), FULL),
            jax.ShapeDtypeStruct((8, span), FULL),
        ],
        scratch_shapes=[pltpu.VMEM((heads, total, bq), FULL)],
        compiler_params=params(),
        name="attend",
        cost_estimate=cost(20 * heads * span * total * HEAD),
    )(qa, ka, vt, near)


def middle_kernel(
    first, info, x0, x1, x2, x3, c0, c1, c2, c3, m0, m1, m2, m3, w0, w1, w2, w3,
    gain, w_ffn, *refs
):
    given, (f_keep, f_give, d_keep, d_give, resid_out, grads_out, grads) = refs[:-7], refs[-7:]
    step = pl.program_id(0)
    hid = w_ffn.shape[1] // 2

    @pl.when(step == 0)
    def _():
        grads[...] = jnp.zeros_like(grads) if first else given[0][...].astype(FULL)

    attn = dot_nn(m0[...], w0[...]) + dot_nn(m1[...], w1[...])
    attn = attn + dot_nn(m2[...], w2[...]) + dot_nn(m3[...], w3[...])
    resid = pick_block(info[step], (x0, x1, x2, x3)).astype(FULL) + attn
    resid_out[...] = resid
    scale = lax.rsqrt(jnp.mean(resid * resid, axis=-1, keepdims=True) + EPSILON)
    normed = (resid * scale * gain[...]).astype(LOW)
    hidden = dot_nn(normed, w_ffn[:, :hid])
    grad = pick_block(info[step], (c0, c1, c2, c3))
    d_active = dot_nn(grad, w_ffn[:, hid:])
    square = hidden * hidden
    th = jnp.tanh(GELU_A * hidden * (1.0 + GELU_B * square))
    half = 0.5 * (1.0 + th)
    active = (hidden * half).astype(LOW)
    slope = half + 0.5 * hidden * (1.0 - th * th) * (GELU_A * (1.0 + (3.0 * GELU_B) * square))
    d_hidden = (d_active * slope).astype(LOW)
    dn = dot_nt(d_hidden, w_ffn[:, :hid]).astype(LOW)
    ffn = dot_nt(active, w_ffn[:, hid:]).astype(LOW)

    @pl.when(info[step] % 2 == 0)
    def _():
        d_keep[0] = dn
        f_keep[0] = ffn

    @pl.when(info[step] % 2 == 1)
    def _():
        d_give[0] = dn
        f_give[0] = ffn

    grads[:, :hid] += dot_tn(normed, d_hidden)
    grads[:, hid:] += dot_tn(grad, active)

    @pl.when(step == RANKS - 1)
    def _():
        grads_out[...] = grads[...].astype(LOW)


def middle(info, xs, cs, pieces, outs, gain, w_ffn, part, given):
    rows, width = xs[0].shape[0] // SPLIT, xs[0].shape[1]
    narrow = pieces[0].shape[1]
    own_block = pl.BlockSpec((rows, width), lambda i, c: (part, 0))
    piece_block = pl.BlockSpec((rows, narrow), lambda i, c: (i, 0))
    rel_block = pl.BlockSpec((1, rows, width), lambda i, c: (c[i] // 2, 0, 0))
    pair_block = pl.BlockSpec((1, rows, width), lambda i, c: (i // 2, 0, 0))
    extra = () if given is None else (given,)
    two = jax.ShapeDtypeStruct((2, rows, width), LOW)
    return pl.pallas_call(
        functools.partial(middle_kernel, given is None),
        grid_spec=pltpu.PrefetchScalarGridSpec(
            num_scalar_prefetch=1,
            grid=(RANKS,),
            in_specs=[own_block] * (2 * RANKS)
            + [piece_block] * RANKS
            + [whole_spec(outs[0].shape)] * RANKS
            + [whole_spec(v.shape) for v in (gain, w_ffn) + extra],
            out_specs=[
                rel_block,
                rel_block,
                pair_block,
                pair_block,
                pl.BlockSpec((rows, width), lambda i, c: (i, 0)),
                whole_spec(w_ffn.shape),
            ],
            scratch_shapes=[pltpu.VMEM(w_ffn.shape, FULL)],
        ),
        out_shape=[two, two, two, two]
        + [
            jax.ShapeDtypeStruct((RANKS * rows, width), FULL),
            jax.ShapeDtypeStruct(w_ffn.shape, LOW),
        ],
        compiler_params=params(),
        name="middle",
        cost_estimate=cost(20 * RANKS * rows * width * w_ffn.shape[1] // 2),
    )(info, *xs, *cs, *pieces, *outs, gain, w_ffn, *extra)


def backward_kernel(
    per, offset, kc, info, qa, ka, kt, va, sum_mine, sum_other, resid_ref,
    c0, c1, c2, c3, gain, wo, ot, lse, near, *refs
):
    given = refs[:-11]
    dq, dk, dv, d_near, g_out, tiles, s_ref, ds_ref, dk_acc, dv_acc, d_rows = refs[-11:]
    head, step = pl.program_id(0), pl.program_id(1)
    bq = qa.shape[0]
    total = ka.shape[0]
    count = RANKS * per
    first = (step + offset) * (bq // TILE)
    here = pl.ds(pl.multiple_of(step * bq, bq), bq)

    @pl.when(step == 0)
    def _():
        if len(given) > 0:
            dk_acc[...] = given[0][...]
            dv_acc[...] = given[1][...]
            d_near[...] = given[2][...]
            g_out[...] = given[3][...]
        else:
            dk_acc[...] = jnp.zeros_like(dk_acc)
            dv_acc[...] = jnp.zeros_like(dv_acc)
            d_near[...] = jnp.zeros_like(d_near)
            g_out[...] = jnp.zeros_like(g_out)

    @pl.when(head == 0)
    def _():
        even = info[2 * step] % 2 == 0
        mine, other = sum_mine[0], sum_other[0]
        d_norm = jnp.concatenate(
            [jnp.where(even, mine, other), jnp.where(even, other, mine)], axis=0
        ).astype(FULL)
        cot = jnp.concatenate(
            [pick_block(info[2 * step + k], (c0, c1, c2, c3)) for k in range(2)], axis=0
        ).astype(FULL)
        resid = resid_ref[...]
        scale = lax.rsqrt(jnp.mean(resid * resid, axis=-1, keepdims=True) + EPSILON)
        unit = resid * scale
        along = d_norm * gain[...]
        rows = cot + scale * (along - unit * jnp.mean(along * unit, axis=-1, keepdims=True))
        d_rows[here, :] = rows.astype(LOW)

    s_ref[...] = dot_nt(ka[...], qa[...])

    def add(d, rows, cols, valid):
        s_ref[rows, cols] = s_ref[rows, cols] + near[0, d] * valid

    near_tiles(first, bq // TILE, per, add)
    grad = d_rows[here, :]
    do = dot_nt(grad, wo[...]).astype(LOW)
    do_t = dot_nt(wo[...], grad).astype(LOW).astype(FULL)
    o_t = ot[...]
    g_out[...] += dot_nn(o_t.astype(LOW), grad)
    delta = jnp.sum(do_t[:HEAD] * o_t, axis=0, keepdims=True)
    lse_row = lse[pl.ds(head, 1), :]
    dq_t = jnp.zeros((TILE, bq), FULL)
    for c in range(total // kc):
        rows = slice(kc * c, kc * c + kc)
        p = jnp.exp(s_ref[rows, :] - lse_row)
        d_p = dot_nt(va[rows, :], do)
        d_s = (p * (d_p - delta)).astype(LOW)
        ds_ref[rows, :] = d_s
        dv_acc[rows, :] += dot_nn(p.astype(LOW), do)
        dk_acc[rows, :] += dot_nn(d_s, qa[...])
        dq_t += dot_nn(kt[:, rows], d_s)
    lane = lax.broadcasted_iota(jnp.int32, (bq, TILE), 1)
    dq[...] = jnp.where(lane < HEAD, dq_t.T, 0.0).astype(LOW)

    def collect(d, rows, cols, valid):
        d_near[0, d] += ds_ref[rows, cols].astype(FULL) * valid

    near_tiles(first, bq // TILE, per, collect)

    @pl.when(step == pl.num_programs(1) - 1)
    def _():
        if dk.dtype == FULL:
            dk[...] = dk_acc[...]
            dv[...] = dv_acc[...]
        else:
            side = lax.broadcasted_iota(jnp.int32, (total, TILE), 1)
            dk[...] = jnp.where(side < HEAD, dk_acc[...], 0.0).astype(LOW)
            dv[...] = jnp.where(side < HEAD, dv_acc[...], 0.0).astype(LOW)
        sums = [
            jnp.sum(dk_acc[k * TILE : k * TILE + TILE, :], axis=0, keepdims=True)
            for k in range(count)
        ]
        tiles[0] = jnp.concatenate(sums, axis=0)


def attend_back(
    info, qa, ka, kt, va, sums, resid, cs, gain, wo, ot, lse, near, part, kc, per, given
):
    total, wide = ka.shape
    heads = wide // TILE
    model = resid.shape[1]
    rows = total // SPLIT // RANKS
    bq = 2 * rows
    span = total // SPLIT
    steps = span // bq
    offset = part * steps
    last = part == SPLIT - 1
    once = lambda h, i: jnp.where(h == 0, i, steps - 1)
    head_cols = pl.BlockSpec((total, TILE), lambda h, i, c: (0, h))
    near_block = pl.BlockSpec((1, 3, TILE, TILE), lambda h, i, c: (h, 0, 0, 0))
    out_block = pl.BlockSpec((HEAD, model), lambda h, i, c: (h, 0))
    kind = LOW if last else FULL
    full = lambda shape: pl.BlockSpec(shape, lambda h, i, c: tuple(0 for _ in shape))
    return pl.pallas_call(
        functools.partial(backward_kernel, per, offset, kc),
        grid_spec=pltpu.PrefetchScalarGridSpec(
            num_scalar_prefetch=1,
            grid=(heads, steps),
            in_specs=[
                pl.BlockSpec((bq, TILE), lambda h, i, c: (i + offset, h)),
                head_cols,
                pl.BlockSpec((TILE, total), lambda h, i, c: (h, 0)),
                head_cols,
            ]
            + [pl.BlockSpec((1, rows, model), lambda h, i, c: (once(h, i), 0, 0))] * 2
            + [pl.BlockSpec((bq, model), lambda h, i, c: (once(h, i), 0))]
            + [pl.BlockSpec((rows, model), lambda h, i, c: (part, 0))] * RANKS
            + [
                full(gain.shape),
                pl.BlockSpec((TILE, model), lambda h, i, c: (h, 0)),
                pl.BlockSpec((HEAD, bq), lambda h, i, c: (h, i)),
                pl.BlockSpec((8, bq), lambda h, i, c: (0, i)),
                near_block,
            ]
            + ([] if len(given) == 0 else [head_cols, head_cols, near_block, out_block]),
            out_specs=[
                pl.BlockSpec((bq, TILE), lambda h, i, c: (i, h)),
                head_cols,
                head_cols,
                near_block,
                out_block,
                pl.BlockSpec((1, RANKS * per, TILE), lambda h, i, c: (h, 0, 0)),
            ],
            scratch_shapes=[
                pltpu.VMEM((total, bq), FULL),
                pltpu.VMEM((total, bq), LOW),
                pltpu.VMEM((total, TILE), FULL),
                pltpu.VMEM((total, TILE), FULL),
                pltpu.VMEM((span, model), LOW),
            ],
        ),
        out_shape=[
            jax.ShapeDtypeStruct((span, wide), LOW),
            jax.ShapeDtypeStruct((total, wide), kind),
            jax.ShapeDtypeStruct((total, wide), kind),
            jax.ShapeDtypeStruct((heads, 3, TILE, TILE), FULL),
            jax.ShapeDtypeStruct((heads * HEAD, model), FULL),
            jax.ShapeDtypeStruct((heads, RANKS * per, TILE), FULL),
        ],
        compiler_params=params(),
        name="attend_back",
        cost_estimate=cost(40 * heads * span * total * HEAD),
    )(info, qa, ka, kt, va, *sums, resid, *cs, gain, wo, ot, lse, near, *given)


def bucket_kernel(d_near, out):
    heads = d_near.shape[0]
    found = [[jnp.zeros((1, TILE), FULL)] * BUCKETS for _ in range(heads)]
    for d in (-1, 0, 1):
        buckets = near_bucket(d)
        for b in buckets_near(d):
            here = buckets == b
            for h in range(heads):
                found[h][b] = found[h][b] + jnp.sum(
                    jnp.where(here, d_near[h, d + 1], 0.0), axis=0, keepdims=True
                )
    for h in range(heads):
        out[h] = jnp.concatenate(found[h], axis=0)


def bucket_sums(d_near):
    heads = d_near.shape[0]
    return pl.pallas_call(
        bucket_kernel,
        out_shape=jax.ShapeDtypeStruct((heads, BUCKETS, TILE), FULL),
        compiler_params=params(),
        name="bucket_sums",
    )(d_near)


def tail_kernel(info, dq0, dq1, dk, dv, w_ref, keep, give):
    wide = dk.shape[1]
    dq = pick_block(pl.program_id(0), (dq0, dq1))
    out = dot_nn(dq, w_ref[:wide, :]) + dot_nn(dk[...], w_ref[wide : 2 * wide, :])
    out = (out + dot_nn(dv[...], w_ref[2 * wide :, :])).astype(LOW)
    rows = out.shape[0] // RANKS
    even = info[0] % 2 == 0
    low = info[0] // 2 == 0
    parts = [out[k * rows : k * rows + rows] for k in range(RANKS)]
    kept = [jnp.where(even, parts[k], parts[k + 1]) for k in (0, 2)]
    given = [jnp.where(even, parts[k + 1], parts[k]) for k in (0, 2)]
    keep[0], keep[1] = jnp.where(low, kept[0], kept[1]), jnp.where(low, kept[1], kept[0])
    give[0], give[1] = jnp.where(low, given[0], given[1]), jnp.where(low, given[1], given[0])


def tail(info, dqs, dk, dv, w_wide):
    total, wide = dk.shape
    model = w_wide.shape[1]
    span = total // SPLIT
    rows = span // RANKS
    rel_block = pl.BlockSpec((2, rows, model), lambda i, c: (i, 0, 0))
    return pl.pallas_call(
        tail_kernel,
        grid_spec=pltpu.PrefetchScalarGridSpec(
            num_scalar_prefetch=1,
            grid=(SPLIT,),
            in_specs=[
                whole_spec((span, wide)),
                whole_spec((span, wide)),
                pl.BlockSpec((span, wide), lambda i, c: (i, 0)),
                pl.BlockSpec((span, wide), lambda i, c: (i, 0)),
                whole_spec(w_wide.shape),
            ],
            out_specs=[rel_block, rel_block],
        ),
        out_shape=[jax.ShapeDtypeStruct((2 * SPLIT, rows, model), LOW)] * 2,
        compiler_params=params(),
        name="tail",
        cost_estimate=cost(6 * total * wide * model),
    )(info, *dqs, dk, dv, w_wide)


def weights_kernel(steps, dq0, dq1, dk, dv, normed, g_out, extra, out, acc):
    step = pl.program_id(0)

    @pl.when(step == 0)
    def _():
        acc[...] = jnp.zeros_like(acc)

    dq = pick_block(step // (steps // 2), (dq0, dq1))
    acc[...] += dot_tn(jnp.concatenate([dq, dk[...], dv[...]], axis=1), normed[...])

    @pl.when(step == steps - 1)
    def _():
        count = acc.shape[0] // TILE
        for j in range(count):
            out[j * HEAD : j * HEAD + HEAD, :] = acc[j * TILE : j * TILE + HEAD, :].astype(LOW)
        base = count * HEAD
        out[base : base + g_out.shape[0], :] = g_out[...].astype(LOW)
        out[base + g_out.shape[0] :, :] = extra[...]


def weights(dqs, dk, dv, normed, g_out, extra):
    total, wide = dk.shape
    model = normed.shape[1]
    steps = 4
    rows = total // steps
    half = steps // 2
    full = lambda shape: pl.BlockSpec(shape, lambda i: tuple(0 for _ in shape))
    block = lambda w: pl.BlockSpec((rows, w), lambda i: (i, 0))
    out_rows = 3 * wide * HEAD // TILE + g_out.shape[0] + extra.shape[0]
    return pl.pallas_call(
        functools.partial(weights_kernel, steps),
        grid=(steps,),
        in_specs=[
            pl.BlockSpec((rows, wide), lambda i: (jnp.minimum(i, half - 1), 0)),
            pl.BlockSpec((rows, wide), lambda i: (jnp.maximum(i - half, 0), 0)),
            block(wide),
            block(wide),
            block(model),
            full(g_out.shape),
            full(extra.shape),
        ],
        out_specs=full((out_rows, model)),
        out_shape=jax.ShapeDtypeStruct((out_rows, model), LOW),
        scratch_shapes=[pltpu.VMEM((3 * wide, model), FULL)],
        compiler_params=params(),
        name="weights",
        cost_estimate=cost(6 * total * wide * model),
    )(*dqs, dk, dv, normed, g_out, extra)


def together(*values):
    return lax.optimization_barrier(values)


def after(value, *given):
    return lax.optimization_barrier((value,) + given)[0]


def swap_seq(value, bit):
    return lax.ppermute(value, "seq", [(i, i ^ bit) for i in range(RANKS)])


def regroup(value, skip):
    pairs = []
    for s in range(RANKS):
        for t in range(RANKS):
            if t != skip and MIX[s] != 0:
                pairs.append((s * RANKS + t, s * RANKS + (t ^ MIX[s])))
    moved = lax.ppermute(value, ("seq", "tensor"), pairs)
    return jnp.where(lax.axis_index("seq") == MIX.index(0), value, moved)


def along_tensor(value, pairs):
    return lax.ppermute(value, "tensor", pairs)


def step_one(own):
    return along_tensor(own, [(0, 1), (2, 3)]), along_tensor(own, [(3, 2), (2, 1)])


def step_two(moved):
    return along_tensor(moved[0], [(1, 2)]), along_tensor(moved[1], [(2, 1), (1, 0)])


def step_three(moved):
    return along_tensor(moved[0], [(2, 3)]), along_tensor(moved[1], [(1, 0)])


HOME = (0, 0, 1, 2)
PLACES = (
    ((None, 0, None, 1), (None, 1, 2, None)),
    ((None, None, 0, None), (1, 2, None, None)),
    ((None, None, None, 0), (2, None, None, None)),
)


def by_rank(values, rank):
    out = values[0]
    for index in range(1, len(values)):
        out = jnp.where(rank == index, values[index], out)
    return out


def keep_step(held, own, moved, places, rank):
    for value, place in zip(moved, places):
        got = by_rank([p is not None for p in place], rank)
        at = by_rank([HOME[k] if p is None else p for k, p in enumerate(place)], rank)
        value = jnp.where(got, value, own)
        held = lax.dynamic_update_slice(held, value[None], (at, 0, 0))
    return held


def swap_dp(value):
    return lax.ppermute(value, "dp", [(0, 1), (1, 0)])


def join_dp(halves, axis):
    if len(halves) == 1:
        return lax.all_gather(halves[0], "dp", axis=axis, tiled=True)
    value, other = halves
    swap = lax.axis_index("dp") == 1
    return jnp.concatenate(
        [jnp.where(swap, other, value), jnp.where(swap, value, other)], axis=axis
    )


def gather_dp(value, axis):
    if lax.axis_size("dp") != 2:
        return join_dp((value,), axis)
    return join_dp((value, swap_dp(value)), axis)


def scatter_dp(value, axis):
    if lax.axis_size("dp") != 2:
        return lax.psum_scatter(value, "dp", scatter_dimension=axis, tiled=True).astype(LOW)
    size = value.shape[axis] // 2
    mine = lax.axis_index("dp")
    keep = lax.dynamic_slice_in_dim(value, mine * size, size, axis)
    give = lax.dynamic_slice_in_dim(value, (1 - mine) * size, size, axis)
    return (keep.astype(FULL) + swap_dp(give.astype(LOW)).astype(FULL)).astype(LOW)


def sum_pair(value, bit):
    return value.astype(FULL) + swap_seq(value, bit).astype(FULL)


def normalize(values):
    scale = lax.rsqrt(jnp.mean(values * values, axis=-1, keepdims=True) + EPSILON)
    return values * scale, scale


def norm_back(grad, unit, scale, gain):
    along = grad * gain
    return scale * (along - unit * jnp.mean(along * unit, axis=-1, keepdims=True))


def body(
    inputs, lengths, gain_attn, w_query, w_key, w_value, w_out, bias_table,
    gain_ffn, w_in, w_down, cotangent,
):
    slots, rows_here, model = inputs.shape
    assert lax.axis_size("seq") == RANKS and lax.axis_size("tensor") == RANKS and slots == 3
    total = RANKS * rows_here
    per = rows_here // TILE
    narrow = w_query.shape[1]
    heads = narrow // HEAD
    hid = w_in.shape[1]
    rank = lax.axis_index("tensor")
    chunk = lax.axis_index("seq")
    mine = lax.axis_index("dp")
    slot = jnp.where(rank == 0, 0, rank - 1)
    length = lax.dynamic_index_in_dim(lengths, slot, 0, keepdims=False)
    order = jnp.bitwise_xor(chunk, jnp.arange(RANKS, dtype=jnp.int32)).astype(jnp.int32)
    info = jnp.concatenate([order, length[None], jnp.zeros((3,), jnp.int32)])
    rows_part = rows_here // SPLIT
    size = gain_attn.shape[0]
    cut = lambda v: v.reshape(SPLIT, rows_part, model)

    x_own = lax.dynamic_index_in_dim(inputs, slot, 0, keepdims=False)
    x_far = swap_seq(x_own, 2)
    x_near = swap_seq(x_own, 1)

    flat = bias_table.reshape(-1)
    small = jnp.stack(
        [gain_attn, gain_ffn, jnp.pad(flat, (0, size - flat.shape[0]))]
        + [jnp.zeros((size,), LOW)] * (EXTRA - 3)
    )
    w_first = after(w_query, x_own)
    pack = jnp.concatenate([w_first.T, w_key.T, w_value.T, w_out, small], axis=0)
    pack = regroup(pack, None)
    w_all = gather_dp(pack, 1)
    main = 4 * narrow
    w_wide = jnp.pad(
        w_all[: 3 * narrow].reshape(3 * heads, HEAD, model), ((0, 0), (0, TILE - HEAD), (0, 0))
    ).reshape(3 * heads * TILE, model)
    gain_one = w_all[main : main + 1].astype(FULL)
    gain_two = w_all[main + 1 : main + 2].astype(FULL)
    table = w_all[main + 2].reshape(-1, size)[:, : flat.shape[0]]
    table = table.reshape(BUCKETS, heads).astype(FULL)
    xs = [x_own, x_near, x_far, swap_seq(x_far, 1)]

    position = chunk * rows_here + jnp.arange(rows_here, dtype=jnp.int32)
    live = jnp.logical_and(position < length, rank != IDLE)
    c_own = lax.dynamic_index_in_dim(cotangent, slot, 0, keepdims=False)
    c_own = jnp.where(live[:, None], c_own, jnp.zeros((), LOW))
    ffn_pack = regroup(after(jnp.concatenate([w_in, w_down.T], axis=1), pack), None)
    c_first = after(c_own, x_far)
    c_far = swap_seq(c_first, 2)

    normed, qa, ka, va, kt, vt, near = project(info, xs, gain_one, w_wide, table, heads, per)

    normed, c_far, ffn_pack = together(normed, c_far, ffn_pack)
    qa, ka, vt, _ = together(qa, ka, vt, normed)
    out_mine = w_all[3 * narrow : main]
    out_near, out_far = swap_seq(out_mine, 1), swap_seq(out_mine, 2)
    ffn_halves = (ffn_pack, swap_dp(ffn_pack)) if lax.axis_size("dp") == 2 else (ffn_pack,)
    cs = [c_own, swap_seq(c_first, 1), c_far, swap_seq(c_far, 1)]
    out_wide = jnp.pad(
        out_mine.reshape(heads, HEAD, model), ((0, 0), (0, TILE - HEAD), (0, 0))
    ).reshape(heads * TILE, model)

    bq = min(512, total // SPLIT)
    attended = [attend(qa, ka, vt, near, 0, bq, per)]
    attended[0], cs, out_far = together(attended[0], cs, out_far)
    outs = [out_mine, out_near, out_far, swap_seq(out_far, 1)]
    mixed = attended[0][0]
    pieces = [[mixed] + [swap_seq(mixed, bit) for bit in (1, 2, 3)]]

    attended.append(attend(after(qa, mixed), ka, vt, near, 1, bq, per))
    attended[1], pieces[0], outs, ffn_halves = together(
        attended[1], pieces[0], outs, ffn_halves
    )
    w_ffn = join_dp(ffn_halves, 0)
    mixed = attended[1][0]
    pieces.append([mixed] + [swap_seq(mixed, bit) for bit in (1, 2, 3)])

    def chip_sum(mid, core):
        return (mid[2].astype(FULL) + core.astype(FULL)).astype(LOW)

    def whole_sum(part):
        both = chip[part].astype(FULL) + chip_far[part].astype(FULL)
        both = both.astype(LOW)
        return both, swap_seq(both, 1)

    def out_rows(part):
        resid = lax.dynamic_index_in_dim(
            mids[part][4].reshape(RANKS, rows_part, model), chunk, 0, keepdims=False
        )
        return (resid + (ffn[part][0] + ffn_far[part].astype(FULL))).astype(LOW)

    mids, chip, chip_far = [], [], []
    for part in range(SPLIT):
        mid = middle(
            info, xs, cs, pieces[part], outs, gain_two, w_ffn, part,
            None if part == 0 else mids[0][5],
        )
        if part == 0:
            mid, pieces[1] = together(mid, pieces[1])
        else:
            mid, chip_far[0] = together(mid, chip_far[0])
        mids.append(mid)
        chip.append(chip_sum(mid, swap_seq(mid[3], 1)))
        chip_far.append(swap_seq(chip[part], 2))
        if part == 0:
            pieces[1] = after(pieces[1], chip[0])

    sums = [whole_sum(0)]
    ffn = [after(mid[:2], chip[1]) for mid in mids]
    ffn = [f[0].astype(FULL) + swap_seq(f[1], 1).astype(FULL) for f in ffn]
    ffn_far = jnp.stack([f[1].astype(LOW) for f in ffn])
    g_ffn = after(mids[1][5], chip[1])
    g_ffn = lax.psum_scatter(g_ffn, "dp", scatter_dimension=0, tiled=True)
    sums[0] = after(sums[0], ffn_far)
    ffn_far = swap_seq(ffn_far, 2)

    args = (gain_two, out_wide)
    back = [
        attend_back(
            info, qa, ka, kt, va, sums[0], mids[0][4], cs, *args, *attended[0][1:], near, 0,
            512, per, (),
        )
    ]
    back[0], chip_far[1], ffn_far, g_ffn = together(back[0], chip_far[1], ffn_far, g_ffn)
    sums.append(whole_sum(1))
    out_own = jnp.concatenate([out_rows(part) for part in range(SPLIT)], axis=0)
    out_own = after(out_own, sums[1][0])
    g_ffn = regroup(g_ffn, IDLE)
    given = back[0][1:5]
    sums[1] = after(sums[1], out_own)
    back.append(
        attend_back(
            info, qa, ka, kt, va, sums[1], mids[1][4], cs, *args, *attended[1][1:], near, 1,
            512, per, given,
        )
    )
    back[1], g_ffn = together(back[1], g_ffn)
    outputs = lax.all_gather(after(out_own, g_ffn), "tensor")
    g_core = swap_seq(g_ffn, 1)
    dk, dv, d_near = back[1][1:4]
    resids = [
        lax.dynamic_index_in_dim(
            mid[4].reshape(RANKS, rows_part, model), chunk, 0, keepdims=False
        )
        for mid in mids
    ]

    dqs = [b[0] for b in back]
    keep, give = tail(info, dqs, dk, dv, w_wide)
    core = swap_seq(give, 1)
    found = bucket_sums(after(d_near, give))
    found, core, g_core = together(found, core, g_core)
    far_low = (keep[1::2].astype(FULL) + core[1::2].astype(FULL)).astype(LOW)
    far = swap_seq(far_low, 2)
    dqs, dk, dv, found, g_core = after((dqs, dk, dv, found, g_core), far_low)
    near_sum = jnp.sum(found, axis=2).T
    tile_sum = back[1][5][:, :, HEAD : HEAD + RANKS * per]
    tiles = tile_at(jnp.arange(RANKS * per), per)
    left = tiles[:, None] < tiles[None, :] - 1
    right = tiles[:, None] > tiles[None, :] + 1
    left_sum = jnp.sum(jnp.where(left, tile_sum, 0.0), axis=(1, 2))
    right_sum = jnp.sum(jnp.where(right, tile_sum, 0.0), axis=(1, 2))
    spot = jnp.arange(BUCKETS)[:, None]
    d_table = near_sum + jnp.where(spot == BUCKETS // 2 - 1, left_sum[None], 0.0)
    d_table = d_table + jnp.where(spot == BUCKETS - 1, right_sum[None], 0.0)
    d_table = d_table.reshape(model // size, flat.shape[0])
    d_table = jnp.pad(d_table, ((0, 0), (0, size - flat.shape[0]))).reshape(1, model)
    extra = jnp.concatenate([d_table, jnp.zeros((EXTRA - 1, model), FULL)], axis=0)
    g_all = weights(dqs, dk, dv, normed, back[1][4], extra.astype(LOW))
    g_all, far = together(g_all, far)
    x_parts, c_parts = cut(x_own).astype(FULL), cut(c_own).astype(FULL)
    own, gain_attn_part, gain_ffn_part = [], 0.0, 0.0
    for part in range(SPLIT):
        total_two = lax.dynamic_index_in_dim(sums[part][0], chunk // 2, 0, keepdims=False)
        total_two = total_two.astype(FULL)
        unit_two, scale_two = normalize(resids[part])
        gain_ffn_part = gain_ffn_part + jnp.sum(total_two * unit_two, axis=0)
        d_resid = c_parts[part] + norm_back(total_two, unit_two, scale_two, gain_two)
        unit, scale = normalize(x_parts[part])
        grad = keep[2 * part].astype(FULL) + core[2 * part].astype(FULL)
        grad = grad + far[part].astype(FULL)
        gain_attn_part = gain_attn_part + jnp.sum(grad * unit, axis=0)
        own.append((d_resid + norm_back(grad, unit, scale, gain_one)).astype(LOW))
    own = jnp.concatenate(own, axis=0)
    gains = jnp.stack([gain_attn_part, gain_ffn_part])
    g_ffn = (g_ffn.astype(FULL) + g_core.astype(FULL)).astype(LOW)
    g_all, g_ffn, gains = after((g_all, g_ffn, gains), own)

    held = jnp.zeros((slots, rows_here, model), LOW)
    home = by_rank(HOME, rank)
    held = lax.dynamic_update_slice(held, own[None], (home, 0, 0))
    one = step_one(own)
    gains = sum_pair(sum_pair(gains, 1), 2)
    g_all = scatter_dp(g_all, 1)
    g_far = swap_seq(after(g_ffn, gains), 2)
    one, g_all, gains, outputs = together(one, g_all, gains, outputs)

    two = step_two(one)
    held = keep_step(held, own, one, PLACES[0], rank)
    own = jnp.where(rank == IDLE, one[0], own)
    g_all = regroup(g_all, IDLE)
    gains = gains + swap_dp(gains) if lax.axis_size("dp") == 2 else lax.psum(gains, "dp")
    gains = gains + along_tensor(gains, [(t, t ^ 1) for t in range(RANKS)])
    g_ffn = g_ffn.astype(FULL) + g_far.astype(FULL)
    g_all = sum_pair(g_all, 1).astype(LOW)
    outputs = jnp.stack([outputs[0], outputs[2], outputs[3]])
    two, g_all, gains, held, g_ffn, outputs = together(two, g_all, gains, held, g_ffn, outputs)

    three = step_three(two)
    held = keep_step(held, own, two, PLACES[1], rank)
    g_all = sum_pair(g_all, 2)
    gains = gains + along_tensor(gains, [(t, t ^ 2) for t in range(RANKS)])
    grad_in, grad_down = g_ffn[:, :hid], g_ffn[:, hid:].T
    three, g_all, gains, held, grad_in, grad_down, outputs = together(
        three, g_all, gains, held, grad_in, grad_down, outputs
    )
    grad_inputs = keep_step(held, own, three, PLACES[2], rank)
    gains = lax.dynamic_slice_in_dim(gains, mine * size, size, 1)
    grad_gain_attn, grad_gain_ffn = gains[0], gains[1]
    grad_table = g_all[main, : flat.shape[0]].reshape(bias_table.shape)
    return (
        outputs,
        grad_inputs,
        grad_gain_attn,
        g_all[:narrow].T,
        g_all[narrow : 2 * narrow].T,
        g_all[2 * narrow : 3 * narrow].T,
        g_all[3 * narrow : main],
        grad_table,
        grad_gain_ffn,
        grad_in,
        grad_down,
    )


def solution(mesh):
    in_specs = (
        P("dp", "seq", None),
        P("dp"),
        P("dp"),
        P("dp", "tensor"),
        P("dp", "tensor"),
        P("dp", "tensor"),
        P("tensor", "dp"),
        P("dp", "tensor"),
        P("dp"),
        P("dp", "tensor"),
        P("tensor", "dp"),
        P("dp", "seq", None),
    )
    out_specs = (
        P("dp", "seq", None),
        P("dp", "seq", None),
        P("dp"),
        P("dp", "tensor"),
        P("dp", "tensor"),
        P("dp", "tensor"),
        P("tensor", "dp"),
        P("dp", "tensor"),
        P("dp"),
        P("dp", "tensor"),
        P("tensor", "dp"),
    )
    return jax.shard_map(body, mesh=mesh, in_specs=in_specs, out_specs=out_specs, check_vma=False)
```

```python
import functools

import jax
import jax.numpy as jnp
from jax import lax
from jax.experimental import pallas as pl
from jax.experimental.pallas import tpu as pltpu
from jax.sharding import PartitionSpec as P

HEAD = 64
BUCKETS = 32
EPSILON = 1e-06
LIMITS = (12, 16, 23, 32, 46, 64, 91)
LOW = jnp.bfloat16
FULL = jnp.float32
TILE = 128
RANKS = 4
MIX = (0, 2, 1, 3)
IDLE = 1
SPLIT = 2
EXTRA = 32
SHORTEN = 64
GELU_A = 0.7978845608028654
GELU_B = 0.044715
KERNEL_MEMORY = 60 * 1024 * 1024


def bucket_of(relative):
    sign_part = jnp.where(relative > 0, 16, 0).astype(jnp.int32)
    distance = jnp.abs(relative)
    far_part = jnp.full(distance.shape, 8, jnp.int32)
    for limit in LIMITS:
        far_part = far_part + (distance >= limit).astype(jnp.int32)
    return sign_part + jnp.where(distance < 8, distance, far_part)


def dot_nn(left, right):
    return lax.dot_general(left, right, (((1,), (0,)), ((), ())), preferred_element_type=FULL)


def dot_nt(left, right):
    return lax.dot_general(left, right, (((1,), (1,)), ((), ())), preferred_element_type=FULL)


def dot_tn(left, right):
    return lax.dot_general(left, right, (((0,), (0,)), ((), ())), preferred_element_type=FULL)


def tile_place(tile, per):
    sub = per // SPLIT
    return ((tile % per) // sub) * (RANKS * sub) + (tile // per) * sub + tile % sub


def tile_at(place, per):
    sub = per // SPLIT
    return ((place // sub) % RANKS) * per + (place // (RANKS * sub)) * sub + place % sub


def cost(flops):
    return pl.CostEstimate(flops=flops // SHORTEN, bytes_accessed=0, transcendentals=0)


def params():
    return pltpu.CompilerParams(vmem_limit_bytes=KERNEL_MEMORY)


def whole_spec(shape):
    return pl.BlockSpec(shape, lambda i, c: tuple(0 for _ in shape))


def near_bucket(d):
    key = lax.broadcasted_iota(jnp.int32, (TILE, TILE), 0)
    query = lax.broadcasted_iota(jnp.int32, (TILE, TILE), 1)
    return bucket_of(TILE * d + key - query)


def buckets_near(d):
    half = BUCKETS // 2
    if d < 0:
        return range(half)
    return range(half, BUCKETS) if d > 0 else range(BUCKETS)


def pick_block(index, refs):
    value = refs[0][...]
    for k in range(1, len(refs)):
        value = jnp.where(index == k, refs[k][...], value)
    return value


def pick_pair(info, chunk, refs):
    return jnp.concatenate([pick_block(info[chunk + k], refs) for k in range(2)], axis=0)


def project_kernel(
    heads, per, info, x0, x1, x2, x3, gain_ref, w_ref, table, normed, qa, ka, va, kt, vt, near
):
    step = pl.program_id(0)

    @pl.when(step == 0)
    def _():
        for d in (-1, 0, 1):
            buckets = near_bucket(d)
            for h in range(heads):
                tile = jnp.zeros((TILE, TILE), FULL)
                for b in buckets_near(d):
                    tile = jnp.where(buckets == b, table[b, h], tile)
                near[h, d + 1] = tile

    rows = 2 * x0.shape[0]
    x = pick_pair(info, (2 * step) % RANKS, (x0, x1, x2, x3)).astype(FULL)
    scale = lax.rsqrt(jnp.mean(x * x, axis=-1, keepdims=True) + EPSILON)
    xn = (x * scale * gain_ref[...]).astype(LOW)
    normed[...] = xn
    y = dot_nt(xn, w_ref[...])
    row = lax.broadcasted_iota(jnp.int32, (rows, TILE), 0)
    lane = lax.broadcasted_iota(jnp.int32, (rows, TILE), 1) - HEAD
    place = step * (rows // TILE) + row // TILE
    count = RANKS * per
    is_tile = jnp.logical_and(lane >= 0, lane < count)
    here = tile_at(place, per)
    there = tile_at(jnp.where(is_tile, lane, 0), per)
    position = here * TILE + row % TILE
    q_extra = jnp.where(jnp.logical_or(lane == place, lane == count), 1.0, 0.0)
    v_extra = jnp.where(lane == 0, 1.0, 0.0)
    dead = jnp.where(jnp.logical_and(lane == count, position >= info[RANKS]), -1e30, 0.0)
    left = jnp.logical_and(is_tile, here < there - 1)
    right = jnp.logical_and(is_tile, here > there + 1)
    wide = heads * TILE
    for h in range(heads):
        before, behind = table[BUCKETS // 2 - 1, h], table[BUCKETS - 1, h]
        k_extra = jnp.where(left, before, jnp.where(right, behind, dead))
        at = slice(TILE * h, TILE * h + TILE)
        qa[:, at] = (y[:, at] + q_extra).astype(LOW)
        kh = y[:, wide + TILE * h : wide + TILE * h + TILE] + k_extra
        vh = y[:, 2 * wide + TILE * h : 2 * wide + TILE * h + TILE] + v_extra
        ka[:, at] = kh.astype(LOW)
        va[:, at] = vh.astype(LOW)
        kt[at, :] = kh.T.astype(LOW)
        vt[at, :] = vh.T.astype(LOW)


def project(info, xs, gain, w_qkv, table, heads, per):
    total = RANKS * xs[0].shape[0]
    rows = xs[0].shape[0] // SPLIT
    width = xs[0].shape[1]
    row_block = lambda w: pl.BlockSpec((2 * rows, w), lambda i, c: (i, 0))
    col_block = lambda w: pl.BlockSpec((w, 2 * rows), lambda i, c: (0, i))
    wide = heads * TILE
    return pl.pallas_call(
        functools.partial(project_kernel, heads, per),
        grid_spec=pltpu.PrefetchScalarGridSpec(
            num_scalar_prefetch=1,
            grid=(RANKS * SPLIT // 2,),
            in_specs=[pl.BlockSpec((rows, width), lambda i, c: (2 * i // RANKS, 0))] * RANKS
            + [
                whole_spec(gain.shape),
                whole_spec(w_qkv.shape),
                pl.BlockSpec(memory_space=pltpu.SMEM),
            ],
            out_specs=[
                row_block(width),
                row_block(wide),
                row_block(wide),
                row_block(wide),
                col_block(wide),
                col_block(wide),
                whole_spec((heads, 3, TILE, TILE)),
            ],
        ),
        out_shape=[
            jax.ShapeDtypeStruct((total, width), LOW),
            jax.ShapeDtypeStruct((total, wide), LOW),
            jax.ShapeDtypeStruct((total, wide), LOW),
            jax.ShapeDtypeStruct((total, wide), LOW),
            jax.ShapeDtypeStruct((wide, total), LOW),
            jax.ShapeDtypeStruct((wide, total), LOW),
            jax.ShapeDtypeStruct((heads, 3, TILE, TILE), FULL),
        ],
        compiler_params=params(),
        name="project",
        cost_estimate=cost(8 * total * width * heads * HEAD),
    )(info, *xs, gain, w_qkv, table)


def near_tiles(first_place, tiles, per, visit):
    count = RANKS * per
    for u in range(tiles):
        here = tile_at(first_place + u, per)
        for d in (-1, 0, 1):
            there = here + d
            valid = jnp.logical_and(there >= 0, there < count)
            place = tile_place(jnp.clip(there, 0, count - 1), per)
            rows = pl.ds(pl.multiple_of(place * TILE, TILE), TILE)
            visit(d + 1, rows, slice(u * TILE, u * TILE + TILE), jnp.where(valid, 1.0, 0.0))


def score_block(h, first_place, per, qa, ka, near, s_ref):
    bq = qa.shape[0]
    at = slice(TILE * h, TILE * h + TILE)
    s_ref[h] = dot_nt(ka[:, at], qa[:, at])

    def add(d, rows, cols, valid):
        s_ref[h, rows, cols] = s_ref[h, rows, cols] + near[h, d] * valid

    near_tiles(first_place, bq // TILE, per, add)


def forward_kernel(heads, per, offset, qa, ka, vt, near, mixed, ot, lse, s_ref):
    bq = qa.shape[0]
    first = (pl.program_id(0) + offset) * (bq // TILE)
    for h in range(heads):
        score_block(h, first, per, qa, ka, near, s_ref)
    parts = []
    for h in range(heads):
        s = s_ref[h]
        top = jnp.max(s, axis=0, keepdims=True)
        p = jnp.exp(s - top).astype(LOW)
        o = dot_nn(vt[TILE * h : TILE * h + TILE, :], p)
        total = o[HEAD : HEAD + 1]
        o = o[:HEAD] * (1.0 / total)
        ot[HEAD * h : HEAD * h + HEAD, :] = o
        lse[h : h + 1, :] = top + jnp.log(total)
        parts.append(o.T)
    mixed[...] = jnp.concatenate(parts, axis=1).astype(LOW)


def attend(qa, ka, vt, near, part, bq, per):
    total, wide = ka.shape
    heads = wide // TILE
    span = total // SPLIT
    steps = span // bq
    offset = part * steps
    full = lambda shape: pl.BlockSpec(shape, lambda i: tuple(0 for _ in shape))
    width = heads * HEAD
    return pl.pallas_call(
        functools.partial(forward_kernel, heads, per, offset),
        grid=(steps,),
        in_specs=[
            pl.BlockSpec((bq, wide), lambda i: (i + offset, 0)),
            full(ka.shape),
            full(vt.shape),
            full(near.shape),
        ],
        out_specs=[
            pl.BlockSpec((bq, width), lambda i: (i, 0)),
            pl.BlockSpec((width, bq), lambda i: (0, i)),
            pl.BlockSpec((8, bq), lambda i: (0, i)),
        ],
        out_shape=[
            jax.ShapeDtypeStruct((span, width), LOW),
            jax.ShapeDtypeStruct((width, span), FULL),
            jax.ShapeDtypeStruct((8, span), FULL),
        ],
        scratch_shapes=[pltpu.VMEM((heads, total, bq), FULL)],
        compiler_params=params(),
        name="attend",
        cost_estimate=cost(20 * heads * span * total * HEAD),
    )(qa, ka, vt, near)


def middle_kernel(
    first, info, x0, x1, x2, x3, c0, c1, c2, c3, m0, m1, m2, m3, w0, w1, w2, w3,
    gain, w_ffn, *refs
):
    given, (f_keep, f_give, d_keep, d_give, resid_out, grads_out, grads) = refs[:-7], refs[-7:]
    step = pl.program_id(0)
    hid = w_ffn.shape[1] // 2

    @pl.when(step == 0)
    def _():
        grads[...] = jnp.zeros_like(grads) if first else given[0][...].astype(FULL)

    attn = dot_nn(m0[...], w0[...]) + dot_nn(m1[...], w1[...])
    attn = attn + dot_nn(m2[...], w2[...]) + dot_nn(m3[...], w3[...])
    resid = pick_block(info[step], (x0, x1, x2, x3)).astype(FULL) + attn
    resid_out[...] = resid
    scale = lax.rsqrt(jnp.mean(resid * resid, axis=-1, keepdims=True) + EPSILON)
    normed = (resid * scale * gain[...]).astype(LOW)
    hidden = dot_nn(normed, w_ffn[:, :hid])
    grad = pick_block(info[step], (c0, c1, c2, c3))
    d_active = dot_nn(grad, w_ffn[:, hid:])
    square = hidden * hidden
    th = jnp.tanh(GELU_A * hidden * (1.0 + GELU_B * square))
    half = 0.5 * (1.0 + th)
    active = (hidden * half).astype(LOW)
    slope = half + 0.5 * hidden * (1.0 - th * th) * (GELU_A * (1.0 + (3.0 * GELU_B) * square))
    d_hidden = (d_active * slope).astype(LOW)
    dn = dot_nt(d_hidden, w_ffn[:, :hid]).astype(LOW)
    ffn = dot_nt(active, w_ffn[:, hid:]).astype(LOW)

    @pl.when(info[step] % 2 == 0)
    def _():
        d_keep[0] = dn
        f_keep[0] = ffn

    @pl.when(info[step] % 2 == 1)
    def _():
        d_give[0] = dn
        f_give[0] = ffn

    grads[:, :hid] += dot_tn(normed, d_hidden)
    grads[:, hid:] += dot_tn(grad, active)

    @pl.when(step == RANKS - 1)
    def _():
        grads_out[...] = grads[...].astype(LOW)


def middle(info, xs, cs, pieces, outs, gain, w_ffn, part, given):
    rows, width = xs[0].shape[0] // SPLIT, xs[0].shape[1]
    narrow = pieces[0].shape[1]
    own_block = pl.BlockSpec((rows, width), lambda i, c: (part, 0))
    piece_block = pl.BlockSpec((rows, narrow), lambda i, c: (i, 0))
    rel_block = pl.BlockSpec((1, rows, width), lambda i, c: (c[i] // 2, 0, 0))
    pair_block = pl.BlockSpec((1, rows, width), lambda i, c: (i // 2, 0, 0))
    extra = () if given is None else (given,)
    two = jax.ShapeDtypeStruct((2, rows, width), LOW)
    return pl.pallas_call(
        functools.partial(middle_kernel, given is None),
        grid_spec=pltpu.PrefetchScalarGridSpec(
            num_scalar_prefetch=1,
            grid=(RANKS,),
            in_specs=[own_block] * (2 * RANKS)
            + [piece_block] * RANKS
            + [whole_spec(outs[0].shape)] * RANKS
            + [whole_spec(v.shape) for v in (gain, w_ffn) + extra],
            out_specs=[
                rel_block,
                rel_block,
                pair_block,
                pair_block,
                pl.BlockSpec((rows, width), lambda i, c: (i, 0)),
                whole_spec(w_ffn.shape),
            ],
            scratch_shapes=[pltpu.VMEM(w_ffn.shape, FULL)],
        ),
        out_shape=[two, two, two, two]
        + [
            jax.ShapeDtypeStruct((RANKS * rows, width), FULL),
            jax.ShapeDtypeStruct(w_ffn.shape, LOW),
        ],
        compiler_params=params(),
        name="middle",
        cost_estimate=cost(20 * RANKS * rows * width * w_ffn.shape[1] // 2),
    )(info, *xs, *cs, *pieces, *outs, gain, w_ffn, *extra)


def backward_kernel(
    per, offset, kc, info, qa, ka, kt, va, sum_mine, sum_other, resid_ref,
    c0, c1, c2, c3, gain, wo, ot, lse, near, *refs
):
    given = refs[:-11]
    dq, dk, dv, d_near, g_out, tiles, s_ref, ds_ref, dk_acc, dv_acc, d_rows = refs[-11:]
    head, step = pl.program_id(0), pl.program_id(1)
    bq = qa.shape[0]
    total = ka.shape[0]
    count = RANKS * per
    first = (step + offset) * (bq // TILE)
    here = pl.ds(pl.multiple_of(step * bq, bq), bq)

    @pl.when(step == 0)
    def _():
        if len(given) > 0:
            dk_acc[...] = given[0][...]
            dv_acc[...] = given[1][...]
            d_near[...] = given[2][...]
            g_out[...] = given[3][...]
        else:
            dk_acc[...] = jnp.zeros_like(dk_acc)
            dv_acc[...] = jnp.zeros_like(dv_acc)
            d_near[...] = jnp.zeros_like(d_near)
            g_out[...] = jnp.zeros_like(g_out)

    @pl.when(head == 0)
    def _():
        even = info[2 * step] % 2 == 0
        mine, other = sum_mine[0], sum_other[0]
        d_norm = jnp.concatenate(
            [jnp.where(even, mine, other), jnp.where(even, other, mine)], axis=0
        ).astype(FULL)
        cot = jnp.concatenate(
            [pick_block(info[2 * step + k], (c0, c1, c2, c3)) for k in range(2)], axis=0
        ).astype(FULL)
        resid = resid_ref[...]
        scale = lax.rsqrt(jnp.mean(resid * resid, axis=-1, keepdims=True) + EPSILON)
        unit = resid * scale
        along = d_norm * gain[...]
        rows = cot + scale * (along - unit * jnp.mean(along * unit, axis=-1, keepdims=True))
        d_rows[here, :] = rows.astype(LOW)

    s_ref[...] = dot_nt(ka[...], qa[...])

    def add(d, rows, cols, valid):
        s_ref[rows, cols] = s_ref[rows, cols] + near[0, d] * valid

    near_tiles(first, bq // TILE, per, add)
    grad = d_rows[here, :]
    do = dot_nt(grad, wo[...]).astype(LOW)
    do_t = dot_nt(wo[...], grad).astype(LOW).astype(FULL)
    o_t = ot[...]
    g_out[...] += dot_nn(o_t.astype(LOW), grad)
    delta = jnp.sum(do_t[:HEAD] * o_t, axis=0, keepdims=True)
    lse_row = lse[pl.ds(head, 1), :]
    dq_t = jnp.zeros((TILE, bq), FULL)
    for c in range(total // kc):
        rows = slice(kc * c, kc * c + kc)
        p = jnp.exp(s_ref[rows, :] - lse_row)
        d_p = dot_nt(va[rows, :], do)
        d_s = (p * (d_p - delta)).astype(LOW)
        ds_ref[rows, :] = d_s
        dv_acc[rows, :] += dot_nn(p.astype(LOW), do)
        dk_acc[rows, :] += dot_nn(d_s, qa[...])
        dq_t += dot_nn(kt[:, rows], d_s)
    lane = lax.broadcasted_iota(jnp.int32, (bq, TILE), 1)
    dq[...] = jnp.where(lane < HEAD, dq_t.T, 0.0).astype(LOW)

    def collect(d, rows, cols, valid):
        d_near[0, d] += ds_ref[rows, cols].astype(FULL) * valid

    near_tiles(first, bq // TILE, per, collect)

    @pl.when(step == pl.num_programs(1) - 1)
    def _():
        if dk.dtype == FULL:
            dk[...] = dk_acc[...]
            dv[...] = dv_acc[...]
        else:
            side = lax.broadcasted_iota(jnp.int32, (total, TILE), 1)
            dk[...] = jnp.where(side < HEAD, dk_acc[...], 0.0).astype(LOW)
            dv[...] = jnp.where(side < HEAD, dv_acc[...], 0.0).astype(LOW)
        sums = [
            jnp.sum(dk_acc[k * TILE : k * TILE + TILE, :], axis=0, keepdims=True)
            for k in range(count)
        ]
        tiles[0] = jnp.concatenate(sums, axis=0)


def attend_back(
    info, qa, ka, kt, va, sums, resid, cs, gain, wo, ot, lse, near, part, kc, per, given
):
    total, wide = ka.shape
    heads = wide // TILE
    model = resid.shape[1]
    rows = total // SPLIT // RANKS
    bq = 2 * rows
    span = total // SPLIT
    steps = span // bq
    offset = part * steps
    last = part == SPLIT - 1
    once = lambda h, i: jnp.where(h == 0, i, steps - 1)
    head_cols = pl.BlockSpec((total, TILE), lambda h, i, c: (0, h))
    near_block = pl.BlockSpec((1, 3, TILE, TILE), lambda h, i, c: (h, 0, 0, 0))
    out_block = pl.BlockSpec((HEAD, model), lambda h, i, c: (h, 0))
    kind = LOW if last else FULL
    full = lambda shape: pl.BlockSpec(shape, lambda h, i, c: tuple(0 for _ in shape))
    return pl.pallas_call(
        functools.partial(backward_kernel, per, offset, kc),
        grid_spec=pltpu.PrefetchScalarGridSpec(
            num_scalar_prefetch=1,
            grid=(heads, steps),
            in_specs=[
                pl.BlockSpec((bq, TILE), lambda h, i, c: (i + offset, h)),
                head_cols,
                pl.BlockSpec((TILE, total), lambda h, i, c: (h, 0)),
                head_cols,
            ]
            + [pl.BlockSpec((1, rows, model), lambda h, i, c: (once(h, i), 0, 0))] * 2
            + [pl.BlockSpec((bq, model), lambda h, i, c: (once(h, i), 0))]
            + [pl.BlockSpec((rows, model), lambda h, i, c: (part, 0))] * RANKS
            + [
                full(gain.shape),
                pl.BlockSpec((TILE, model), lambda h, i, c: (h, 0)),
                pl.BlockSpec((HEAD, bq), lambda h, i, c: (h, i)),
                pl.BlockSpec((8, bq), lambda h, i, c: (0, i)),
                near_block,
            ]
            + ([] if len(given) == 0 else [head_cols, head_cols, near_block, out_block]),
            out_specs=[
                pl.BlockSpec((bq, TILE), lambda h, i, c: (i, h)),
                head_cols,
                head_cols,
                near_block,
                out_block,
                pl.BlockSpec((1, RANKS * per, TILE), lambda h, i, c: (h, 0, 0)),
            ],
            scratch_shapes=[
                pltpu.VMEM((total, bq), FULL),
                pltpu.VMEM((total, bq), LOW),
                pltpu.VMEM((total, TILE), FULL),
                pltpu.VMEM((total, TILE), FULL),
                pltpu.VMEM((span, model), LOW),
            ],
        ),
        out_shape=[
            jax.ShapeDtypeStruct((span, wide), LOW),
            jax.ShapeDtypeStruct((total, wide), kind),
            jax.ShapeDtypeStruct((total, wide), kind),
            jax.ShapeDtypeStruct((heads, 3, TILE, TILE), FULL),
            jax.ShapeDtypeStruct((heads * HEAD, model), FULL),
            jax.ShapeDtypeStruct((heads, RANKS * per, TILE), FULL),
        ],
        compiler_params=params(),
        name="attend_back",
        cost_estimate=cost(40 * heads * span * total * HEAD),
    )(info, qa, ka, kt, va, *sums, resid, *cs, gain, wo, ot, lse, near, *given)


def bucket_kernel(d_near, out):
    heads = d_near.shape[0]
    found = [[jnp.zeros((1, TILE), FULL)] * BUCKETS for _ in range(heads)]
    for d in (-1, 0, 1):
        buckets = near_bucket(d)
        for b in buckets_near(d):
            here = buckets == b
            for h in range(heads):
                found[h][b] = found[h][b] + jnp.sum(
                    jnp.where(here, d_near[h, d + 1], 0.0), axis=0, keepdims=True
                )
    for h in range(heads):
        out[h] = jnp.concatenate(found[h], axis=0)


def bucket_sums(d_near):
    heads = d_near.shape[0]
    return pl.pallas_call(
        bucket_kernel,
        out_shape=jax.ShapeDtypeStruct((heads, BUCKETS, TILE), FULL),
        compiler_params=params(),
        name="bucket_sums",
    )(d_near)


def tail_kernel(info, dq0, dq1, dk, dv, w_ref, keep, give):
    wide = dk.shape[1]
    dq = pick_block(pl.program_id(0), (dq0, dq1))
    out = dot_nn(dq, w_ref[:wide, :]) + dot_nn(dk[...], w_ref[wide : 2 * wide, :])
    out = (out + dot_nn(dv[...], w_ref[2 * wide :, :])).astype(LOW)
    rows = out.shape[0] // RANKS
    even = info[0] % 2 == 0
    low = info[0] // 2 == 0
    parts = [out[k * rows : k * rows + rows] for k in range(RANKS)]
    kept = [jnp.where(even, parts[k], parts[k + 1]) for k in (0, 2)]
    given = [jnp.where(even, parts[k + 1], parts[k]) for k in (0, 2)]
    keep[0], keep[1] = jnp.where(low, kept[0], kept[1]), jnp.where(low, kept[1], kept[0])
    give[0], give[1] = jnp.where(low, given[0], given[1]), jnp.where(low, given[1], given[0])


def tail(info, dqs, dk, dv, w_wide):
    total, wide = dk.shape
    model = w_wide.shape[1]
    span = total // SPLIT
    rows = span // RANKS
    rel_block = pl.BlockSpec((2, rows, model), lambda i, c: (i, 0, 0))
    return pl.pallas_call(
        tail_kernel,
        grid_spec=pltpu.PrefetchScalarGridSpec(
            num_scalar_prefetch=1,
            grid=(SPLIT,),
            in_specs=[
                whole_spec((span, wide)),
                whole_spec((span, wide)),
                pl.BlockSpec((span, wide), lambda i, c: (i, 0)),
                pl.BlockSpec((span, wide), lambda i, c: (i, 0)),
                whole_spec(w_wide.shape),
            ],
            out_specs=[rel_block, rel_block],
        ),
        out_shape=[jax.ShapeDtypeStruct((2 * SPLIT, rows, model), LOW)] * 2,
        compiler_params=params(),
        name="tail",
        cost_estimate=cost(6 * total * wide * model),
    )(info, *dqs, dk, dv, w_wide)


def weights_kernel(steps, dq0, dq1, dk, dv, normed, g_out, extra, out, acc):
    step = pl.program_id(0)

    @pl.when(step == 0)
    def _():
        acc[...] = jnp.zeros_like(acc)

    dq = pick_block(step // (steps // 2), (dq0, dq1))
    acc[...] += dot_tn(jnp.concatenate([dq, dk[...], dv[...]], axis=1), normed[...])

    @pl.when(step == steps - 1)
    def _():
        count = acc.shape[0] // TILE
        for j in range(count):
            out[j * HEAD : j * HEAD + HEAD, :] = acc[j * TILE : j * TILE + HEAD, :].astype(LOW)
        base = count * HEAD
        out[base : base + g_out.shape[0], :] = g_out[...].astype(LOW)
        out[base + g_out.shape[0] :, :] = extra[...]


def weights(dqs, dk, dv, normed, g_out, extra):
    total, wide = dk.shape
    model = normed.shape[1]
    steps = 4
    rows = total // steps
    half = steps // 2
    full = lambda shape: pl.BlockSpec(shape, lambda i: tuple(0 for _ in shape))
    block = lambda w: pl.BlockSpec((rows, w), lambda i: (i, 0))
    out_rows = 3 * wide * HEAD // TILE + g_out.shape[0] + extra.shape[0]
    return pl.pallas_call(
        functools.partial(weights_kernel, steps),
        grid=(steps,),
        in_specs=[
            pl.BlockSpec((rows, wide), lambda i: (jnp.minimum(i, half - 1), 0)),
            pl.BlockSpec((rows, wide), lambda i: (jnp.maximum(i - half, 0), 0)),
            block(wide),
            block(wide),
            block(model),
            full(g_out.shape),
            full(extra.shape),
        ],
        out_specs=full((out_rows, model)),
        out_shape=jax.ShapeDtypeStruct((out_rows, model), LOW),
        scratch_shapes=[pltpu.VMEM((3 * wide, model), FULL)],
        compiler_params=params(),
        name="weights",
        cost_estimate=cost(6 * total * wide * model),
    )(*dqs, dk, dv, normed, g_out, extra)


def together(*values):
    return lax.optimization_barrier(values)


def after(value, *given):
    return lax.optimization_barrier((value,) + given)[0]


def swap_seq(value, bit):
    return lax.ppermute(value, "seq", [(i, i ^ bit) for i in range(RANKS)])


def regroup(value, skip):
    pairs = []
    for s in range(RANKS):
        for t in range(RANKS):
            if t != skip and MIX[s] != 0:
                pairs.append((s * RANKS + t, s * RANKS + (t ^ MIX[s])))
    moved = lax.ppermute(value, ("seq", "tensor"), pairs)
    return jnp.where(lax.axis_index("seq") == MIX.index(0), value, moved)


def along_tensor(value, pairs):
    return lax.ppermute(value, "tensor", pairs)


def step_one(own):
    return along_tensor(own, [(0, 1), (2, 3)]), along_tensor(own, [(3, 2), (2, 1)])


def step_two(moved):
    return along_tensor(moved[0], [(1, 2)]), along_tensor(moved[1], [(2, 1), (1, 0)])


def step_three(moved):
    return along_tensor(moved[0], [(2, 3)]), along_tensor(moved[1], [(1, 0)])


HOME = (0, 0, 1, 2)
PLACES = (
    ((None, 0, None, 1), (None, 1, 2, None)),
    ((None, None, 0, None), (1, 2, None, None)),
    ((None, None, None, 0), (2, None, None, None)),
)


def by_rank(values, rank):
    out = values[0]
    for index in range(1, len(values)):
        out = jnp.where(rank == index, values[index], out)
    return out


def keep_step(held, own, moved, places, rank):
    for value, place in zip(moved, places):
        got = by_rank([p is not None for p in place], rank)
        at = by_rank([HOME[k] if p is None else p for k, p in enumerate(place)], rank)
        value = jnp.where(got, value, own)
        held = lax.dynamic_update_slice(held, value[None], (at, 0, 0))
    return held


def swap_dp(value):
    return lax.ppermute(value, "dp", [(0, 1), (1, 0)])


def join_dp(halves, axis):
    if len(halves) == 1:
        return lax.all_gather(halves[0], "dp", axis=axis, tiled=True)
    value, other = halves
    swap = lax.axis_index("dp") == 1
    return jnp.concatenate(
        [jnp.where(swap, other, value), jnp.where(swap, value, other)], axis=axis
    )


def gather_dp(value, axis):
    if lax.axis_size("dp") != 2:
        return join_dp((value,), axis)
    return join_dp((value, swap_dp(value)), axis)


def scatter_dp(value, axis):
    if lax.axis_size("dp") != 2:
        return lax.psum_scatter(value, "dp", scatter_dimension=axis, tiled=True).astype(LOW)
    size = value.shape[axis] // 2
    mine = lax.axis_index("dp")
    keep = lax.dynamic_slice_in_dim(value, mine * size, size, axis)
    give = lax.dynamic_slice_in_dim(value, (1 - mine) * size, size, axis)
    return (keep.astype(FULL) + swap_dp(give.astype(LOW)).astype(FULL)).astype(LOW)


def sum_pair(value, bit):
    return value.astype(FULL) + swap_seq(value, bit).astype(FULL)


def normalize(values):
    scale = lax.rsqrt(jnp.mean(values * values, axis=-1, keepdims=True) + EPSILON)
    return values * scale, scale


def norm_back(grad, unit, scale, gain):
    along = grad * gain
    return scale * (along - unit * jnp.mean(along * unit, axis=-1, keepdims=True))


def body(
    inputs, lengths, gain_attn, w_query, w_key, w_value, w_out, bias_table,
    gain_ffn, w_in, w_down, cotangent,
):
    slots, rows_here, model = inputs.shape
    assert lax.axis_size("seq") == RANKS and lax.axis_size("tensor") == RANKS and slots == 3
    total = RANKS * rows_here
    per = rows_here // TILE
    narrow = w_query.shape[1]
    heads = narrow // HEAD
    hid = w_in.shape[1]
    rank = lax.axis_index("tensor")
    chunk = lax.axis_index("seq")
    mine = lax.axis_index("dp")
    slot = jnp.where(rank == 0, 0, rank - 1)
    length = lax.dynamic_index_in_dim(lengths, slot, 0, keepdims=False)
    order = jnp.bitwise_xor(chunk, jnp.arange(RANKS, dtype=jnp.int32)).astype(jnp.int32)
    info = jnp.concatenate([order, length[None], jnp.zeros((3,), jnp.int32)])
    rows_part = rows_here // SPLIT
    size = gain_attn.shape[0]
    cut = lambda v: v.reshape(SPLIT, rows_part, model)

    x_own = lax.dynamic_index_in_dim(inputs, slot, 0, keepdims=False)
    x_far = swap_seq(x_own, 2)
    x_near = swap_seq(x_own, 1)

    flat = bias_table.reshape(-1)
    small = jnp.stack(
        [gain_attn, gain_ffn, jnp.pad(flat, (0, size - flat.shape[0]))]
        + [jnp.zeros((size,), LOW)] * (EXTRA - 3)
    )
    w_first = after(w_query, x_own)
    pack = jnp.concatenate([w_first.T, w_key.T, w_value.T, w_out, small], axis=0)
    pack = regroup(pack, None)
    w_all = gather_dp(pack, 1)
    main = 4 * narrow
    w_wide = jnp.pad(
        w_all[: 3 * narrow].reshape(3 * heads, HEAD, model), ((0, 0), (0, TILE - HEAD), (0, 0))
    ).reshape(3 * heads * TILE, model)
    gain_one = w_all[main : main + 1].astype(FULL)
    gain_two = w_all[main + 1 : main + 2].astype(FULL)
    table = w_all[main + 2].reshape(-1, size)[:, : flat.shape[0]]
    table = table.reshape(BUCKETS, heads).astype(FULL)
    xs = [x_own, x_near, x_far, swap_seq(x_far, 1)]

    position = chunk * rows_here + jnp.arange(rows_here, dtype=jnp.int32)
    live = jnp.logical_and(position < length, rank != IDLE)
    c_own = lax.dynamic_index_in_dim(cotangent, slot, 0, keepdims=False)
    c_own = jnp.where(live[:, None], c_own, jnp.zeros((), LOW))
    ffn_pack = regroup(after(jnp.concatenate([w_in, w_down.T], axis=1), pack), None)
    c_first = after(c_own, x_far)
    c_far = swap_seq(c_first, 2)

    normed, qa, ka, va, kt, vt, near = project(info, xs, gain_one, w_wide, table, heads, per)

    normed, c_far, ffn_pack = together(normed, c_far, ffn_pack)
    qa, ka, vt, _ = together(qa, ka, vt, normed)
    out_mine = w_all[3 * narrow : main]
    out_near, out_far = swap_seq(out_mine, 1), swap_seq(out_mine, 2)
    ffn_halves = (ffn_pack, swap_dp(ffn_pack)) if lax.axis_size("dp") == 2 else (ffn_pack,)
    cs = [c_own, swap_seq(c_first, 1), c_far, swap_seq(c_far, 1)]
    out_wide = jnp.pad(
        out_mine.reshape(heads, HEAD, model), ((0, 0), (0, TILE - HEAD), (0, 0))
    ).reshape(heads * TILE, model)

    bq = min(1024, total // SPLIT)
    attended = [attend(qa, ka, vt, near, 0, bq, per)]
    attended[0], cs, out_far = together(attended[0], cs, out_far)
    outs = [out_mine, out_near, out_far, swap_seq(out_far, 1)]
    mixed = attended[0][0]
    pieces = [[mixed] + [swap_seq(mixed, bit) for bit in (1, 2, 3)]]

    attended.append(attend(after(qa, mixed), ka, vt, near, 1, bq, per))
    attended[1], pieces[0], outs, ffn_halves = together(
        attended[1], pieces[0], outs, ffn_halves
    )
    w_ffn = join_dp(ffn_halves, 0)
    mixed = attended[1][0]
    pieces.append([mixed] + [swap_seq(mixed, bit) for bit in (1, 2, 3)])

    def chip_sum(mid, core):
        return (mid[2].astype(FULL) + core.astype(FULL)).astype(LOW)

    def whole_sum(part):
        both = chip[part].astype(FULL) + chip_far[part].astype(FULL)
        both = both.astype(LOW)
        return both, swap_seq(both, 1)

    def out_rows(part):
        resid = lax.dynamic_index_in_dim(
            mids[part][4].reshape(RANKS, rows_part, model), chunk, 0, keepdims=False
        )
        return (resid + (ffn[part][0] + ffn_far[part].astype(FULL))).astype(LOW)

    mids, chip, chip_far = [], [], []
    for part in range(SPLIT):
        mid = middle(
            info, xs, cs, pieces[part], outs, gain_two, w_ffn, part,
            None if part == 0 else mids[0][5],
        )
        if part == 0:
            mid, pieces[1] = together(mid, pieces[1])
        else:
            mid, chip_far[0] = together(mid, chip_far[0])
        mids.append(mid)
        chip.append(chip_sum(mid, swap_seq(mid[3], 1)))
        chip_far.append(swap_seq(chip[part], 2))
        if part == 0:
            pieces[1] = after(pieces[1], chip[0])

    sums = [whole_sum(0)]
    ffn = [after(mid[:2], chip[1]) for mid in mids]
    ffn = [f[0].astype(FULL) + swap_seq(f[1], 1).astype(FULL) for f in ffn]
    ffn_far = jnp.stack([f[1].astype(LOW) for f in ffn])
    g_ffn = after(mids[1][5], chip[1])
    g_ffn = lax.psum_scatter(g_ffn, "dp", scatter_dimension=0, tiled=True)
    sums[0] = after(sums[0], ffn_far)
    ffn_far = swap_seq(ffn_far, 2)

    args = (gain_two, out_wide)
    back = [
        attend_back(
            info, qa, ka, kt, va, sums[0], mids[0][4], cs, *args, *attended[0][1:], near, 0,
            512, per, (),
        )
    ]
    back[0], chip_far[1], ffn_far, g_ffn = together(back[0], chip_far[1], ffn_far, g_ffn)
    sums.append(whole_sum(1))
    out_own = jnp.concatenate([out_rows(part) for part in range(SPLIT)], axis=0)
    out_own = after(out_own, sums[1][0])
    g_ffn = regroup(g_ffn, IDLE)
    given = back[0][1:5]
    sums[1] = after(sums[1], out_own)
    back.append(
        attend_back(
            info, qa, ka, kt, va, sums[1], mids[1][4], cs, *args, *attended[1][1:], near, 1,
            512, per, given,
        )
    )
    back[1], g_ffn = together(back[1], g_ffn)
    outputs = lax.all_gather(after(out_own, g_ffn), "tensor")
    g_core = swap_seq(g_ffn, 1)
    dk, dv, d_near = back[1][1:4]
    resids = [
        lax.dynamic_index_in_dim(
            mid[4].reshape(RANKS, rows_part, model), chunk, 0, keepdims=False
        )
        for mid in mids
    ]

    dqs = [b[0] for b in back]
    keep, give = tail(info, dqs, dk, dv, w_wide)
    core = swap_seq(give, 1)
    found = bucket_sums(after(d_near, give))
    found, core, g_core = together(found, core, g_core)
    far_low = (keep[1::2].astype(FULL) + core[1::2].astype(FULL)).astype(LOW)
    far = swap_seq(far_low, 2)
    dqs, dk, dv, found, g_core = after((dqs, dk, dv, found, g_core), far_low)
    near_sum = jnp.sum(found, axis=2).T
    tile_sum = back[1][5][:, :, HEAD : HEAD + RANKS * per]
    tiles = tile_at(jnp.arange(RANKS * per), per)
    left = tiles[:, None] < tiles[None, :] - 1
    right = tiles[:, None] > tiles[None, :] + 1
    left_sum = jnp.sum(jnp.where(left, tile_sum, 0.0), axis=(1, 2))
    right_sum = jnp.sum(jnp.where(right, tile_sum, 0.0), axis=(1, 2))
    spot = jnp.arange(BUCKETS)[:, None]
    d_table = near_sum + jnp.where(spot == BUCKETS // 2 - 1, left_sum[None], 0.0)
    d_table = d_table + jnp.where(spot == BUCKETS - 1, right_sum[None], 0.0)
    d_table = d_table.reshape(model // size, flat.shape[0])
    d_table = jnp.pad(d_table, ((0, 0), (0, size - flat.shape[0]))).reshape(1, model)
    extra = jnp.concatenate([d_table, jnp.zeros((EXTRA - 1, model), FULL)], axis=0)
    g_all = weights(dqs, dk, dv, normed, back[1][4], extra.astype(LOW))
    g_all, far = together(g_all, far)
    x_parts, c_parts = cut(x_own).astype(FULL), cut(c_own).astype(FULL)
    own, gain_attn_part, gain_ffn_part = [], 0.0, 0.0
    for part in range(SPLIT):
        total_two = lax.dynamic_index_in_dim(sums[part][0], chunk // 2, 0, keepdims=False)
        total_two = total_two.astype(FULL)
        unit_two, scale_two = normalize(resids[part])
        gain_ffn_part = gain_ffn_part + jnp.sum(total_two * unit_two, axis=0)
        d_resid = c_parts[part] + norm_back(total_two, unit_two, scale_two, gain_two)
        unit, scale = normalize(x_parts[part])
        grad = keep[2 * part].astype(FULL) + core[2 * part].astype(FULL)
        grad = grad + far[part].astype(FULL)
        gain_attn_part = gain_attn_part + jnp.sum(grad * unit, axis=0)
        own.append((d_resid + norm_back(grad, unit, scale, gain_one)).astype(LOW))
    own = jnp.concatenate(own, axis=0)
    gains = jnp.stack([gain_attn_part, gain_ffn_part])
    g_ffn = (g_ffn.astype(FULL) + g_core.astype(FULL)).astype(LOW)
    g_all, g_ffn, gains = after((g_all, g_ffn, gains), own)

    held = jnp.zeros((slots, rows_here, model), LOW)
    home = by_rank(HOME, rank)
    held = lax.dynamic_update_slice(held, own[None], (home, 0, 0))
    one = step_one(own)
    gains = sum_pair(sum_pair(gains, 1), 2)
    g_all = scatter_dp(g_all, 1)
    g_far = swap_seq(after(g_ffn, gains), 2)
    one, g_all, gains, outputs = together(one, g_all, gains, outputs)

    two = step_two(one)
    held = keep_step(held, own, one, PLACES[0], rank)
    own = jnp.where(rank == IDLE, one[0], own)
    g_all = regroup(g_all, IDLE)
    gains = gains + swap_dp(gains) if lax.axis_size("dp") == 2 else lax.psum(gains, "dp")
    gains = gains + along_tensor(gains, [(t, t ^ 1) for t in range(RANKS)])
    g_ffn = g_ffn.astype(FULL) + g_far.astype(FULL)
    g_all = sum_pair(g_all, 1).astype(LOW)
    outputs = jnp.stack([outputs[0], outputs[2], outputs[3]])
    two, g_all, gains, held, g_ffn, outputs = together(two, g_all, gains, held, g_ffn, outputs)

    three = step_three(two)
    held = keep_step(held, own, two, PLACES[1], rank)
    g_all = sum_pair(g_all, 2)
    gains = gains + along_tensor(gains, [(t, t ^ 2) for t in range(RANKS)])
    grad_in, grad_down = g_ffn[:, :hid], g_ffn[:, hid:].T
    three, g_all, gains, held, grad_in, grad_down, outputs = together(
        three, g_all, gains, held, grad_in, grad_down, outputs
    )
    grad_inputs = keep_step(held, own, three, PLACES[2], rank)
    gains = lax.dynamic_slice_in_dim(gains, mine * size, size, 1)
    grad_gain_attn, grad_gain_ffn = gains[0], gains[1]
    grad_table = g_all[main, : flat.shape[0]].reshape(bias_table.shape)
    return (
        outputs,
        grad_inputs,
        grad_gain_attn,
        g_all[:narrow].T,
        g_all[narrow : 2 * narrow].T,
        g_all[2 * narrow : 3 * narrow].T,
        g_all[3 * narrow : main],
        grad_table,
        grad_gain_ffn,
        grad_in,
        grad_down,
    )


def solution(mesh):
    in_specs = (
        P("dp", "seq", None),
        P("dp"),
        P("dp"),
        P("dp", "tensor"),
        P("dp", "tensor"),
        P("dp", "tensor"),
        P("tensor", "dp"),
        P("dp", "tensor"),
        P("dp"),
        P("dp", "tensor"),
        P("tensor", "dp"),
        P("dp", "seq", None),
    )
    out_specs = (
        P("dp", "seq", None),
        P("dp", "seq", None),
        P("dp"),
        P("dp", "tensor"),
        P("dp", "tensor"),
        P("dp", "tensor"),
        P("tensor", "dp"),
        P("dp", "tensor"),
        P("dp"),
        P("dp", "tensor"),
        P("tensor", "dp"),
    )
    return jax.shard_map(body, mesh=mesh, in_specs=in_specs, out_specs=out_specs, check_vma=False)
```

```python
import functools

import jax
import jax.numpy as jnp
from jax import lax
from jax.experimental import pallas as pl
from jax.experimental.pallas import tpu as pltpu
from jax.sharding import PartitionSpec as P

HEAD = 64
BUCKETS = 32
EPSILON = 1e-06
LIMITS = (12, 16, 23, 32, 46, 64, 91)
LOW = jnp.bfloat16
FULL = jnp.float32
TILE = 128
RANKS = 4
MIX = (0, 2, 1, 3)
IDLE = 1
SPLIT = 2
EXTRA = 32
SHORTEN = 64
GELU_A = 0.7978845608028654
GELU_B = 0.044715
KERNEL_MEMORY = 60 * 1024 * 1024


def bucket_of(relative):
    sign_part = jnp.where(relative > 0, 16, 0).astype(jnp.int32)
    distance = jnp.abs(relative)
    far_part = jnp.full(distance.shape, 8, jnp.int32)
    for limit in LIMITS:
        far_part = far_part + (distance >= limit).astype(jnp.int32)
    return sign_part + jnp.where(distance < 8, distance, far_part)


def dot_nn(left, right):
    return lax.dot_general(left, right, (((1,), (0,)), ((), ())), preferred_element_type=FULL)


def dot_nt(left, right):
    return lax.dot_general(left, right, (((1,), (1,)), ((), ())), preferred_element_type=FULL)


def dot_tn(left, right):
    return lax.dot_general(left, right, (((0,), (0,)), ((), ())), preferred_element_type=FULL)


def tile_place(tile, per):
    sub = per // SPLIT
    return ((tile % per) // sub) * (RANKS * sub) + (tile // per) * sub + tile % sub


def tile_at(place, per):
    sub = per // SPLIT
    return ((place // sub) % RANKS) * per + (place // (RANKS * sub)) * sub + place % sub


def cost(flops):
    return pl.CostEstimate(flops=flops // SHORTEN, bytes_accessed=0, transcendentals=0)


def params():
    return pltpu.CompilerParams(vmem_limit_bytes=KERNEL_MEMORY)


def whole_spec(shape):
    return pl.BlockSpec(shape, lambda i, c: tuple(0 for _ in shape))


def near_bucket(d):
    key = lax.broadcasted_iota(jnp.int32, (TILE, TILE), 0)
    query = lax.broadcasted_iota(jnp.int32, (TILE, TILE), 1)
    return bucket_of(TILE * d + key - query)


def buckets_near(d):
    half = BUCKETS // 2
    if d < 0:
        return range(half)
    return range(half, BUCKETS) if d > 0 else range(BUCKETS)


def pick_block(index, refs):
    value = refs[0][...]
    for k in range(1, len(refs)):
        value = jnp.where(index == k, refs[k][...], value)
    return value


def pick_pair(info, chunk, refs):
    return jnp.concatenate([pick_block(info[chunk + k], refs) for k in range(2)], axis=0)


def project_kernel(
    heads, per, info, x0, x1, x2, x3, gain_ref, w_ref, table, normed, qa, ka, va, kt, vt, near
):
    step = pl.program_id(0)

    @pl.when(step == 0)
    def _():
        for d in (-1, 0, 1):
            buckets = near_bucket(d)
            for h in range(heads):
                tile = jnp.zeros((TILE, TILE), FULL)
                for b in buckets_near(d):
                    tile = jnp.where(buckets == b, table[b, h], tile)
                near[h, d + 1] = tile

    rows = 2 * x0.shape[0]
    x = pick_pair(info, (2 * step) % RANKS, (x0, x1, x2, x3)).astype(FULL)
    scale = lax.rsqrt(jnp.mean(x * x, axis=-1, keepdims=True) + EPSILON)
    xn = (x * scale * gain_ref[...]).astype(LOW)
    normed[...] = xn
    y = dot_nt(xn, w_ref[...])
    row = lax.broadcasted_iota(jnp.int32, (rows, TILE), 0)
    lane = lax.broadcasted_iota(jnp.int32, (rows, TILE), 1) - HEAD
    place = step * (rows // TILE) + row // TILE
    count = RANKS * per
    is_tile = jnp.logical_and(lane >= 0, lane < count)
    here = tile_at(place, per)
    there = tile_at(jnp.where(is_tile, lane, 0), per)
    position = here * TILE + row % TILE
    q_extra = jnp.where(jnp.logical_or(lane == place, lane == count), 1.0, 0.0)
    v_extra = jnp.where(lane == 0, 1.0, 0.0)
    dead = jnp.where(jnp.logical_and(lane == count, position >= info[RANKS]), -1e30, 0.0)
    left = jnp.logical_and(is_tile, here < there - 1)
    right = jnp.logical_and(is_tile, here > there + 1)
    wide = heads * TILE
    for h in range(heads):
        before, behind = table[BUCKETS // 2 - 1, h], table[BUCKETS - 1, h]
        k_extra = jnp.where(left, before, jnp.where(right, behind, dead))
        at = slice(TILE * h, TILE * h + TILE)
        qa[:, at] = (y[:, at] + q_extra).astype(LOW)
        kh = y[:, wide + TILE * h : wide + TILE * h + TILE] + k_extra
        vh = y[:, 2 * wide + TILE * h : 2 * wide + TILE * h + TILE] + v_extra
        ka[:, at] = kh.astype(LOW)
        va[:, at] = vh.astype(LOW)
        kt[at, :] = kh.T.astype(LOW)
        vt[at, :] = vh.T.astype(LOW)


def project(info, xs, gain, w_qkv, table, heads, per):
    total = RANKS * xs[0].shape[0]
    rows = xs[0].shape[0] // SPLIT
    width = xs[0].shape[1]
    row_block = lambda w: pl.BlockSpec((2 * rows, w), lambda i, c: (i, 0))
    col_block = lambda w: pl.BlockSpec((w, 2 * rows), lambda i, c: (0, i))
    wide = heads * TILE
    return pl.pallas_call(
        functools.partial(project_kernel, heads, per),
        grid_spec=pltpu.PrefetchScalarGridSpec(
            num_scalar_prefetch=1,
            grid=(RANKS * SPLIT // 2,),
            in_specs=[pl.BlockSpec((rows, width), lambda i, c: (2 * i // RANKS, 0))] * RANKS
            + [
                whole_spec(gain.shape),
                whole_spec(w_qkv.shape),
                pl.BlockSpec(memory_space=pltpu.SMEM),
            ],
            out_specs=[
                row_block(width),
                row_block(wide),
                row_block(wide),
                row_block(wide),
                col_block(wide),
                col_block(wide),
                whole_spec((heads, 3, TILE, TILE)),
            ],
        ),
        out_shape=[
            jax.ShapeDtypeStruct((total, width), LOW),
            jax.ShapeDtypeStruct((total, wide), LOW),
            jax.ShapeDtypeStruct((total, wide), LOW),
            jax.ShapeDtypeStruct((total, wide), LOW),
            jax.ShapeDtypeStruct((wide, total), LOW),
            jax.ShapeDtypeStruct((wide, total), LOW),
            jax.ShapeDtypeStruct((heads, 3, TILE, TILE), FULL),
        ],
        compiler_params=params(),
        name="project",
        cost_estimate=cost(8 * total * width * heads * HEAD),
    )(info, *xs, gain, w_qkv, table)


def near_tiles(first_place, tiles, per, visit):
    count = RANKS * per
    for u in range(tiles):
        here = tile_at(first_place + u, per)
        for d in (-1, 0, 1):
            there = here + d
            valid = jnp.logical_and(there >= 0, there < count)
            place = tile_place(jnp.clip(there, 0, count - 1), per)
            rows = pl.ds(pl.multiple_of(place * TILE, TILE), TILE)
            visit(d + 1, rows, slice(u * TILE, u * TILE + TILE), jnp.where(valid, 1.0, 0.0))


def score_block(h, first_place, per, qa, ka, near, s_ref):
    bq = qa.shape[0]
    at = slice(TILE * h, TILE * h + TILE)
    s_ref[h] = dot_nt(ka[:, at], qa[:, at])

    def add(d, rows, cols, valid):
        s_ref[h, rows, cols] = s_ref[h, rows, cols] + near[h, d] * valid

    near_tiles(first_place, bq // TILE, per, add)


def forward_kernel(heads, per, offset, qa, ka, vt, near, mixed, ot, lse, s_ref):
    bq = qa.shape[0]
    first = (pl.program_id(0) + offset) * (bq // TILE)
    for h in range(heads):
        score_block(h, first, per, qa, ka, near, s_ref)
    parts = []
    for h in range(heads):
        s = s_ref[h]
        top = jnp.max(s, axis=0, keepdims=True)
        p = jnp.exp(s - top).astype(LOW)
        o = dot_nn(vt[TILE * h : TILE * h + TILE, :], p)
        total = o[HEAD : HEAD + 1]
        o = o[:HEAD] * (1.0 / total)
        ot[HEAD * h : HEAD * h + HEAD, :] = o
        lse[h : h + 1, :] = top + jnp.log(total)
        parts.append(o.T)
    mixed[...] = jnp.concatenate(parts, axis=1).astype(LOW)


def attend(qa, ka, vt, near, part, bq, per):
    total, wide = ka.shape
    heads = wide // TILE
    span = total // SPLIT
    steps = span // bq
    offset = part * steps
    full = lambda shape: pl.BlockSpec(shape, lambda i: tuple(0 for _ in shape))
    width = heads * HEAD
    return pl.pallas_call(
        functools.partial(forward_kernel, heads, per, offset),
        grid=(steps,),
        in_specs=[
            pl.BlockSpec((bq, wide), lambda i: (i + offset, 0)),
            full(ka.shape),
            full(vt.shape),
            full(near.shape),
        ],
        out_specs=[
            pl.BlockSpec((bq, width), lambda i: (i, 0)),
            pl.BlockSpec((width, bq), lambda i: (0, i)),
            pl.BlockSpec((8, bq), lambda i: (0, i)),
        ],
        out_shape=[
            jax.ShapeDtypeStruct((span, width), LOW),
            jax.ShapeDtypeStruct((width, span), FULL),
            jax.ShapeDtypeStruct((8, span), FULL),
        ],
        scratch_shapes=[pltpu.VMEM((heads, total, bq), FULL)],
        compiler_params=params(),
        name="attend",
        cost_estimate=cost(20 * heads * span * total * HEAD),
    )(qa, ka, vt, near)


def middle_kernel(
    first, info, x0, x1, x2, x3, c0, c1, c2, c3, m0, m1, m2, m3, w0, w1, w2, w3,
    gain, w_ffn, *refs
):
    given, (f_keep, f_give, d_keep, d_give, resid_out, grads_out, grads) = refs[:-7], refs[-7:]
    step = pl.program_id(0)
    hid = w_ffn.shape[1] // 2

    @pl.when(step == 0)
    def _():
        grads[...] = jnp.zeros_like(grads) if first else given[0][...].astype(FULL)

    attn = dot_nn(m0[...], w0[...]) + dot_nn(m1[...], w1[...])
    attn = attn + dot_nn(m2[...], w2[...]) + dot_nn(m3[...], w3[...])
    resid = pick_block(info[step], (x0, x1, x2, x3)).astype(FULL) + attn
    resid_out[...] = resid
    scale = lax.rsqrt(jnp.mean(resid * resid, axis=-1, keepdims=True) + EPSILON)
    normed = (resid * scale * gain[...]).astype(LOW)
    hidden = dot_nn(normed, w_ffn[:, :hid])
    grad = pick_block(info[step], (c0, c1, c2, c3))
    d_active = dot_nn(grad, w_ffn[:, hid:])
    square = hidden * hidden
    th = jnp.tanh(GELU_A * hidden * (1.0 + GELU_B * square))
    half = 0.5 * (1.0 + th)
    active = (hidden * half).astype(LOW)
    slope = half + 0.5 * hidden * (1.0 - th * th) * (GELU_A * (1.0 + (3.0 * GELU_B) * square))
    d_hidden = (d_active * slope).astype(LOW)
    dn = dot_nt(d_hidden, w_ffn[:, :hid]).astype(LOW)
    ffn = dot_nt(active, w_ffn[:, hid:]).astype(LOW)

    @pl.when(info[step] % 2 == 0)
    def _():
        d_keep[0] = dn
        f_keep[0] = ffn

    @pl.when(info[step] % 2 == 1)
    def _():
        d_give[0] = dn
        f_give[0] = ffn

    grads[:, :hid] += dot_tn(normed, d_hidden)
    grads[:, hid:] += dot_tn(grad, active)

    @pl.when(step == RANKS - 1)
    def _():
        grads_out[...] = grads[...].astype(LOW)


def middle(info, xs, cs, pieces, outs, gain, w_ffn, part, given):
    rows, width = xs[0].shape[0] // SPLIT, xs[0].shape[1]
    narrow = pieces[0].shape[1]
    own_block = pl.BlockSpec((rows, width), lambda i, c: (part, 0))
    piece_block = pl.BlockSpec((rows, narrow), lambda i, c: (i, 0))
    rel_block = pl.BlockSpec((1, rows, width), lambda i, c: (c[i] // 2, 0, 0))
    pair_block = pl.BlockSpec((1, rows, width), lambda i, c: (i // 2, 0, 0))
    extra = () if given is None else (given,)
    two = jax.ShapeDtypeStruct((2, rows, width), LOW)
    return pl.pallas_call(
        functools.partial(middle_kernel, given is None),
        grid_spec=pltpu.PrefetchScalarGridSpec(
            num_scalar_prefetch=1,
            grid=(RANKS,),
            in_specs=[own_block] * (2 * RANKS)
            + [piece_block] * RANKS
            + [whole_spec(outs[0].shape)] * RANKS
            + [whole_spec(v.shape) for v in (gain, w_ffn) + extra],
            out_specs=[
                rel_block,
                rel_block,
                pair_block,
                pair_block,
                pl.BlockSpec((rows, width), lambda i, c: (i, 0)),
                whole_spec(w_ffn.shape),
            ],
            scratch_shapes=[pltpu.VMEM(w_ffn.shape, FULL)],
        ),
        out_shape=[two, two, two, two]
        + [
            jax.ShapeDtypeStruct((RANKS * rows, width), FULL),
            jax.ShapeDtypeStruct(w_ffn.shape, LOW),
        ],
        compiler_params=params(),
        name="middle",
        cost_estimate=cost(20 * RANKS * rows * width * w_ffn.shape[1] // 2),
    )(info, *xs, *cs, *pieces, *outs, gain, w_ffn, *extra)


def backward_kernel(
    per, offset, kc, info, qa, ka, kt, va, sum_mine, sum_other, resid_ref,
    c0, c1, c2, c3, gain, wo, ot, lse, near, *refs
):
    given = refs[:-11]
    dq, dk, dv, d_near, g_out, tiles, s_ref, ds_ref, dk_acc, dv_acc, d_rows = refs[-11:]
    head, step = pl.program_id(0), pl.program_id(1)
    bq = qa.shape[0]
    total = ka.shape[0]
    count = RANKS * per
    first = (step + offset) * (bq // TILE)
    here = pl.ds(pl.multiple_of(step * bq, bq), bq)

    @pl.when(step == 0)
    def _():
        if len(given) > 0:
            dk_acc[...] = given[0][...]
            dv_acc[...] = given[1][...]
            d_near[...] = given[2][...]
            g_out[...] = given[3][...]
        else:
            dk_acc[...] = jnp.zeros_like(dk_acc)
            dv_acc[...] = jnp.zeros_like(dv_acc)
            d_near[...] = jnp.zeros_like(d_near)
            g_out[...] = jnp.zeros_like(g_out)

    @pl.when(head == 0)
    def _():
        even = info[0] % 2 == 0
        blocks = []
        for k in range(sum_mine.shape[0]):
            mine, other = sum_mine[k], sum_other[k]
            blocks += [jnp.where(even, mine, other), jnp.where(even, other, mine)]
        d_norm = jnp.concatenate(blocks, axis=0).astype(FULL)
        cot = jnp.concatenate(
            [
                pick_block(info[len(blocks) * step + k], (c0, c1, c2, c3))
                for k in range(len(blocks))
            ],
            axis=0,
        ).astype(FULL)
        resid = resid_ref[...]
        scale = lax.rsqrt(jnp.mean(resid * resid, axis=-1, keepdims=True) + EPSILON)
        unit = resid * scale
        along = d_norm * gain[...]
        rows = cot + scale * (along - unit * jnp.mean(along * unit, axis=-1, keepdims=True))
        d_rows[here, :] = rows.astype(LOW)

    s_ref[...] = dot_nt(ka[...], qa[...])

    def add(d, rows, cols, valid):
        s_ref[rows, cols] = s_ref[rows, cols] + near[0, d] * valid

    near_tiles(first, bq // TILE, per, add)
    grad = d_rows[here, :]
    do = dot_nt(grad, wo[...]).astype(LOW)
    do_t = dot_nt(wo[...], grad).astype(LOW).astype(FULL)
    o_t = ot[...]
    g_out[...] += dot_nn(o_t.astype(LOW), grad)
    delta = jnp.sum(do_t[:HEAD] * o_t, axis=0, keepdims=True)
    lse_row = lse[pl.ds(head, 1), :]
    dq_t = jnp.zeros((TILE, bq), FULL)
    for c in range(total // kc):
        rows = slice(kc * c, kc * c + kc)
        p = jnp.exp(s_ref[rows, :] - lse_row)
        d_p = dot_nt(va[rows, :], do)
        d_s = (p * (d_p - delta)).astype(LOW)
        ds_ref[rows, :] = d_s
        dv_acc[rows, :] += dot_nn(p.astype(LOW), do)
        dk_acc[rows, :] += dot_nn(d_s, qa[...])
        dq_t += dot_nn(kt[:, rows], d_s)
    lane = lax.broadcasted_iota(jnp.int32, (bq, TILE), 1)
    dq[...] = jnp.where(lane < HEAD, dq_t.T, 0.0).astype(LOW)

    def collect(d, rows, cols, valid):
        d_near[0, d] += ds_ref[rows, cols].astype(FULL) * valid

    near_tiles(first, bq // TILE, per, collect)

    @pl.when(step == pl.num_programs(1) - 1)
    def _():
        if dk.dtype == FULL:
            dk[...] = dk_acc[...]
            dv[...] = dv_acc[...]
        else:
            side = lax.broadcasted_iota(jnp.int32, (total, TILE), 1)
            dk[...] = jnp.where(side < HEAD, dk_acc[...], 0.0).astype(LOW)
            dv[...] = jnp.where(side < HEAD, dv_acc[...], 0.0).astype(LOW)
        sums = [
            jnp.sum(dk_acc[k * TILE : k * TILE + TILE, :], axis=0, keepdims=True)
            for k in range(count)
        ]
        tiles[0] = jnp.concatenate(sums, axis=0)


def attend_back(
    info, qa, ka, kt, va, sums, resid, cs, gain, wo, ot, lse, near, part, kc, per, given
):
    total, wide = ka.shape
    heads = wide // TILE
    model = resid.shape[1]
    rows = total // SPLIT // RANKS
    bq = RANKS * rows
    span = total // SPLIT
    steps = span // bq
    offset = part * steps
    last = part == SPLIT - 1
    once = lambda h, i: jnp.where(h == 0, i, steps - 1)
    head_cols = pl.BlockSpec((total, TILE), lambda h, i, c: (0, h))
    near_block = pl.BlockSpec((1, 3, TILE, TILE), lambda h, i, c: (h, 0, 0, 0))
    out_block = pl.BlockSpec((HEAD, model), lambda h, i, c: (h, 0))
    kind = LOW if last else FULL
    full = lambda shape: pl.BlockSpec(shape, lambda h, i, c: tuple(0 for _ in shape))
    return pl.pallas_call(
        functools.partial(backward_kernel, per, offset, kc),
        grid_spec=pltpu.PrefetchScalarGridSpec(
            num_scalar_prefetch=1,
            grid=(heads, steps),
            in_specs=[
                pl.BlockSpec((bq, TILE), lambda h, i, c: (i + offset, h)),
                head_cols,
                pl.BlockSpec((TILE, total), lambda h, i, c: (h, 0)),
                head_cols,
            ]
            + [pl.BlockSpec((2, rows, model), lambda h, i, c: (once(h, i), 0, 0))] * 2
            + [pl.BlockSpec((bq, model), lambda h, i, c: (once(h, i), 0))]
            + [pl.BlockSpec((rows, model), lambda h, i, c: (part, 0))] * RANKS
            + [
                full(gain.shape),
                pl.BlockSpec((TILE, model), lambda h, i, c: (h, 0)),
                pl.BlockSpec((HEAD, bq), lambda h, i, c: (h, i)),
                pl.BlockSpec((8, bq), lambda h, i, c: (0, i)),
                near_block,
            ]
            + ([] if len(given) == 0 else [head_cols, head_cols, near_block, out_block]),
            out_specs=[
                pl.BlockSpec((bq, TILE), lambda h, i, c: (i, h)),
                head_cols,
                head_cols,
                near_block,
                out_block,
                pl.BlockSpec((1, RANKS * per, TILE), lambda h, i, c: (h, 0, 0)),
            ],
            scratch_shapes=[
                pltpu.VMEM((total, bq), FULL),
                pltpu.VMEM((total, bq), LOW),
                pltpu.VMEM((total, TILE), FULL),
                pltpu.VMEM((total, TILE), FULL),
                pltpu.VMEM((span, model), LOW),
            ],
        ),
        out_shape=[
            jax.ShapeDtypeStruct((span, wide), LOW),
            jax.ShapeDtypeStruct((total, wide), kind),
            jax.ShapeDtypeStruct((total, wide), kind),
            jax.ShapeDtypeStruct((heads, 3, TILE, TILE), FULL),
            jax.ShapeDtypeStruct((heads * HEAD, model), FULL),
            jax.ShapeDtypeStruct((heads, RANKS * per, TILE), FULL),
        ],
        compiler_params=params(),
        name="attend_back",
        cost_estimate=cost(40 * heads * span * total * HEAD),
    )(info, qa, ka, kt, va, *sums, resid, *cs, gain, wo, ot, lse, near, *given)


def bucket_kernel(d_near, out):
    heads = d_near.shape[0]
    found = [[jnp.zeros((1, TILE), FULL)] * BUCKETS for _ in range(heads)]
    for d in (-1, 0, 1):
        buckets = near_bucket(d)
        for b in buckets_near(d):
            here = buckets == b
            for h in range(heads):
                found[h][b] = found[h][b] + jnp.sum(
                    jnp.where(here, d_near[h, d + 1], 0.0), axis=0, keepdims=True
                )
    for h in range(heads):
        out[h] = jnp.concatenate(found[h], axis=0)


def bucket_sums(d_near):
    heads = d_near.shape[0]
    return pl.pallas_call(
        bucket_kernel,
        out_shape=jax.ShapeDtypeStruct((heads, BUCKETS, TILE), FULL),
        compiler_params=params(),
        name="bucket_sums",
    )(d_near)


def tail_kernel(info, dq0, dq1, dk, dv, w_ref, keep, give):
    wide = dk.shape[1]
    dq = pick_block(pl.program_id(0), (dq0, dq1))
    out = dot_nn(dq, w_ref[:wide, :]) + dot_nn(dk[...], w_ref[wide : 2 * wide, :])
    out = (out + dot_nn(dv[...], w_ref[2 * wide :, :])).astype(LOW)
    rows = out.shape[0] // RANKS
    even = info[0] % 2 == 0
    low = info[0] // 2 == 0
    parts = [out[k * rows : k * rows + rows] for k in range(RANKS)]
    kept = [jnp.where(even, parts[k], parts[k + 1]) for k in (0, 2)]
    given = [jnp.where(even, parts[k + 1], parts[k]) for k in (0, 2)]
    keep[0], keep[1] = jnp.where(low, kept[0], kept[1]), jnp.where(low, kept[1], kept[0])
    give[0], give[1] = jnp.where(low, given[0], given[1]), jnp.where(low, given[1], given[0])


def tail(info, dqs, dk, dv, w_wide):
    total, wide = dk.shape
    model = w_wide.shape[1]
    span = total // SPLIT
    rows = span // RANKS
    rel_block = pl.BlockSpec((2, rows, model), lambda i, c: (i, 0, 0))
    return pl.pallas_call(
        tail_kernel,
        grid_spec=pltpu.PrefetchScalarGridSpec(
            num_scalar_prefetch=1,
            grid=(SPLIT,),
            in_specs=[
                whole_spec((span, wide)),
                whole_spec((span, wide)),
                pl.BlockSpec((span, wide), lambda i, c: (i, 0)),
                pl.BlockSpec((span, wide), lambda i, c: (i, 0)),
                whole_spec(w_wide.shape),
            ],
            out_specs=[rel_block, rel_block],
        ),
        out_shape=[jax.ShapeDtypeStruct((2 * SPLIT, rows, model), LOW)] * 2,
        compiler_params=params(),
        name="tail",
        cost_estimate=cost(6 * total * wide * model),
    )(info, *dqs, dk, dv, w_wide)


def weights_kernel(steps, dq0, dq1, dk, dv, normed, g_out, extra, out, acc):
    step = pl.program_id(0)

    @pl.when(step == 0)
    def _():
        acc[...] = jnp.zeros_like(acc)

    dq = pick_block(step // (steps // 2), (dq0, dq1))
    acc[...] += dot_tn(jnp.concatenate([dq, dk[...], dv[...]], axis=1), normed[...])

    @pl.when(step == steps - 1)
    def _():
        count = acc.shape[0] // TILE
        for j in range(count):
            out[j * HEAD : j * HEAD + HEAD, :] = acc[j * TILE : j * TILE + HEAD, :].astype(LOW)
        base = count * HEAD
        out[base : base + g_out.shape[0], :] = g_out[...].astype(LOW)
        out[base + g_out.shape[0] :, :] = extra[...]


def weights(dqs, dk, dv, normed, g_out, extra):
    total, wide = dk.shape
    model = normed.shape[1]
    steps = 4
    rows = total // steps
    half = steps // 2
    full = lambda shape: pl.BlockSpec(shape, lambda i: tuple(0 for _ in shape))
    block = lambda w: pl.BlockSpec((rows, w), lambda i: (i, 0))
    out_rows = 3 * wide * HEAD // TILE + g_out.shape[0] + extra.shape[0]
    return pl.pallas_call(
        functools.partial(weights_kernel, steps),
        grid=(steps,),
        in_specs=[
            pl.BlockSpec((rows, wide), lambda i: (jnp.minimum(i, half - 1), 0)),
            pl.BlockSpec((rows, wide), lambda i: (jnp.maximum(i - half, 0), 0)),
            block(wide),
            block(wide),
            block(model),
            full(g_out.shape),
            full(extra.shape),
        ],
        out_specs=full((out_rows, model)),
        out_shape=jax.ShapeDtypeStruct((out_rows, model), LOW),
        scratch_shapes=[pltpu.VMEM((3 * wide, model), FULL)],
        compiler_params=params(),
        name="weights",
        cost_estimate=cost(6 * total * wide * model),
    )(*dqs, dk, dv, normed, g_out, extra)


def together(*values):
    return lax.optimization_barrier(values)


def after(value, *given):
    return lax.optimization_barrier((value,) + given)[0]


def swap_seq(value, bit):
    return lax.ppermute(value, "seq", [(i, i ^ bit) for i in range(RANKS)])


def regroup(value, skip):
    pairs = []
    for s in range(RANKS):
        for t in range(RANKS):
            if t != skip and MIX[s] != 0:
                pairs.append((s * RANKS + t, s * RANKS + (t ^ MIX[s])))
    moved = lax.ppermute(value, ("seq", "tensor"), pairs)
    return jnp.where(lax.axis_index("seq") == MIX.index(0), value, moved)


def along_tensor(value, pairs):
    return lax.ppermute(value, "tensor", pairs)


def step_one(own):
    return along_tensor(own, [(0, 1), (2, 3)]), along_tensor(own, [(3, 2), (2, 1)])


def step_two(moved):
    return along_tensor(moved[0], [(1, 2)]), along_tensor(moved[1], [(2, 1), (1, 0)])


def step_three(moved):
    return along_tensor(moved[0], [(2, 3)]), along_tensor(moved[1], [(1, 0)])


HOME = (0, 0, 1, 2)
PLACES = (
    ((None, 0, None, 1), (None, 1, 2, None)),
    ((None, None, 0, None), (1, 2, None, None)),
    ((None, None, None, 0), (2, None, None, None)),
)


def by_rank(values, rank):
    out = values[0]
    for index in range(1, len(values)):
        out = jnp.where(rank == index, values[index], out)
    return out


def keep_step(held, own, moved, places, rank):
    for value, place in zip(moved, places):
        got = by_rank([p is not None for p in place], rank)
        at = by_rank([HOME[k] if p is None else p for k, p in enumerate(place)], rank)
        value = jnp.where(got, value, own)
        held = lax.dynamic_update_slice(held, value[None], (at, 0, 0))
    return held


def swap_dp(value):
    return lax.ppermute(value, "dp", [(0, 1), (1, 0)])


def join_dp(halves, axis):
    if len(halves) == 1:
        return lax.all_gather(halves[0], "dp", axis=axis, tiled=True)
    value, other = halves
    swap = lax.axis_index("dp") == 1
    return jnp.concatenate(
        [jnp.where(swap, other, value), jnp.where(swap, value, other)], axis=axis
    )


def gather_dp(value, axis):
    if lax.axis_size("dp") != 2:
        return join_dp((value,), axis)
    return join_dp((value, swap_dp(value)), axis)


def scatter_dp(value, axis):
    if lax.axis_size("dp") != 2:
        return lax.psum_scatter(value, "dp", scatter_dimension=axis, tiled=True).astype(LOW)
    size = value.shape[axis] // 2
    mine = lax.axis_index("dp")
    keep = lax.dynamic_slice_in_dim(value, mine * size, size, axis)
    give = lax.dynamic_slice_in_dim(value, (1 - mine) * size, size, axis)
    return (keep.astype(FULL) + swap_dp(give.astype(LOW)).astype(FULL)).astype(LOW)


def sum_pair(value, bit):
    return value.astype(FULL) + swap_seq(value, bit).astype(FULL)


def normalize(values):
    scale = lax.rsqrt(jnp.mean(values * values, axis=-1, keepdims=True) + EPSILON)
    return values * scale, scale


def norm_back(grad, unit, scale, gain):
    along = grad * gain
    return scale * (along - unit * jnp.mean(along * unit, axis=-1, keepdims=True))


def body(
    inputs, lengths, gain_attn, w_query, w_key, w_value, w_out, bias_table,
    gain_ffn, w_in, w_down, cotangent,
):
    slots, rows_here, model = inputs.shape
    assert lax.axis_size("seq") == RANKS and lax.axis_size("tensor") == RANKS and slots == 3
    total = RANKS * rows_here
    per = rows_here // TILE
    narrow = w_query.shape[1]
    heads = narrow // HEAD
    hid = w_in.shape[1]
    rank = lax.axis_index("tensor")
    chunk = lax.axis_index("seq")
    mine = lax.axis_index("dp")
    slot = jnp.where(rank == 0, 0, rank - 1)
    length = lax.dynamic_index_in_dim(lengths, slot, 0, keepdims=False)
    order = jnp.bitwise_xor(chunk, jnp.arange(RANKS, dtype=jnp.int32)).astype(jnp.int32)
    info = jnp.concatenate([order, length[None], jnp.zeros((3,), jnp.int32)])
    rows_part = rows_here // SPLIT
    size = gain_attn.shape[0]
    cut = lambda v: v.reshape(SPLIT, rows_part, model)

    x_own = lax.dynamic_index_in_dim(inputs, slot, 0, keepdims=False)
    x_far = swap_seq(x_own, 2)
    x_near = swap_seq(x_own, 1)

    flat = bias_table.reshape(-1)
    small = jnp.stack(
        [gain_attn, gain_ffn, jnp.pad(flat, (0, size - flat.shape[0]))]
        + [jnp.zeros((size,), LOW)] * (EXTRA - 3)
    )
    w_first = after(w_query, x_own)
    pack = jnp.concatenate([w_first.T, w_key.T, w_value.T, w_out, small], axis=0)
    pack = regroup(pack, None)
    w_all = gather_dp(pack, 1)
    main = 4 * narrow
    w_wide = jnp.pad(
        w_all[: 3 * narrow].reshape(3 * heads, HEAD, model), ((0, 0), (0, TILE - HEAD), (0, 0))
    ).reshape(3 * heads * TILE, model)
    gain_one = w_all[main : main + 1].astype(FULL)
    gain_two = w_all[main + 1 : main + 2].astype(FULL)
    table = w_all[main + 2].reshape(-1, size)[:, : flat.shape[0]]
    table = table.reshape(BUCKETS, heads).astype(FULL)
    xs = [x_own, x_near, x_far, swap_seq(x_far, 1)]

    position = chunk * rows_here + jnp.arange(rows_here, dtype=jnp.int32)
    live = jnp.logical_and(position < length, rank != IDLE)
    c_own = lax.dynamic_index_in_dim(cotangent, slot, 0, keepdims=False)
    c_own = jnp.where(live[:, None], c_own, jnp.zeros((), LOW))
    ffn_pack = regroup(after(jnp.concatenate([w_in, w_down.T], axis=1), pack), None)
    c_first = after(c_own, x_far)
    c_far = swap_seq(c_first, 2)

    normed, qa, ka, va, kt, vt, near = project(info, xs, gain_one, w_wide, table, heads, per)

    normed, c_far, ffn_pack = together(normed, c_far, ffn_pack)
    qa, ka, vt, _ = together(qa, ka, vt, normed)
    out_mine = w_all[3 * narrow : main]
    out_near, out_far = swap_seq(out_mine, 1), swap_seq(out_mine, 2)
    ffn_halves = (ffn_pack, swap_dp(ffn_pack)) if lax.axis_size("dp") == 2 else (ffn_pack,)
    cs = [c_own, swap_seq(c_first, 1), c_far, swap_seq(c_far, 1)]
    out_wide = jnp.pad(
        out_mine.reshape(heads, HEAD, model), ((0, 0), (0, TILE - HEAD), (0, 0))
    ).reshape(heads * TILE, model)

    bq = min(1024, total // SPLIT)
    attended = [attend(qa, ka, vt, near, 0, bq, per)]
    attended[0], cs, out_far = together(attended[0], cs, out_far)
    outs = [out_mine, out_near, out_far, swap_seq(out_far, 1)]
    mixed = attended[0][0]
    pieces = [[mixed] + [swap_seq(mixed, bit) for bit in (1, 2, 3)]]

    attended.append(attend(after(qa, mixed), ka, vt, near, 1, bq, per))
    attended[1], pieces[0], outs, ffn_halves = together(
        attended[1], pieces[0], outs, ffn_halves
    )
    w_ffn = join_dp(ffn_halves, 0)
    mixed = attended[1][0]
    pieces.append([mixed] + [swap_seq(mixed, bit) for bit in (1, 2, 3)])

    def chip_sum(mid, core):
        return (mid[2].astype(FULL) + core.astype(FULL)).astype(LOW)

    def whole_sum(part):
        both = chip[part].astype(FULL) + chip_far[part].astype(FULL)
        both = both.astype(LOW)
        return both, swap_seq(both, 1)

    def out_rows(part):
        resid = lax.dynamic_index_in_dim(
            mids[part][4].reshape(RANKS, rows_part, model), chunk, 0, keepdims=False
        )
        return (resid + (ffn[part][0] + ffn_far[part].astype(FULL))).astype(LOW)

    mids, chip, chip_far = [], [], []
    for part in range(SPLIT):
        mid = middle(
            info, xs, cs, pieces[part], outs, gain_two, w_ffn, part,
            None if part == 0 else mids[0][5],
        )
        if part == 0:
            mid, pieces[1] = together(mid, pieces[1])
        else:
            mid, chip_far[0] = together(mid, chip_far[0])
        mids.append(mid)
        chip.append(chip_sum(mid, swap_seq(mid[3], 1)))
        chip_far.append(swap_seq(chip[part], 2))
        if part == 0:
            pieces[1] = after(pieces[1], chip[0])

    sums = [whole_sum(0)]
    ffn = [after(mid[:2], chip[1]) for mid in mids]
    ffn = [f[0].astype(FULL) + swap_seq(f[1], 1).astype(FULL) for f in ffn]
    ffn_far = jnp.stack([f[1].astype(LOW) for f in ffn])
    g_ffn = after(mids[1][5], chip[1])
    g_ffn = lax.psum_scatter(g_ffn, "dp", scatter_dimension=0, tiled=True)
    sums[0] = after(sums[0], ffn_far)
    ffn_far = swap_seq(ffn_far, 2)

    args = (gain_two, out_wide)
    back = [
        attend_back(
            info, qa, ka, kt, va, sums[0], mids[0][4], cs, *args, *attended[0][1:], near, 0,
            512, per, (),
        )
    ]
    back[0], chip_far[1], ffn_far, g_ffn = together(back[0], chip_far[1], ffn_far, g_ffn)
    sums.append(whole_sum(1))
    out_own = jnp.concatenate([out_rows(part) for part in range(SPLIT)], axis=0)
    out_own = after(out_own, sums[1][0])
    g_ffn = regroup(g_ffn, IDLE)
    given = back[0][1:5]
    sums[1] = after(sums[1], out_own)
    back.append(
        attend_back(
            info, qa, ka, kt, va, sums[1], mids[1][4], cs, *args, *attended[1][1:], near, 1,
            512, per, given,
        )
    )
    back[1], g_ffn = together(back[1], g_ffn)
    outputs = lax.all_gather(after(out_own, g_ffn), "tensor")
    g_core = swap_seq(g_ffn, 1)
    dk, dv, d_near = back[1][1:4]
    resids = [
        lax.dynamic_index_in_dim(
            mid[4].reshape(RANKS, rows_part, model), chunk, 0, keepdims=False
        )
        for mid in mids
    ]

    dqs = [b[0] for b in back]
    keep, give = tail(info, dqs, dk, dv, w_wide)
    core = swap_seq(give, 1)
    found = bucket_sums(after(d_near, give))
    found, core, g_core = together(found, core, g_core)
    far_low = (keep[1::2].astype(FULL) + core[1::2].astype(FULL)).astype(LOW)
    far = swap_seq(far_low, 2)
    dqs, dk, dv, found, g_core = after((dqs, dk, dv, found, g_core), far_low)
    near_sum = jnp.sum(found, axis=2).T
    tile_sum = back[1][5][:, :, HEAD : HEAD + RANKS * per]
    tiles = tile_at(jnp.arange(RANKS * per), per)
    left = tiles[:, None] < tiles[None, :] - 1
    right = tiles[:, None] > tiles[None, :] + 1
    left_sum = jnp.sum(jnp.where(left, tile_sum, 0.0), axis=(1, 2))
    right_sum = jnp.sum(jnp.where(right, tile_sum, 0.0), axis=(1, 2))
    spot = jnp.arange(BUCKETS)[:, None]
    d_table = near_sum + jnp.where(spot == BUCKETS // 2 - 1, left_sum[None], 0.0)
    d_table = d_table + jnp.where(spot == BUCKETS - 1, right_sum[None], 0.0)
    d_table = d_table.reshape(model // size, flat.shape[0])
    d_table = jnp.pad(d_table, ((0, 0), (0, size - flat.shape[0]))).reshape(1, model)
    extra = jnp.concatenate([d_table, jnp.zeros((EXTRA - 1, model), FULL)], axis=0)
    g_all = weights(dqs, dk, dv, normed, back[1][4], extra.astype(LOW))
    g_all, far = together(g_all, far)
    x_parts, c_parts = cut(x_own).astype(FULL), cut(c_own).astype(FULL)
    own, gain_attn_part, gain_ffn_part = [], 0.0, 0.0
    for part in range(SPLIT):
        total_two = lax.dynamic_index_in_dim(sums[part][0], chunk // 2, 0, keepdims=False)
        total_two = total_two.astype(FULL)
        unit_two, scale_two = normalize(resids[part])
        gain_ffn_part = gain_ffn_part + jnp.sum(total_two * unit_two, axis=0)
        d_resid = c_parts[part] + norm_back(total_two, unit_two, scale_two, gain_two)
        unit, scale = normalize(x_parts[part])
        grad = keep[2 * part].astype(FULL) + core[2 * part].astype(FULL)
        grad = grad + far[part].astype(FULL)
        gain_attn_part = gain_attn_part + jnp.sum(grad * unit, axis=0)
        own.append((d_resid + norm_back(grad, unit, scale, gain_one)).astype(LOW))
    own = jnp.concatenate(own, axis=0)
    gains = jnp.stack([gain_attn_part, gain_ffn_part])
    g_ffn = (g_ffn.astype(FULL) + g_core.astype(FULL)).astype(LOW)
    g_all, g_ffn, gains = after((g_all, g_ffn, gains), own)

    held = jnp.zeros((slots, rows_here, model), LOW)
    home = by_rank(HOME, rank)
    held = lax.dynamic_update_slice(held, own[None], (home, 0, 0))
    one = step_one(own)
    gains = sum_pair(sum_pair(gains, 1), 2)
    g_all = scatter_dp(g_all, 1)
    g_far = swap_seq(after(g_ffn, gains), 2)
    one, g_all, gains, outputs = together(one, g_all, gains, outputs)

    two = step_two(one)
    held = keep_step(held, own, one, PLACES[0], rank)
    own = jnp.where(rank == IDLE, one[0], own)
    g_all = regroup(g_all, IDLE)
    gains = gains + swap_dp(gains) if lax.axis_size("dp") == 2 else lax.psum(gains, "dp")
    gains = gains + along_tensor(gains, [(t, t ^ 1) for t in range(RANKS)])
    g_ffn = g_ffn.astype(FULL) + g_far.astype(FULL)
    g_all = sum_pair(g_all, 1).astype(LOW)
    outputs = jnp.stack([outputs[0], outputs[2], outputs[3]])
    two, g_all, gains, held, g_ffn, outputs = together(two, g_all, gains, held, g_ffn, outputs)

    three = step_three(two)
    held = keep_step(held, own, two, PLACES[1], rank)
    g_all = sum_pair(g_all, 2)
    gains = gains + along_tensor(gains, [(t, t ^ 2) for t in range(RANKS)])
    grad_in, grad_down = g_ffn[:, :hid], g_ffn[:, hid:].T
    three, g_all, gains, held, grad_in, grad_down, outputs = together(
        three, g_all, gains, held, grad_in, grad_down, outputs
    )
    grad_inputs = keep_step(held, own, three, PLACES[2], rank)
    gains = lax.dynamic_slice_in_dim(gains, mine * size, size, 1)
    grad_gain_attn, grad_gain_ffn = gains[0], gains[1]
    grad_table = g_all[main, : flat.shape[0]].reshape(bias_table.shape)
    return (
        outputs,
        grad_inputs,
        grad_gain_attn,
        g_all[:narrow].T,
        g_all[narrow : 2 * narrow].T,
        g_all[2 * narrow : 3 * narrow].T,
        g_all[3 * narrow : main],
        grad_table,
        grad_gain_ffn,
        grad_in,
        grad_down,
    )


def solution(mesh):
    in_specs = (
        P("dp", "seq", None),
        P("dp"),
        P("dp"),
        P("dp", "tensor"),
        P("dp", "tensor"),
        P("dp", "tensor"),
        P("tensor", "dp"),
        P("dp", "tensor"),
        P("dp"),
        P("dp", "tensor"),
        P("tensor", "dp"),
        P("dp", "seq", None),
    )
    out_specs = (
        P("dp", "seq", None),
        P("dp", "seq", None),
        P("dp"),
        P("dp", "tensor"),
        P("dp", "tensor"),
        P("dp", "tensor"),
        P("tensor", "dp"),
        P("dp", "tensor"),
        P("dp"),
        P("dp", "tensor"),
        P("tensor", "dp"),
    )
    return jax.shard_map(body, mesh=mesh, in_specs=in_specs, out_specs=out_specs, check_vma=False)
```

```python
import functools

import jax
import jax.numpy as jnp
from jax import lax
from jax.experimental import pallas as pl
from jax.experimental.pallas import tpu as pltpu
from jax.sharding import PartitionSpec as P

HEAD = 64
BUCKETS = 32
EPSILON = 1e-06
LIMITS = (12, 16, 23, 32, 46, 64, 91)
LOW = jnp.bfloat16
FULL = jnp.float32
TILE = 128
RANKS = 4
MIX = (0, 2, 1, 3)
IDLE = 1
SPLIT = 2
EXTRA = 32
SHORTEN = 64
GELU_A = 0.7978845608028654
GELU_B = 0.044715
KERNEL_MEMORY = 60 * 1024 * 1024


def bucket_of(relative):
    sign_part = jnp.where(relative > 0, 16, 0).astype(jnp.int32)
    distance = jnp.abs(relative)
    far_part = jnp.full(distance.shape, 8, jnp.int32)
    for limit in LIMITS:
        far_part = far_part + (distance >= limit).astype(jnp.int32)
    return sign_part + jnp.where(distance < 8, distance, far_part)


def dot_nn(left, right):
    return lax.dot_general(left, right, (((1,), (0,)), ((), ())), preferred_element_type=FULL)


def dot_nt(left, right):
    return lax.dot_general(left, right, (((1,), (1,)), ((), ())), preferred_element_type=FULL)


def dot_tn(left, right):
    return lax.dot_general(left, right, (((0,), (0,)), ((), ())), preferred_element_type=FULL)


def tile_place(tile, per):
    sub = per // SPLIT
    return ((tile % per) // sub) * (RANKS * sub) + (tile // per) * sub + tile % sub


def tile_at(place, per):
    sub = per // SPLIT
    return ((place // sub) % RANKS) * per + (place // (RANKS * sub)) * sub + place % sub


def cost(flops):
    return pl.CostEstimate(flops=flops // SHORTEN, bytes_accessed=0, transcendentals=0)


def params():
    return pltpu.CompilerParams(vmem_limit_bytes=KERNEL_MEMORY)


def whole_spec(shape):
    return pl.BlockSpec(shape, lambda i, c: tuple(0 for _ in shape))


def near_bucket(d):
    key = lax.broadcasted_iota(jnp.int32, (TILE, TILE), 0)
    query = lax.broadcasted_iota(jnp.int32, (TILE, TILE), 1)
    return bucket_of(TILE * d + key - query)


def buckets_near(d):
    half = BUCKETS // 2
    if d < 0:
        return range(half)
    return range(half, BUCKETS) if d > 0 else range(BUCKETS)


def pick_block(index, refs):
    value = refs[0][...]
    for k in range(1, len(refs)):
        value = jnp.where(index == k, refs[k][...], value)
    return value


def project_kernel(
    heads, per, info, x0, x1, x2, x3, gain_ref, w_ref, table, normed, qa, ka, va, kt, vt, near
):
    step = pl.program_id(0)

    @pl.when(step == 0)
    def _():
        for d in (-1, 0, 1):
            buckets = near_bucket(d)
            for h in range(heads):
                tile = jnp.zeros((TILE, TILE), FULL)
                for b in buckets_near(d):
                    tile = jnp.where(buckets == b, table[b, h], tile)
                near[h, d + 1] = tile

    rows = RANKS * x0.shape[0]
    refs = (x0, x1, x2, x3)
    x = jnp.concatenate([pick_block(info[k], refs) for k in range(RANKS)], axis=0).astype(FULL)
    scale = lax.rsqrt(jnp.mean(x * x, axis=-1, keepdims=True) + EPSILON)
    xn = (x * scale * gain_ref[...]).astype(LOW)
    normed[...] = xn
    y = dot_nt(xn, w_ref[...])
    row = lax.broadcasted_iota(jnp.int32, (rows, TILE), 0)
    lane = lax.broadcasted_iota(jnp.int32, (rows, TILE), 1) - HEAD
    place = step * (rows // TILE) + row // TILE
    count = RANKS * per
    is_tile = jnp.logical_and(lane >= 0, lane < count)
    here = tile_at(place, per)
    there = tile_at(jnp.where(is_tile, lane, 0), per)
    position = here * TILE + row % TILE
    q_extra = jnp.where(jnp.logical_or(lane == place, lane == count), 1.0, 0.0)
    v_extra = jnp.where(lane == 0, 1.0, 0.0)
    dead = jnp.where(jnp.logical_and(lane == count, position >= info[RANKS]), -1e30, 0.0)
    left = jnp.logical_and(is_tile, here < there - 1)
    right = jnp.logical_and(is_tile, here > there + 1)
    wide = heads * TILE
    for h in range(heads):
        before, behind = table[BUCKETS // 2 - 1, h], table[BUCKETS - 1, h]
        k_extra = jnp.where(left, before, jnp.where(right, behind, dead))
        at = slice(TILE * h, TILE * h + TILE)
        qa[:, at] = (y[:, at] + q_extra).astype(LOW)
        kh = y[:, wide + TILE * h : wide + TILE * h + TILE] + k_extra
        vh = y[:, 2 * wide + TILE * h : 2 * wide + TILE * h + TILE] + v_extra
        ka[:, at] = kh.astype(LOW)
        va[:, at] = vh.astype(LOW)
        kt[at, :] = kh.T.astype(LOW)
        vt[at, :] = vh.T.astype(LOW)


def project(info, xs, gain, w_qkv, table, heads, per):
    total = RANKS * xs[0].shape[0]
    rows = xs[0].shape[0] // SPLIT
    width = xs[0].shape[1]
    row_block = lambda w: pl.BlockSpec((RANKS * rows, w), lambda i, c: (i, 0))
    col_block = lambda w: pl.BlockSpec((w, RANKS * rows), lambda i, c: (0, i))
    wide = heads * TILE
    return pl.pallas_call(
        functools.partial(project_kernel, heads, per),
        grid_spec=pltpu.PrefetchScalarGridSpec(
            num_scalar_prefetch=1,
            grid=(SPLIT,),
            in_specs=[pl.BlockSpec((rows, width), lambda i, c: (i, 0))] * RANKS
            + [
                whole_spec(gain.shape),
                whole_spec(w_qkv.shape),
                pl.BlockSpec(memory_space=pltpu.SMEM),
            ],
            out_specs=[
                row_block(width),
                row_block(wide),
                row_block(wide),
                row_block(wide),
                col_block(wide),
                col_block(wide),
                whole_spec((heads, 3, TILE, TILE)),
            ],
        ),
        out_shape=[
            jax.ShapeDtypeStruct((total, width), LOW),
            jax.ShapeDtypeStruct((total, wide), LOW),
            jax.ShapeDtypeStruct((total, wide), LOW),
            jax.ShapeDtypeStruct((total, wide), LOW),
            jax.ShapeDtypeStruct((wide, total), LOW),
            jax.ShapeDtypeStruct((wide, total), LOW),
            jax.ShapeDtypeStruct((heads, 3, TILE, TILE), FULL),
        ],
        compiler_params=params(),
        name="project",
        cost_estimate=cost(8 * total * width * heads * HEAD),
    )(info, *xs, gain, w_qkv, table)


def near_tiles(first_place, tiles, per, visit):
    count = RANKS * per
    for u in range(tiles):
        here = tile_at(first_place + u, per)
        for d in (-1, 0, 1):
            there = here + d
            valid = jnp.logical_and(there >= 0, there < count)
            place = tile_place(jnp.clip(there, 0, count - 1), per)
            rows = pl.ds(pl.multiple_of(place * TILE, TILE), TILE)
            visit(d + 1, rows, slice(u * TILE, u * TILE + TILE), jnp.where(valid, 1.0, 0.0))


def score_block(h, first_place, per, qa, ka, near, s_ref):
    bq = qa.shape[0]
    at = slice(TILE * h, TILE * h + TILE)
    s_ref[h] = dot_nt(ka[:, at], qa[:, at])

    def add(d, rows, cols, valid):
        s_ref[h, rows, cols] = s_ref[h, rows, cols] + near[h, d] * valid

    near_tiles(first_place, bq // TILE, per, add)


def forward_kernel(heads, per, offset, qa, ka, vt, near, mixed, ot, lse, s_ref):
    bq = qa.shape[0]
    first = (pl.program_id(0) + offset) * (bq // TILE)
    for h in range(heads):
        score_block(h, first, per, qa, ka, near, s_ref)
    parts = []
    for h in range(heads):
        s = s_ref[h]
        top = jnp.max(s, axis=0, keepdims=True)
        p = jnp.exp(s - top).astype(LOW)
        o = dot_nn(vt[TILE * h : TILE * h + TILE, :], p)
        total = o[HEAD : HEAD + 1]
        o = o[:HEAD] * (1.0 / total)
        ot[HEAD * h : HEAD * h + HEAD, :] = o
        lse[h : h + 1, :] = top + jnp.log(total)
        parts.append(o.T)
    mixed[...] = jnp.concatenate(parts, axis=1).astype(LOW)


def attend(qa, ka, vt, near, part, bq, per):
    total, wide = ka.shape
    heads = wide // TILE
    span = total // SPLIT
    steps = span // bq
    offset = part * steps
    full = lambda shape: pl.BlockSpec(shape, lambda i: tuple(0 for _ in shape))
    width = heads * HEAD
    return pl.pallas_call(
        functools.partial(forward_kernel, heads, per, offset),
        grid=(steps,),
        in_specs=[
            pl.BlockSpec((bq, wide), lambda i: (i + offset, 0)),
            full(ka.shape),
            full(vt.shape),
            full(near.shape),
        ],
        out_specs=[
            pl.BlockSpec((bq, width), lambda i: (i, 0)),
            pl.BlockSpec((width, bq), lambda i: (0, i)),
            pl.BlockSpec((8, bq), lambda i: (0, i)),
        ],
        out_shape=[
            jax.ShapeDtypeStruct((span, width), LOW),
            jax.ShapeDtypeStruct((width, span), FULL),
            jax.ShapeDtypeStruct((8, span), FULL),
        ],
        scratch_shapes=[pltpu.VMEM((heads, total, bq), FULL)],
        compiler_params=params(),
        name="attend",
        cost_estimate=cost(20 * heads * span * total * HEAD),
    )(qa, ka, vt, near)


def middle_kernel(
    first, info, x0, x1, x2, x3, c0, c1, c2, c3, m0, m1, m2, m3, w0, w1, w2, w3,
    gain, w_ffn, *refs
):
    given, (f_keep, f_give, d_keep, d_give, resid_out, grads_out, grads) = refs[:-7], refs[-7:]
    step = pl.program_id(0)
    hid = w_ffn.shape[1] // 2

    @pl.when(step == 0)
    def _():
        grads[...] = jnp.zeros_like(grads) if first else given[0][...].astype(FULL)

    attn = dot_nn(m0[...], w0[...]) + dot_nn(m1[...], w1[...])
    attn = attn + dot_nn(m2[...], w2[...]) + dot_nn(m3[...], w3[...])
    resid = pick_block(info[step], (x0, x1, x2, x3)).astype(FULL) + attn
    resid_out[...] = resid
    scale = lax.rsqrt(jnp.mean(resid * resid, axis=-1, keepdims=True) + EPSILON)
    normed = (resid * scale * gain[...]).astype(LOW)
    hidden = dot_nn(normed, w_ffn[:, :hid])
    grad = pick_block(info[step], (c0, c1, c2, c3))
    d_active = dot_nn(grad, w_ffn[:, hid:])
    square = hidden * hidden
    th = jnp.tanh(GELU_A * hidden * (1.0 + GELU_B * square))
    half = 0.5 * (1.0 + th)
    active = (hidden * half).astype(LOW)
    slope = half + 0.5 * hidden * (1.0 - th * th) * (GELU_A * (1.0 + (3.0 * GELU_B) * square))
    d_hidden = (d_active * slope).astype(LOW)
    dn = dot_nt(d_hidden, w_ffn[:, :hid]).astype(LOW)
    ffn = dot_nt(active, w_ffn[:, hid:]).astype(LOW)

    @pl.when(info[step] % 2 == 0)
    def _():
        d_keep[0] = dn
        f_keep[0] = ffn

    @pl.when(info[step] % 2 == 1)
    def _():
        d_give[0] = dn
        f_give[0] = ffn

    grads[:, :hid] += dot_tn(normed, d_hidden)
    grads[:, hid:] += dot_tn(grad, active)

    @pl.when(step == RANKS - 1)
    def _():
        grads_out[...] = grads[...].astype(LOW)


def middle(info, xs, cs, pieces, outs, gain, w_ffn, part, given):
    rows, width = xs[0].shape[0] // SPLIT, xs[0].shape[1]
    narrow = pieces[0].shape[1]
    own_block = pl.BlockSpec((rows, width), lambda i, c: (part, 0))
    piece_block = pl.BlockSpec((rows, narrow), lambda i, c: (i, 0))
    rel_block = pl.BlockSpec((1, rows, width), lambda i, c: (c[i] // 2, 0, 0))
    pair_block = pl.BlockSpec((1, rows, width), lambda i, c: (i // 2, 0, 0))
    extra = () if given is None else (given,)
    two = jax.ShapeDtypeStruct((2, rows, width), LOW)
    return pl.pallas_call(
        functools.partial(middle_kernel, given is None),
        grid_spec=pltpu.PrefetchScalarGridSpec(
            num_scalar_prefetch=1,
            grid=(RANKS,),
            in_specs=[own_block] * (2 * RANKS)
            + [piece_block] * RANKS
            + [whole_spec(outs[0].shape)] * RANKS
            + [whole_spec(v.shape) for v in (gain, w_ffn) + extra],
            out_specs=[
                rel_block,
                rel_block,
                pair_block,
                pair_block,
                pl.BlockSpec((rows, width), lambda i, c: (i, 0)),
                whole_spec(w_ffn.shape),
            ],
            scratch_shapes=[pltpu.VMEM(w_ffn.shape, FULL)],
        ),
        out_shape=[two, two, two, two]
        + [
            jax.ShapeDtypeStruct((RANKS * rows, width), FULL),
            jax.ShapeDtypeStruct(w_ffn.shape, LOW),
        ],
        compiler_params=params(),
        name="middle",
        cost_estimate=cost(20 * RANKS * rows * width * w_ffn.shape[1] // 2),
    )(info, *xs, *cs, *pieces, *outs, gain, w_ffn, *extra)


def backward_kernel(
    per, offset, kc, info, qa, ka, kt, va, sum_mine, sum_other, resid_ref,
    c0, c1, c2, c3, gain, wo, ot, lse, near, *refs
):
    given = refs[:-11]
    dq, dk, dv, d_near, g_out, tiles, s_ref, ds_ref, dk_acc, dv_acc, d_rows = refs[-11:]
    head, step = pl.program_id(0), pl.program_id(1)
    bq = qa.shape[0]
    total = ka.shape[0]
    count = RANKS * per
    first = (step + offset) * (bq // TILE)
    here = pl.ds(pl.multiple_of(step * bq, bq), bq)

    @pl.when(step == 0)
    def _():
        if len(given) > 0:
            dk_acc[...] = given[0][...]
            dv_acc[...] = given[1][...]
            d_near[...] = given[2][...]
            g_out[...] = given[3][...]
        else:
            dk_acc[...] = jnp.zeros_like(dk_acc)
            dv_acc[...] = jnp.zeros_like(dv_acc)
            d_near[...] = jnp.zeros_like(d_near)
            g_out[...] = jnp.zeros_like(g_out)

    @pl.when(head == 0)
    def _():
        even = info[0] % 2 == 0
        blocks = []
        for k in range(sum_mine.shape[0]):
            mine, other = sum_mine[k], sum_other[k]
            blocks += [jnp.where(even, mine, other), jnp.where(even, other, mine)]
        d_norm = jnp.concatenate(blocks, axis=0).astype(FULL)
        cot = jnp.concatenate(
            [
                pick_block(info[len(blocks) * step + k], (c0, c1, c2, c3))
                for k in range(len(blocks))
            ],
            axis=0,
        ).astype(FULL)
        resid = resid_ref[...]
        scale = lax.rsqrt(jnp.mean(resid * resid, axis=-1, keepdims=True) + EPSILON)
        unit = resid * scale
        along = d_norm * gain[...]
        rows = cot + scale * (along - unit * jnp.mean(along * unit, axis=-1, keepdims=True))
        d_rows[here, :] = rows.astype(LOW)

    s_ref[...] = dot_nt(ka[...], qa[...])

    def add(d, rows, cols, valid):
        s_ref[rows, cols] = s_ref[rows, cols] + near[0, d] * valid

    near_tiles(first, bq // TILE, per, add)
    grad = d_rows[here, :]
    do = dot_nt(grad, wo[...]).astype(LOW)
    do_t = dot_nt(wo[...], grad).astype(LOW).astype(FULL)
    o_t = ot[...]
    g_out[...] += dot_nn(o_t.astype(LOW), grad)
    delta = jnp.sum(do_t[:HEAD] * o_t, axis=0, keepdims=True)
    lse_row = lse[pl.ds(head, 1), :]
    dq_t = jnp.zeros((TILE, bq), FULL)
    for c in range(total // kc):
        rows = slice(kc * c, kc * c + kc)
        p = jnp.exp(s_ref[rows, :] - lse_row)
        d_p = dot_nt(va[rows, :], do)
        d_s = (p * (d_p - delta)).astype(LOW)
        ds_ref[rows, :] = d_s
        dv_acc[rows, :] += dot_nn(p.astype(LOW), do)
        dk_acc[rows, :] += dot_nn(d_s, qa[...])
        dq_t += dot_nn(kt[:, rows], d_s)
    lane = lax.broadcasted_iota(jnp.int32, (bq, TILE), 1)
    dq[...] = jnp.where(lane < HEAD, dq_t.T, 0.0).astype(LOW)

    def collect(d, rows, cols, valid):
        d_near[0, d] += ds_ref[rows, cols].astype(FULL) * valid

    near_tiles(first, bq // TILE, per, collect)

    @pl.when(step == pl.num_programs(1) - 1)
    def _():
        if dk.dtype == FULL:
            dk[...] = dk_acc[...]
            dv[...] = dv_acc[...]
        else:
            side = lax.broadcasted_iota(jnp.int32, (total, TILE), 1)
            dk[...] = jnp.where(side < HEAD, dk_acc[...], 0.0).astype(LOW)
            dv[...] = jnp.where(side < HEAD, dv_acc[...], 0.0).astype(LOW)
        sums = [
            jnp.sum(dk_acc[k * TILE : k * TILE + TILE, :], axis=0, keepdims=True)
            for k in range(count)
        ]
        tiles[0] = jnp.concatenate(sums, axis=0)


def attend_back(
    info, qa, ka, kt, va, sums, resid, cs, gain, wo, ot, lse, near, part, kc, per, given
):
    total, wide = ka.shape
    heads = wide // TILE
    model = resid.shape[1]
    rows = total // SPLIT // RANKS
    bq = RANKS * rows
    span = total // SPLIT
    steps = span // bq
    offset = part * steps
    last = part == SPLIT - 1
    once = lambda h, i: jnp.where(h == 0, i, steps - 1)
    head_cols = pl.BlockSpec((total, TILE), lambda h, i, c: (0, h))
    near_block = pl.BlockSpec((1, 3, TILE, TILE), lambda h, i, c: (h, 0, 0, 0))
    out_block = pl.BlockSpec((HEAD, model), lambda h, i, c: (h, 0))
    kind = LOW if last else FULL
    full = lambda shape: pl.BlockSpec(shape, lambda h, i, c: tuple(0 for _ in shape))
    return pl.pallas_call(
        functools.partial(backward_kernel, per, offset, kc),
        grid_spec=pltpu.PrefetchScalarGridSpec(
            num_scalar_prefetch=1,
            grid=(heads, steps),
            in_specs=[
                pl.BlockSpec((bq, TILE), lambda h, i, c: (i + offset, h)),
                head_cols,
                pl.BlockSpec((TILE, total), lambda h, i, c: (h, 0)),
                head_cols,
            ]
            + [pl.BlockSpec((2, rows, model), lambda h, i, c: (once(h, i), 0, 0))] * 2
            + [pl.BlockSpec((bq, model), lambda h, i, c: (once(h, i), 0))]
            + [pl.BlockSpec((rows, model), lambda h, i, c: (part, 0))] * RANKS
            + [
                full(gain.shape),
                pl.BlockSpec((TILE, model), lambda h, i, c: (h, 0)),
                pl.BlockSpec((HEAD, bq), lambda h, i, c: (h, i)),
                pl.BlockSpec((8, bq), lambda h, i, c: (0, i)),
                near_block,
            ]
            + ([] if len(given) == 0 else [head_cols, head_cols, near_block, out_block]),
            out_specs=[
                pl.BlockSpec((bq, TILE), lambda h, i, c: (i, h)),
                head_cols,
                head_cols,
                near_block,
                out_block,
                pl.BlockSpec((1, RANKS * per, TILE), lambda h, i, c: (h, 0, 0)),
            ],
            scratch_shapes=[
                pltpu.VMEM((total, bq), FULL),
                pltpu.VMEM((total, bq), LOW),
                pltpu.VMEM((total, TILE), FULL),
                pltpu.VMEM((total, TILE), FULL),
                pltpu.VMEM((span, model), LOW),
            ],
        ),
        out_shape=[
            jax.ShapeDtypeStruct((span, wide), LOW),
            jax.ShapeDtypeStruct((total, wide), kind),
            jax.ShapeDtypeStruct((total, wide), kind),
            jax.ShapeDtypeStruct((heads, 3, TILE, TILE), FULL),
            jax.ShapeDtypeStruct((heads * HEAD, model), FULL),
            jax.ShapeDtypeStruct((heads, RANKS * per, TILE), FULL),
        ],
        compiler_params=params(),
        name="attend_back",
        cost_estimate=cost(40 * heads * span * total * HEAD),
    )(info, qa, ka, kt, va, *sums, resid, *cs, gain, wo, ot, lse, near, *given)


def bucket_kernel(d_near, out):
    heads = d_near.shape[0]
    found = [[jnp.zeros((1, TILE), FULL)] * BUCKETS for _ in range(heads)]
    for d in (-1, 0, 1):
        buckets = near_bucket(d)
        for b in buckets_near(d):
            here = buckets == b
            for h in range(heads):
                found[h][b] = found[h][b] + jnp.sum(
                    jnp.where(here, d_near[h, d + 1], 0.0), axis=0, keepdims=True
                )
    for h in range(heads):
        out[h] = jnp.concatenate(found[h], axis=0)


def bucket_sums(d_near):
    heads = d_near.shape[0]
    return pl.pallas_call(
        bucket_kernel,
        out_shape=jax.ShapeDtypeStruct((heads, BUCKETS, TILE), FULL),
        compiler_params=params(),
        name="bucket_sums",
    )(d_near)


def tail_kernel(info, dq0, dq1, dk, dv, w_ref, keep, give):
    wide = dk.shape[1]
    dq = pick_block(pl.program_id(0), (dq0, dq1))
    out = dot_nn(dq, w_ref[:wide, :]) + dot_nn(dk[...], w_ref[wide : 2 * wide, :])
    out = (out + dot_nn(dv[...], w_ref[2 * wide :, :])).astype(LOW)
    rows = out.shape[0] // RANKS
    even = info[0] % 2 == 0
    low = info[0] // 2 == 0
    parts = [out[k * rows : k * rows + rows] for k in range(RANKS)]
    kept = [jnp.where(even, parts[k], parts[k + 1]) for k in (0, 2)]
    given = [jnp.where(even, parts[k + 1], parts[k]) for k in (0, 2)]
    keep[0], keep[1] = jnp.where(low, kept[0], kept[1]), jnp.where(low, kept[1], kept[0])
    give[0], give[1] = jnp.where(low, given[0], given[1]), jnp.where(low, given[1], given[0])


def tail(info, dqs, dk, dv, w_wide):
    total, wide = dk.shape
    model = w_wide.shape[1]
    span = total // SPLIT
    rows = span // RANKS
    rel_block = pl.BlockSpec((2, rows, model), lambda i, c: (i, 0, 0))
    return pl.pallas_call(
        tail_kernel,
        grid_spec=pltpu.PrefetchScalarGridSpec(
            num_scalar_prefetch=1,
            grid=(SPLIT,),
            in_specs=[
                whole_spec((span, wide)),
                whole_spec((span, wide)),
                pl.BlockSpec((span, wide), lambda i, c: (i, 0)),
                pl.BlockSpec((span, wide), lambda i, c: (i, 0)),
                whole_spec(w_wide.shape),
            ],
            out_specs=[rel_block, rel_block],
        ),
        out_shape=[jax.ShapeDtypeStruct((2 * SPLIT, rows, model), LOW)] * 2,
        compiler_params=params(),
        name="tail",
        cost_estimate=cost(6 * total * wide * model),
    )(info, *dqs, dk, dv, w_wide)


def weights_kernel(steps, dq0, dq1, dk, dv, normed, g_out, extra, out, acc):
    step = pl.program_id(0)

    @pl.when(step == 0)
    def _():
        acc[...] = jnp.zeros_like(acc)

    dq = pick_block(step // (steps // 2), (dq0, dq1))
    acc[...] += dot_tn(jnp.concatenate([dq, dk[...], dv[...]], axis=1), normed[...])

    @pl.when(step == steps - 1)
    def _():
        count = acc.shape[0] // TILE
        for j in range(count):
            out[j * HEAD : j * HEAD + HEAD, :] = acc[j * TILE : j * TILE + HEAD, :].astype(LOW)
        base = count * HEAD
        out[base : base + g_out.shape[0], :] = g_out[...].astype(LOW)
        out[base + g_out.shape[0] :, :] = extra[...]


def weights(dqs, dk, dv, normed, g_out, extra):
    total, wide = dk.shape
    model = normed.shape[1]
    steps = 4
    rows = total // steps
    half = steps // 2
    full = lambda shape: pl.BlockSpec(shape, lambda i: tuple(0 for _ in shape))
    block = lambda w: pl.BlockSpec((rows, w), lambda i: (i, 0))
    out_rows = 3 * wide * HEAD // TILE + g_out.shape[0] + extra.shape[0]
    return pl.pallas_call(
        functools.partial(weights_kernel, steps),
        grid=(steps,),
        in_specs=[
            pl.BlockSpec((rows, wide), lambda i: (jnp.minimum(i, half - 1), 0)),
            pl.BlockSpec((rows, wide), lambda i: (jnp.maximum(i - half, 0), 0)),
            block(wide),
            block(wide),
            block(model),
            full(g_out.shape),
            full(extra.shape),
        ],
        out_specs=full((out_rows, model)),
        out_shape=jax.ShapeDtypeStruct((out_rows, model), LOW),
        scratch_shapes=[pltpu.VMEM((3 * wide, model), FULL)],
        compiler_params=params(),
        name="weights",
        cost_estimate=cost(6 * total * wide * model),
    )(*dqs, dk, dv, normed, g_out, extra)


def together(*values):
    return lax.optimization_barrier(values)


def after(value, *given):
    return lax.optimization_barrier((value,) + given)[0]


def swap_seq(value, bit):
    return lax.ppermute(value, "seq", [(i, i ^ bit) for i in range(RANKS)])


def regroup(value, skip):
    pairs = []
    for s in range(RANKS):
        for t in range(RANKS):
            if t != skip and MIX[s] != 0:
                pairs.append((s * RANKS + t, s * RANKS + (t ^ MIX[s])))
    moved = lax.ppermute(value, ("seq", "tensor"), pairs)
    return jnp.where(lax.axis_index("seq") == MIX.index(0), value, moved)


def along_tensor(value, pairs):
    return lax.ppermute(value, "tensor", pairs)


def step_one(own):
    return along_tensor(own, [(0, 1), (2, 3)]), along_tensor(own, [(3, 2), (2, 1)])


def step_two(moved):
    return along_tensor(moved[0], [(1, 2)]), along_tensor(moved[1], [(2, 1), (1, 0)])


def step_three(moved):
    return along_tensor(moved[0], [(2, 3)]), along_tensor(moved[1], [(1, 0)])


HOME = (0, 0, 1, 2)
PLACES = (
    ((None, 0, None, 1), (None, 1, 2, None)),
    ((None, None, 0, None), (1, 2, None, None)),
    ((None, None, None, 0), (2, None, None, None)),
)


def by_rank(values, rank):
    out = values[0]
    for index in range(1, len(values)):
        out = jnp.where(rank == index, values[index], out)
    return out


def keep_step(held, own, moved, places, rank):
    for value, place in zip(moved, places):
        got = by_rank([p is not None for p in place], rank)
        at = by_rank([HOME[k] if p is None else p for k, p in enumerate(place)], rank)
        value = jnp.where(got, value, own)
        held = lax.dynamic_update_slice(held, value[None], (at, 0, 0))
    return held


def swap_dp(value):
    return lax.ppermute(value, "dp", [(0, 1), (1, 0)])


def join_dp(halves, axis):
    if len(halves) == 1:
        return lax.all_gather(halves[0], "dp", axis=axis, tiled=True)
    value, other = halves
    swap = lax.axis_index("dp") == 1
    return jnp.concatenate(
        [jnp.where(swap, other, value), jnp.where(swap, value, other)], axis=axis
    )


def gather_dp(value, axis):
    if lax.axis_size("dp") != 2:
        return join_dp((value,), axis)
    return join_dp((value, swap_dp(value)), axis)


def scatter_dp(value, axis):
    if lax.axis_size("dp") != 2:
        return lax.psum_scatter(value, "dp", scatter_dimension=axis, tiled=True).astype(LOW)
    size = value.shape[axis] // 2
    mine = lax.axis_index("dp")
    keep = lax.dynamic_slice_in_dim(value, mine * size, size, axis)
    give = lax.dynamic_slice_in_dim(value, (1 - mine) * size, size, axis)
    return (keep.astype(FULL) + swap_dp(give.astype(LOW)).astype(FULL)).astype(LOW)


def sum_pair(value, bit):
    return value.astype(FULL) + swap_seq(value, bit).astype(FULL)


def normalize(values):
    scale = lax.rsqrt(jnp.mean(values * values, axis=-1, keepdims=True) + EPSILON)
    return values * scale, scale


def norm_back(grad, unit, scale, gain):
    along = grad * gain
    return scale * (along - unit * jnp.mean(along * unit, axis=-1, keepdims=True))


def body(
    inputs, lengths, gain_attn, w_query, w_key, w_value, w_out, bias_table,
    gain_ffn, w_in, w_down, cotangent,
):
    slots, rows_here, model = inputs.shape
    assert lax.axis_size("seq") == RANKS and lax.axis_size("tensor") == RANKS and slots == 3
    total = RANKS * rows_here
    per = rows_here // TILE
    narrow = w_query.shape[1]
    heads = narrow // HEAD
    hid = w_in.shape[1]
    rank = lax.axis_index("tensor")
    chunk = lax.axis_index("seq")
    mine = lax.axis_index("dp")
    slot = jnp.where(rank == 0, 0, rank - 1)
    length = lax.dynamic_index_in_dim(lengths, slot, 0, keepdims=False)
    order = jnp.bitwise_xor(chunk, jnp.arange(RANKS, dtype=jnp.int32)).astype(jnp.int32)
    info = jnp.concatenate([order, length[None], jnp.zeros((3,), jnp.int32)])
    rows_part = rows_here // SPLIT
    size = gain_attn.shape[0]
    cut = lambda v: v.reshape(SPLIT, rows_part, model)

    x_own = lax.dynamic_index_in_dim(inputs, slot, 0, keepdims=False)
    x_far = swap_seq(x_own, 2)
    x_near = swap_seq(x_own, 1)

    flat = bias_table.reshape(-1)
    small = jnp.stack(
        [gain_attn, gain_ffn, jnp.pad(flat, (0, size - flat.shape[0]))]
        + [jnp.zeros((size,), LOW)] * (EXTRA - 3)
    )
    w_first = after(w_query, x_own)
    pack = jnp.concatenate([w_first.T, w_key.T, w_value.T, w_out, small], axis=0)
    pack = regroup(pack, None)
    w_all = gather_dp(pack, 1)
    main = 4 * narrow
    w_wide = jnp.pad(
        w_all[: 3 * narrow].reshape(3 * heads, HEAD, model), ((0, 0), (0, TILE - HEAD), (0, 0))
    ).reshape(3 * heads * TILE, model)
    gain_one = w_all[main : main + 1].astype(FULL)
    gain_two = w_all[main + 1 : main + 2].astype(FULL)
    table = w_all[main + 2].reshape(-1, size)[:, : flat.shape[0]]
    table = table.reshape(BUCKETS, heads).astype(FULL)
    xs = [x_own, x_near, x_far, swap_seq(x_far, 1)]

    position = chunk * rows_here + jnp.arange(rows_here, dtype=jnp.int32)
    live = jnp.logical_and(position < length, rank != IDLE)
    c_own = lax.dynamic_index_in_dim(cotangent, slot, 0, keepdims=False)
    c_own = jnp.where(live[:, None], c_own, jnp.zeros((), LOW))
    ffn_pack = regroup(after(jnp.concatenate([w_in, w_down.T], axis=1), pack), None)
    c_first = after(c_own, x_far)
    c_far = swap_seq(c_first, 2)

    normed, qa, ka, va, kt, vt, near = project(info, xs, gain_one, w_wide, table, heads, per)

    normed, c_far, ffn_pack = together(normed, c_far, ffn_pack)
    qa, ka, vt, _ = together(qa, ka, vt, normed)
    out_mine = w_all[3 * narrow : main]
    out_near, out_far = swap_seq(out_mine, 1), swap_seq(out_mine, 2)
    ffn_halves = (ffn_pack, swap_dp(ffn_pack)) if lax.axis_size("dp") == 2 else (ffn_pack,)
    cs = [c_own, swap_seq(c_first, 1), c_far, swap_seq(c_far, 1)]
    out_wide = jnp.pad(
        out_mine.reshape(heads, HEAD, model), ((0, 0), (0, TILE - HEAD), (0, 0))
    ).reshape(heads * TILE, model)

    bq = min(1024, total // SPLIT)
    attended = [attend(qa, ka, vt, near, 0, bq, per)]
    attended[0], cs, out_far = together(attended[0], cs, out_far)
    outs = [out_mine, out_near, out_far, swap_seq(out_far, 1)]
    mixed = attended[0][0]
    pieces = [[mixed] + [swap_seq(mixed, bit) for bit in (1, 2, 3)]]

    attended.append(attend(after(qa, mixed), ka, vt, near, 1, bq, per))
    attended[1], pieces[0], outs, ffn_halves = together(
        attended[1], pieces[0], outs, ffn_halves
    )
    w_ffn = join_dp(ffn_halves, 0)
    mixed = attended[1][0]
    pieces.append([mixed] + [swap_seq(mixed, bit) for bit in (1, 2, 3)])

    def chip_sum(mid, core):
        return (mid[2].astype(FULL) + core.astype(FULL)).astype(LOW)

    def whole_sum(part):
        both = chip[part].astype(FULL) + chip_far[part].astype(FULL)
        both = both.astype(LOW)
        return both, swap_seq(both, 1)

    def out_rows(part):
        resid = lax.dynamic_index_in_dim(
            mids[part][4].reshape(RANKS, rows_part, model), chunk, 0, keepdims=False
        )
        return (resid + (ffn[part][0] + ffn_far[part].astype(FULL))).astype(LOW)

    mids, chip, chip_far = [], [], []
    for part in range(SPLIT):
        mid = middle(
            info, xs, cs, pieces[part], outs, gain_two, w_ffn, part,
            None if part == 0 else mids[0][5],
        )
        if part == 0:
            mid, pieces[1] = together(mid, pieces[1])
        else:
            mid, chip_far[0] = together(mid, chip_far[0])
        mids.append(mid)
        chip.append(chip_sum(mid, swap_seq(mid[3], 1)))
        chip_far.append(swap_seq(chip[part], 2))
        if part == 0:
            pieces[1] = after(pieces[1], chip[0])

    sums = [whole_sum(0)]
    ffn = [after(mid[:2], chip[1]) for mid in mids]
    ffn = [f[0].astype(FULL) + swap_seq(f[1], 1).astype(FULL) for f in ffn]
    ffn_far = jnp.stack([f[1].astype(LOW) for f in ffn])
    g_ffn = after(mids[1][5], chip[1])
    g_ffn = lax.psum_scatter(g_ffn, "dp", scatter_dimension=0, tiled=True)
    sums[0] = after(sums[0], ffn_far)
    ffn_far = swap_seq(ffn_far, 2)

    args = (gain_two, out_wide)
    back = [
        attend_back(
            info, qa, ka, kt, va, sums[0], mids[0][4], cs, *args, *attended[0][1:], near, 0,
            512, per, (),
        )
    ]
    back[0], chip_far[1], ffn_far, g_ffn = together(back[0], chip_far[1], ffn_far, g_ffn)
    sums.append(whole_sum(1))
    out_own = jnp.concatenate([out_rows(part) for part in range(SPLIT)], axis=0)
    out_own = after(out_own, sums[1][0])
    g_ffn = regroup(g_ffn, IDLE)
    given = back[0][1:5]
    sums[1] = after(sums[1], out_own)
    back.append(
        attend_back(
            info, qa, ka, kt, va, sums[1], mids[1][4], cs, *args, *attended[1][1:], near, 1,
            512, per, given,
        )
    )
    back[1], g_ffn = together(back[1], g_ffn)
    outputs = lax.all_gather(after(out_own, g_ffn), "tensor")
    g_core = swap_seq(g_ffn, 1)
    dk, dv, d_near = back[1][1:4]
    resids = [
        lax.dynamic_index_in_dim(
            mid[4].reshape(RANKS, rows_part, model), chunk, 0, keepdims=False
        )
        for mid in mids
    ]

    dqs = [b[0] for b in back]
    keep, give = tail(info, dqs, dk, dv, w_wide)
    core = swap_seq(give, 1)
    found = bucket_sums(after(d_near, give))
    found, core, g_core = together(found, core, g_core)
    far_low = (keep[1::2].astype(FULL) + core[1::2].astype(FULL)).astype(LOW)
    far = swap_seq(far_low, 2)
    dqs, dk, dv, found, g_core = after((dqs, dk, dv, found, g_core), far_low)
    near_sum = jnp.sum(found, axis=2).T
    tile_sum = back[1][5][:, :, HEAD : HEAD + RANKS * per]
    tiles = tile_at(jnp.arange(RANKS * per), per)
    left = tiles[:, None] < tiles[None, :] - 1
    right = tiles[:, None] > tiles[None, :] + 1
    left_sum = jnp.sum(jnp.where(left, tile_sum, 0.0), axis=(1, 2))
    right_sum = jnp.sum(jnp.where(right, tile_sum, 0.0), axis=(1, 2))
    spot = jnp.arange(BUCKETS)[:, None]
    d_table = near_sum + jnp.where(spot == BUCKETS // 2 - 1, left_sum[None], 0.0)
    d_table = d_table + jnp.where(spot == BUCKETS - 1, right_sum[None], 0.0)
    d_table = d_table.reshape(model // size, flat.shape[0])
    d_table = jnp.pad(d_table, ((0, 0), (0, size - flat.shape[0]))).reshape(1, model)
    extra = jnp.concatenate([d_table, jnp.zeros((EXTRA - 1, model), FULL)], axis=0)
    g_all = weights(dqs, dk, dv, normed, back[1][4], extra.astype(LOW))
    g_all, far = together(g_all, far)
    x_parts, c_parts = cut(x_own).astype(FULL), cut(c_own).astype(FULL)
    own, gain_attn_part, gain_ffn_part = [], 0.0, 0.0
    for part in range(SPLIT):
        total_two = lax.dynamic_index_in_dim(sums[part][0], chunk // 2, 0, keepdims=False)
        total_two = total_two.astype(FULL)
        unit_two, scale_two = normalize(resids[part])
        gain_ffn_part = gain_ffn_part + jnp.sum(total_two * unit_two, axis=0)
        d_resid = c_parts[part] + norm_back(total_two, unit_two, scale_two, gain_two)
        unit, scale = normalize(x_parts[part])
        grad = keep[2 * part].astype(FULL) + core[2 * part].astype(FULL)
        grad = grad + far[part].astype(FULL)
        gain_attn_part = gain_attn_part + jnp.sum(grad * unit, axis=0)
        own.append((d_resid + norm_back(grad, unit, scale, gain_one)).astype(LOW))
    own = jnp.concatenate(own, axis=0)
    gains = jnp.stack([gain_attn_part, gain_ffn_part])
    g_ffn = (g_ffn.astype(FULL) + g_core.astype(FULL)).astype(LOW)
    g_all, g_ffn, gains = after((g_all, g_ffn, gains), own)

    held = jnp.zeros((slots, rows_here, model), LOW)
    home = by_rank(HOME, rank)
    held = lax.dynamic_update_slice(held, own[None], (home, 0, 0))
    one = step_one(own)
    gains = sum_pair(sum_pair(gains, 1), 2)
    g_all = scatter_dp(g_all, 1)
    g_far = swap_seq(after(g_ffn, gains), 2)
    one, g_all, gains, outputs = together(one, g_all, gains, outputs)

    two = step_two(one)
    held = keep_step(held, own, one, PLACES[0], rank)
    own = jnp.where(rank == IDLE, one[0], own)
    g_all = regroup(g_all, IDLE)
    gains = gains + swap_dp(gains) if lax.axis_size("dp") == 2 else lax.psum(gains, "dp")
    gains = gains + along_tensor(gains, [(t, t ^ 1) for t in range(RANKS)])
    g_ffn = g_ffn.astype(FULL) + g_far.astype(FULL)
    g_all = sum_pair(g_all, 1).astype(LOW)
    outputs = jnp.stack([outputs[0], outputs[2], outputs[3]])
    two, g_all, gains, held, g_ffn, outputs = together(two, g_all, gains, held, g_ffn, outputs)

    three = step_three(two)
    held = keep_step(held, own, two, PLACES[1], rank)
    g_all = sum_pair(g_all, 2)
    gains = gains + along_tensor(gains, [(t, t ^ 2) for t in range(RANKS)])
    grad_in, grad_down = g_ffn[:, :hid], g_ffn[:, hid:].T
    three, g_all, gains, held, grad_in, grad_down, outputs = together(
        three, g_all, gains, held, grad_in, grad_down, outputs
    )
    grad_inputs = keep_step(held, own, three, PLACES[2], rank)
    gains = lax.dynamic_slice_in_dim(gains, mine * size, size, 1)
    grad_gain_attn, grad_gain_ffn = gains[0], gains[1]
    grad_table = g_all[main, : flat.shape[0]].reshape(bias_table.shape)
    return (
        outputs,
        grad_inputs,
        grad_gain_attn,
        g_all[:narrow].T,
        g_all[narrow : 2 * narrow].T,
        g_all[2 * narrow : 3 * narrow].T,
        g_all[3 * narrow : main],
        grad_table,
        grad_gain_ffn,
        grad_in,
        grad_down,
    )


def solution(mesh):
    in_specs = (
        P("dp", "seq", None),
        P("dp"),
        P("dp"),
        P("dp", "tensor"),
        P("dp", "tensor"),
        P("dp", "tensor"),
        P("tensor", "dp"),
        P("dp", "tensor"),
        P("dp"),
        P("dp", "tensor"),
        P("tensor", "dp"),
        P("dp", "seq", None),
    )
    out_specs = (
        P("dp", "seq", None),
        P("dp", "seq", None),
        P("dp"),
        P("dp", "tensor"),
        P("dp", "tensor"),
        P("dp", "tensor"),
        P("tensor", "dp"),
        P("dp", "tensor"),
        P("dp"),
        P("dp", "tensor"),
        P("tensor", "dp"),
    )
    return jax.shard_map(body, mesh=mesh, in_specs=in_specs, out_specs=out_specs, check_vma=False)
```
